32 devices in a mesh: section: 4 (over y, x), strip: 8 (over z, core).
Axes of the slice: x: 2, y: 2, z: 4, core: 2. Of those that a mesh axis runs over, the one named last changes fastest.
Arguments:
- cotangent: bfloat16 [1, 512, 2048], P(None, 'strip'), may hold values from -6 to 6
- activations: bfloat16 [4, 1, 512, 2048], P('section', None, 'strip'), may hold values from -6 to 6
- weights: bfloat16 [4, 2, 3, 3, 64, 64], P('section'), may hold values from -0.25 to 0.25
- biases: float32 [4, 2, 64], P('section'), may hold values from -3 to 3
Outputs:
- noise_grad: bfloat16 [4, 1, 512, 2048], P('section', None, 'strip')
- weight_grad: float32 [4, 2, 3, 3, 64, 64], P('section')
- bias_grad: float32 [4, 2, 64], P('section')
The draws below stay inside these ranges and needn't reach their ends.
All inputs are finite; a program needn't handle non-finite values.
Results may differ from the reference program's by a relative error of at most 0.01.
Values may be sent and summed in bfloat16 or wider, within the bound.
No kernel may reach another device: no remote copies, remote signals or barrier semaphores. Data moves between devices by JAX's collectives and lax.ppermute only.
A program may use at most 64 MiB of HBM per device.

```python
import math
import jax
import jax.numpy as jnp
from jax import lax

CH = 64
CONVS = 2
ROWS = 64
COLS = 32
SAMPLES = 1
SECTIONS = 4
HEIGHT = 512
N_STRIP = 8


def level_of(stream_key, dims, shards, least, top_value):
    def one(axis_at, parts):
        steps = jax.random.uniform(jax.random.fold_in(jax.random.fold_in(stream_key, 6), axis_at), (parts,), jnp.float32, least / len(shards), top_value / len(shards))
        return jnp.repeat(jnp.exp(steps), dims[axis_at] // parts).reshape((-1,) + (1,) * (len(dims) - axis_at - 1))

    level = one(*shards[0])
    for cut in shards[1:]:
        level = level * one(*cut)
    return level


def gaussian(rng, shape, deviation, reach, cuts=(), kind=jnp.bfloat16):
    result = jax.random.normal(rng, shape, jnp.float32) * deviation
    if len(cuts) > 0:
        result = level_of(rng, shape, cuts, -0.22, 0.18) * result
    return jnp.clip(result, min=-reach, max=reach).astype(kind)


def setup_inputs(seed: int = 0) -> dict:
    arg_keys = jax.random.split(jax.random.key(seed), 5)
    cotangent = gaussian(arg_keys[0], (SAMPLES, HEIGHT, COLS * CH), 1.0, 6.0, ((1, 8),))
    activations = gaussian(arg_keys[1], (SECTIONS, SAMPLES, HEIGHT, COLS * CH), 1.0, 6.0, ((0, 4), (2, 8)))
    weights = gaussian(arg_keys[2], (SECTIONS, CONVS, 3, 3, CH, CH), (9 * CH) ** -0.5, 0.25, ((0, 4),))
    biases = gaussian(arg_keys[3], (SECTIONS, CONVS, CH), 0.5, 3.0, ((0, 4),), jnp.float32)
    return dict(cotangent=cotangent, activations=activations, weights=weights, biases=biases)


LEAK = 0.05

def activate(value):
    return LEAK * value + (1.0 - LEAK) * jax.nn.softplus(value)

def steepness(value):
    return LEAK + (1.0 - LEAK) * jax.nn.sigmoid(value)

def conv_same(field_in, kernel):
    return lax.conv_general_dilated(field_in, kernel, (1, 1), ((1, 1), (1, 1)), dimension_numbers=('NHWC', 'HWIO', 'NHWC'), preferred_element_type=jnp.float32)

def flipped(kernel):
    return jnp.transpose(kernel[::-1, ::-1], (0, 1, 3, 2))

def weight_taps(field_in, error):
    padded = jnp.pad(field_in, ((0, 0), (1, 1), (1, 1), (0, 0)))
    height = error.shape[1]
    col_span = error.shape[2]
    tap_list = []
    for row_tap in range(3):
        for col_tap in range(3):
            window = padded[:, row_tap:row_tap + height, col_tap:col_tap + col_span].reshape(-1, CH)
            tap_list.append(jnp.dot(window.T, error.reshape(-1, CH), preferred_element_type=jnp.float32))
    return jnp.stack(tap_list).reshape(3, 3, CH, CH)

def coarsen(grad_up, section_level):
    fine_rows = ROWS * 3 ** section_level // 4 ** section_level
    coarse_rows = ROWS * 3 ** (section_level + 1) // 4 ** (section_level + 1)
    fine_cols = COLS * 3 ** section_level // 4 ** section_level
    coarse_cols = COLS * 3 ** (section_level + 1) // 4 ** (section_level + 1)
    fine_height = N_STRIP * fine_rows
    coarse_height = N_STRIP * coarse_rows
    wide_grad = grad_up.astype(jnp.float32)
    row_pos = jnp.arange(fine_height, dtype=jnp.int32)
    row_num = jnp.maximum(6 * row_pos - 1, 0)
    row_low = row_num // 8
    row_frac = (row_num - 8 * row_low).astype(jnp.float32) / 8.0
    row_high = jnp.minimum(row_low + 1, coarse_height - 1)
    by_rows = jnp.zeros((SAMPLES, coarse_height, fine_cols, CH), jnp.float32)
    by_rows = by_rows.at[:, row_low].add(wide_grad * (1.0 - row_frac)[None, :, None, None])
    by_rows = by_rows.at[:, row_high].add(wide_grad * row_frac[None, :, None, None])
    col_pos = jnp.arange(fine_cols, dtype=jnp.int32)
    col_num = jnp.maximum((2 * col_pos + 1) * coarse_cols - fine_cols, 0)
    col_den = 2 * fine_cols
    col_low = col_num // col_den
    col_frac = (col_num - col_den * col_low).astype(jnp.float32) / float(col_den)
    col_high = jnp.minimum(col_low + 1, coarse_cols - 1)
    by_cols = jnp.zeros((SAMPLES, coarse_height, coarse_cols, CH), jnp.float32)
    by_cols = by_cols.at[:, :, col_low].add(by_rows * (1.0 - col_frac)[None, None, :, None])
    by_cols = by_cols.at[:, :, col_high].add(by_rows * col_frac[None, None, :, None])
    return by_cols.astype(jnp.bfloat16)

def reference(cotangent, activations, weights, biases):
    grad_out = cotangent.reshape(SAMPLES, HEIGHT, COLS, CH)
    noise_list = []
    kernel_list = []
    bias_list = []
    for section_level in range(SECTIONS):
        live_rows = ROWS * 3 ** section_level // 4 ** section_level
        live_cols = COLS * 3 ** section_level // 4 ** section_level
        field_in = activations[section_level].reshape(SAMPLES, N_STRIP, ROWS, COLS, CH)[:, :, :live_rows, :live_cols]
        field_in = field_in.reshape(SAMPLES, N_STRIP * live_rows, live_cols, CH)
        kernel_in = weights[section_level, 0]
        kernel_out = weights[section_level, 1]
        pre_in = conv_same(field_in, kernel_in) + biases[section_level, 0]
        hidden = activate(pre_in).astype(jnp.bfloat16)
        pre_out = conv_same(hidden, kernel_out) + biases[section_level, 1]
        error_out = (grad_out.astype(jnp.float32) * steepness(pre_out)).astype(jnp.bfloat16)
        back_hidden = conv_same(error_out, flipped(kernel_out))
        error_in = (back_hidden * steepness(pre_in)).astype(jnp.bfloat16)
        back_input = conv_same(error_in, flipped(kernel_in))
        grad_up = (grad_out.astype(jnp.float32) + back_input).astype(jnp.bfloat16)
        scale_back = 1.0 / math.sqrt(SAMPLES * N_STRIP * live_rows * live_cols)
        kernel_list.append(jnp.stack([weight_taps(field_in, error_in), weight_taps(hidden, error_out)]) * scale_back)
        bias_list.append(jnp.stack([lax.optimization_barrier(jnp.sum(error_in.astype(jnp.float32), axis=(0, 1, 2))), lax.optimization_barrier(jnp.sum(error_out.astype(jnp.float32), axis=(0, 1, 2)))]) * scale_back)
        noise = back_input.astype(jnp.bfloat16).reshape(SAMPLES, N_STRIP, live_rows, live_cols, CH)
        noise = jnp.pad(noise, ((0, 0), (0, 0), (0, ROWS - live_rows), (0, COLS - live_cols), (0, 0)))
        noise_list.append(noise.reshape(SAMPLES, HEIGHT, COLS * CH))
        if section_level + 1 < SECTIONS:
            grad_out = coarsen(grad_up, section_level)
    return (jnp.stack(noise_list), jnp.stack(kernel_list), jnp.stack(bias_list))
```

```python
import functools
import math

import jax
import jax.numpy as jnp
import numpy as np
from jax import lax
from jax.experimental import pallas as pl
from jax.experimental.pallas import tpu as pltpu
from jax.sharding import PartitionSpec as P

LEAK = 0.05
LANES = 128
F32 = jnp.float32
BF16 = jnp.bfloat16
TAPS = 9
VMEM_BYTES = 56 * 1024 * 1024


def up_to(value, step):
    return -(-value // step) * step


class Level:
    def __init__(self, level, rows, cols):
        self.level = level
        self.rows = rows * 3**level // 4**level
        self.cols = cols * 3**level // 4**level
        self.pairs = -(-self.cols // 2)
        self.odd_pairs = -(-(self.cols + 1) // 2)

    def margin(self, error):
        self.error = error
        self.x_margin = error + 2
        self.x_rows = self.rows + 2 * (error + 2)
        self.hidden_rows = up_to(self.rows + 2 * (error + 1), 16)
        self.out_rows = up_to(self.rows + 2 * error, 16)
        self.in_rows = up_to(self.rows + 2 * (error - 1), 16)
        self.back_rows = up_to(self.rows + 2 * (error - 2), 16)
        self.own_rows = up_to(self.rows, 16)
        self.alloc = up_to(max(self.hidden_rows, self.x_margin + self.own_rows + 2) + 2, 8)


def levels_of(rows, cols, count):
    levels = [Level(s, rows, cols) for s in range(count)]
    levels[-1].margin(2)
    for s in range(count - 2, -1, -1):
        fine, coarse = levels[s], levels[s + 1]
        first = -coarse.error
        last = coarse.rows + coarse.error - 1
        low = 4 * (first // 3) + (-1, 1, 2)[first % 3]
        high = 4 * (last // 3) + (1, 2, 4)[last % 3]
        fine.margin(max(-low, high - fine.rows + 1) + 2)
        fine.k_first = first // 3
        fine.k_count = up_to(last // 3 - fine.k_first + 1, 8)
        fine.up_shift = -3 * fine.k_first - coarse.error
        start = fine.error - 2 + 4 * fine.k_first - 1
        fine.gu_row = max(0, -start)
        fine.gu_start = start + fine.gu_row
        assert fine.rows % 4 == 0
    return levels


def column_weights(fine, coarse):
    matrix = np.zeros((coarse, fine), np.float32)
    for x in range(fine):
        num = max((2 * x + 1) * coarse - fine, 0)
        low = num // (2 * fine)
        frac = np.float32(num - 2 * fine * low) / np.float32(2 * fine)
        matrix[low, x] += np.float32(1.0) - frac
        matrix[min(low + 1, coarse - 1), x] += frac
    return matrix


def lane_index(shape):
    return lax.broadcasted_iota(jnp.int32, shape, len(shape) - 1)


def half_swap(value):
    return pltpu.roll(value, LANES // 2, value.ndim - 1)


def twice(bias):
    return jnp.concatenate([bias, bias], axis=1)


def rounded(value):
    return value.astype(BF16).astype(F32)


def image_mask(level, base, count, strip, strips):
    row = lax.broadcasted_iota(jnp.int32, (1, count, LANES), 1) + base
    low = jnp.where(strip == 0, 0, -(10**6))
    high = jnp.where(strip == strips - 1, level.rows, 10**6)
    return (row >= low) & (row < high)


def odd_column_mask(level, first, count, mask):
    if first > 0 and 2 * (first + count - 1) < level.cols:
        return mask
    shape = (count, mask.shape[1], LANES)
    half = lax.broadcasted_iota(jnp.int32, shape, 2) // (LANES // 2)
    col = 2 * (first + lax.broadcasted_iota(jnp.int32, shape, 0)) - 1 + half
    return mask & (col >= 0) & (col < level.cols)


def conv(source, kernel, count, rows, chunk, emit):
    for first in range(0, count, chunk):
        size = min(chunk, count - first)
        parts = []
        for dy in range(3):
            block = source[first : first + size + 1, dy : dy + rows, :].astype(BF16)
            parts.append(block[:size].reshape(size * rows, LANES))
            parts.append(block[1:].reshape(size * rows, LANES))
        stacked = jnp.concatenate(parts, axis=1)
        result = jnp.dot(stacked, kernel[...], preferred_element_type=F32)
        emit(first, size, result.reshape(size, rows, LANES))


def kernel_terms(source, error, count, source_row, error_row, level):
    rows = level.own_rows
    err = error[0:count, error_row : error_row + rows, :]
    if rows != level.rows:
        row = lax.broadcasted_iota(jnp.int32, (1, rows, LANES), 1)
        err = jnp.where(row < level.rows, err, 0.0)
    total = jnp.sum(err, axis=(0, 1)).reshape(1, LANES)
    parts = []
    for dy in range(3):
        block = source[0 : count + 1, source_row + dy : source_row + dy + rows, :].astype(BF16)
        parts.append(block[:count].reshape(count * rows, LANES))
        parts.append(block[1:].reshape(count * rows, LANES))
    stacked = jnp.concatenate(parts, axis=1)
    product = lax.dot_general(
        err.astype(BF16).reshape(count * rows, LANES),
        stacked,
        (((0,), (0,)), ((), ())),
        preferred_element_type=F32,
    )
    return product, total


def pack_kernel_terms(out_ref, product, total, scale):
    half = LANES // 2
    by_tap = product.T * scale
    lane = lane_index((1, LANES))
    for dy in range(3):
        block = by_tap[dy * 2 * LANES : (dy + 1) * 2 * LANES]
        folded = block[: 3 * half] + half_swap(block)[half:]
        out_ref[dy * 96 : dy * 96 + 96, :] = jnp.where(lane < half, folded[:96], half_swap(folded[96:]))
    bias = (total + half_swap(total)) * scale
    out_ref[288:304, :] = jnp.broadcast_to(bias, (16, LANES))


def toeplitz(taps):
    half = LANES // 2
    zero = jnp.zeros((half, half), F32)
    rows = []
    for dy in range(3):
        for k in range(4):
            left = taps[dy * 3 + k] if k < 3 else zero
            right = taps[dy * 3 + k - 1] if k > 0 else zero
            rows.append(jnp.concatenate([left, right], axis=1))
    return jnp.concatenate(rows, axis=0)


def toeplitz_back(taps):
    half = LANES // 2
    zero = jnp.zeros((half, half), F32)
    columns = []
    for dy in range(3):
        for k in range(4):
            top = taps[(2 - dy) * 3 + 2 - k] if k < 3 else zero
            bottom = taps[(2 - dy) * 3 + 3 - k] if k > 0 else zero
            columns.append(jnp.concatenate([top, bottom], axis=0))
    pairs = [jnp.concatenate(columns[i : i + 2], axis=1).T for i in range(0, 12, 2)]
    return jnp.concatenate(pairs, axis=0)


def forward(level, xb, hb, kernels, bias, d_in, d_out, strip, strips, chunk, hidden_out=None):
    base = -(level.error + 1)
    mask = image_mask(level, base, level.hidden_rows, strip, strips)
    if level.alloc > level.hidden_rows:
        hb[0 : level.pairs + 1, level.hidden_rows : level.alloc, :] = jnp.zeros(
            (level.pairs + 1, level.alloc - level.hidden_rows, LANES), F32
        )
    if level.odd_pairs < level.pairs + 1:
        hb[level.odd_pairs : level.pairs + 1, 0 : level.alloc, :] = jnp.zeros(
            (level.pairs + 1 - level.odd_pairs, level.alloc, LANES), F32
        )
    bias_in, bias_out = bias[0:1], bias[1:2]

    def first_layer(first, size, value):
        pre = value + bias_in
        small = jnp.exp(-jnp.abs(pre))
        soft = jnp.maximum(pre, 0.0) + jnp.log(1.0 + small)
        act = LEAK * pre + (1.0 - LEAK) * soft
        keep = odd_column_mask(level, first, size, mask)
        hb[first : first + size, 0 : level.hidden_rows, :] = jnp.where(keep, rounded(act), 0.0)
        d_in[first : first + size, 0 : level.hidden_rows, :] = slope(pre)

    conv(xb, kernels[0], level.odd_pairs, level.hidden_rows, chunk, first_layer)

    def second_layer(first, size, value):
        d_out(first, size, slope(value + bias_out))

    conv(hb, kernels[1], level.pairs, level.out_rows, chunk, second_layer)


def slope(value):
    return LEAK + (1.0 - LEAK) * (0.5 + 0.5 * jnp.tanh(0.5 * value))


def backward(level, eo, ei, kernels, d_in, grad, grad_row, noise, gu, bi, strip, strips, chunk):
    mask_in = image_mask(level, -(level.error - 1), level.in_rows, strip, strips)
    if level.odd_pairs < level.pairs + 1:
        ei[level.odd_pairs : level.pairs + 1, 0 : level.alloc, :] = jnp.zeros(
            (level.pairs + 1 - level.odd_pairs, level.alloc, LANES), F32
        )

    def inner(first, size, value):
        keep = odd_column_mask(level, first, size, mask_in)
        part = d_in[first : first + size, 2 : 2 + level.in_rows, :]
        ei[first : first + size, 0 : level.in_rows, :] = jnp.where(keep, rounded(value * part), 0.0)

    conv(eo, kernels[1], level.odd_pairs, level.in_rows, chunk, inner)
    mask_back = image_mask(level, -(level.error - 2), level.back_rows, strip, strips)

    def outer(first, size, value):
        if noise is not None:
            bi[first : first + size, 0 : level.back_rows, :] = value
        if gu is not None:
            part = grad[first : first + size, grad_row + 2 : grad_row + 2 + level.back_rows, :]
            gu[first : first + size, level.gu_row : level.gu_row + level.back_rows, :] = jnp.where(mask_back, rounded(part + value), 0.0)

    conv(ei, kernels[0], level.pairs, level.back_rows, chunk, outer)
    if noise is not None:
        total_rows = noise.shape[0]
        row = lax.broadcasted_iota(jnp.int32, (level.own_rows, LANES), 0)
        lane = lane_index((level.own_rows, LANES))
        for p in range(noise.shape[1] // LANES):
            at = slice(p * LANES, (p + 1) * LANES)
            if p < level.pairs:
                part = bi[p, level.error - 2 : level.error - 2 + level.own_rows, :]
                if level.own_rows != level.rows:
                    part = jnp.where(row < level.rows, part, 0.0)
                if 2 * p + 1 >= level.cols:
                    part = jnp.where(lane < LANES // 2, part, 0.0)
                noise[0 : level.own_rows, at] = part.astype(BF16)
                if level.own_rows < total_rows:
                    noise[level.own_rows : total_rows, at] = jnp.zeros((total_rows - level.own_rows, LANES), BF16)
            else:
                noise[:, at] = jnp.zeros((total_rows, LANES), BF16)


def coarsen(fine, coarse, gu, rc, emit, strip, strips):
    count = fine.k_count
    start = fine.gu_start
    for p in range(fine.pairs):
        f = [gu[p, pl.ds(start + a, count, stride=4), :] for a in range(6)]
        rc[p, pl.ds(0, count, stride=3), :] = 0.125 * f[0] + 0.875 * f[1] + 0.375 * f[2]
        rc[p, pl.ds(1, count, stride=3), :] = 0.625 * f[2] + 0.625 * f[3]
        rc[p, pl.ds(2, count, stride=3), :] = 0.375 * f[3] + 0.875 * f[4] + 0.125 * f[5]
    top = -3 * fine.k_first
    low = top + coarse.rows - 1
    on_top = jnp.where(strip == 0, 1.0, 0.0).astype(F32)
    on_low = jnp.where(strip == strips - 1, 1.0, 0.0).astype(F32)
    all_pairs = slice(0, fine.pairs)
    rc[all_pairs, top : top + 1, :] = rc[all_pairs, top : top + 1, :] + on_top * rc[all_pairs, top - 1 : top, :]
    rc[all_pairs, low : low + 1, :] = rc[all_pairs, low : low + 1, :] + on_low * rc[all_pairs, low + 1 : low + 2, :]
    matrix = column_weights(fine.cols, coarse.cols)
    matrix = np.pad(matrix, ((0, 2 * coarse.pairs - coarse.cols), (0, 2 * fine.pairs - fine.cols)))
    lane = lane_index((1, LANES))

    def weights(low_lanes, high_lanes):
        return jnp.where(lane < LANES // 2, np.float32(low_lanes), np.float32(high_lanes))

    for m in range(coarse.pairs):
        total = None
        for q in range(fine.pairs):
            same = (matrix[2 * m, 2 * q], matrix[2 * m + 1, 2 * q + 1])
            cross = (matrix[2 * m, 2 * q + 1], matrix[2 * m + 1, 2 * q])
            value = rc[q, 0 : 3 * count, :] if any(same) or any(cross) else None
            for pair, moved in ((same, False), (cross, True)):
                if any(pair):
                    term = (half_swap(value) if moved else value) * weights(*pair)
                    total = term if total is None else total + term
        emit(m, total)


def fill_input(level, xb, act, top, low, tmp, payload_rows):
    margin = level.x_margin
    zero = jnp.zeros((level.alloc, LANES), F32)
    xb[0, 0 : level.alloc, :] = zero
    xb[level.pairs + 1, 0 : level.alloc, :] = zero
    lane = lane_index((1, LANES))
    for p in range(level.pairs):
        at = slice(p * LANES, (p + 1) * LANES)
        upper, own, lower = top(at), act[0 : level.own_rows, at].astype(F32), low(at)
        if 2 * p + 1 >= level.cols:
            upper, own, lower = (jnp.where(lane < LANES // 2, v, 0.0) for v in (upper, own, lower))
        end = margin + level.rows
        if end + margin < level.alloc:
            xb[p + 1, end + margin : level.alloc, :] = jnp.zeros((level.alloc - end - margin, LANES), F32)
        tmp[0, 0:32, :] = upper
        tmp[1, 0:32, :] = lower
        xb[p + 1, 0:margin, :] = tmp[0, payload_rows - margin : payload_rows, :]
        xb[p + 1, margin : margin + level.own_rows, :] = own
        xb[p + 1, end : end + margin, :] = tmp[1, 0:margin, :]
        after = up_to(end + margin, 1)
        if margin + level.own_rows > after:
            xb[p + 1, after : margin + level.own_rows, :] = jnp.zeros((margin + level.own_rows - after, LANES), F32)


def flat_to_pairs(level, flat, xb):
    zero = jnp.zeros((level.alloc, LANES), F32)
    xb[0, 0 : level.alloc, :] = zero
    xb[level.pairs + 1, 0 : level.alloc, :] = zero
    for p in range(level.pairs):
        xb[p + 1, 0 : level.x_rows, :] = flat[p * level.x_rows : (p + 1) * level.x_rows, :]
        if level.alloc > level.x_rows:
            xb[p + 1, level.x_rows : level.alloc, :] = jnp.zeros((level.alloc - level.x_rows, LANES), F32)


def call(body, out_shape, scratch, operands, flops, nbytes):
    return pl.pallas_call(
        body,
        out_shape=out_shape,
        in_specs=[pl.BlockSpec(memory_space=pltpu.VMEM)] * len(operands),
        out_specs=[pl.BlockSpec(memory_space=pltpu.VMEM)] * len(out_shape),
        scratch_shapes=scratch,
        compiler_params=pltpu.CompilerParams(vmem_limit_bytes=VMEM_BYTES),
        cost_estimate=pl.CostEstimate(flops=flops, bytes_accessed=nbytes, transcendentals=0),
    )(*operands)


def sds(shape, dtype):
    return jax.ShapeDtypeStruct(shape, dtype)


def buffer(level, extra):
    return pltpu.VMEM((level.pairs + extra, level.alloc, LANES), F32)


def local(strips, sections, cotangent, activations, weights, biases):
    row_count, flat_width = activations.shape[2:]
    channels = weights.shape[-1]
    cols = flat_width // channels
    assert 2 * channels == LANES and sections == 4 and cotangent.shape[0] == 1
    levels = levels_of(row_count, cols, sections)
    fine, second, third, last = levels
    x_margin, g_margin = fine.x_margin, fine.error
    payload = up_to(x_margin + g_margin, 16)
    pair_count = fine.pairs
    cot = cotangent[0]
    act = activations[0, 0]
    taps = weights.reshape(2 * TAPS, channels, channels)
    bias = biases[0]
    chunk = 4

    def ids():
        return lax.axis_index("section"), lax.axis_index("strip")

    def halo_body(act_ref, cot_ref, swap_ref, cross_ref, xs, cs, ts):
        section, strip = ids()
        odd = lax.rem(strip, 2) == 1
        live = jnp.int32(fine.rows)
        for level in levels[1:]:
            live = jnp.where(section == level.level, level.rows, live)
        for p in range(pair_count):
            at = slice(p * LANES, (p + 1) * LANES)
            xs[p, :, :] = act_ref[:, at].astype(F32)
            cs[p, :, :] = cot_ref[:, at].astype(F32)
            ts[0, p, 0:x_margin, :] = xs[p, 0:x_margin, :]
            ts[0, p, x_margin : x_margin + g_margin, :] = cs[p, 0:g_margin, :]
            ts[1, p, 0:x_margin, :] = xs[p, pl.ds(live - x_margin, x_margin), :]
            ts[1, p, x_margin : x_margin + g_margin, :] = cs[p, row_count - g_margin : row_count, :]
            upper = ts[0, p, 0:payload, :]
            lower = ts[1, p, 0:payload, :]
            swap_ref[:, at] = jnp.where(odd, upper, lower).astype(BF16)
            cross_ref[:, at] = jnp.where(odd, lower, upper).astype(BF16)

    halo_shape = sds((payload, flat_width), BF16)
    to_swap, to_cross = call(
        halo_body,
        [halo_shape, halo_shape],
        [
            pltpu.VMEM((pair_count, row_count, LANES), F32),
            pltpu.VMEM((pair_count, row_count, LANES), F32),
            pltpu.VMEM((2, pair_count, payload, LANES), F32),
        ],
        [act, cot],
        10**6,
        10**6,
    )
    swap_pairs = [(i, i ^ 1) for i in range(strips)]
    cross_pairs = [(i, i + 1) for i in range(1, strips - 1, 2)] + [(i + 1, i) for i in range(1, strips - 1, 2)]
    from_cross = lax.ppermute(to_cross, "strip", cross_pairs)
    from_swap = lax.ppermute(to_swap, "strip", swap_pairs)

    def expand(tap_list, forward_ref, back_ref):
        for c in range(2):
            chosen = tap_list[c * TAPS : (c + 1) * TAPS]
            forward_ref[c, :, :] = toeplitz(chosen).astype(BF16)
            back_ref[c, :, :] = toeplitz_back(chosen).astype(BF16)

    def matrix_body(taps_ref, forward_ref, back_ref, packed_ref):
        values = [taps_ref[t].astype(F32) for t in range(2 * TAPS)]
        expand(values, forward_ref, back_ref)
        half = channels // 2
        for t in range(2 * TAPS):
            packed_ref[t * half : (t + 1) * half, :] = jnp.concatenate(
                [values[t][:half], values[t][half:]], axis=1
            ).astype(BF16)

    matrix_shape = sds((2, 6 * LANES, LANES), BF16)
    packed_rows = TAPS * channels
    fwd_own, back_own, packed_own = call(
        matrix_body,
        [matrix_shape, matrix_shape, sds((packed_rows, LANES), BF16)],
        [],
        [taps],
        10**6,
        10**6,
    )

    g_rows = second.rows + 2 * second.error
    g_flat = up_to(second.pairs * g_rows, 16)
    x_flat = up_to(max(second.pairs * second.x_rows, third.pairs * third.x_rows), 16)
    g_flat = max(g_flat, 16)
    ship_rows = max(x_flat + packed_rows, g_flat) + 16

    def halo_readers(swap_ref, cross_ref, strip):
        odd = lax.rem(strip, 2) == 1

        def top(at):
            return jnp.where(odd, swap_ref[:, at].astype(F32), cross_ref[:, at].astype(F32))

        def low(at):
            return jnp.where(odd, cross_ref[:, at].astype(F32), swap_ref[:, at].astype(F32))

        return top, low

    def chain_body(
        act_ref, cot_ref, swap_ref, cross_ref, fwd_ref, back_ref, packed_ref, bias_ref,
        hop_ref, ship_ref, noise_ref, hid_ref, ein_ref, eout_ref,
        xb, hb, db, gb, eo, ei, bi, gu, rc, flat, tmp, bias_tmp,
    ):
        section, strip = ids()
        top, low = halo_readers(swap_ref, cross_ref, strip)

        @pl.when(section == 0)
        def _():
            level = fine
            fill_input(level, xb, act_ref, top, low, tmp, x_margin)
            zero = jnp.zeros((level.alloc, LANES), F32)
            eo[0, 0 : level.alloc, :] = zero
            eo[level.pairs + 1, 0 : level.alloc, :] = zero
            for p in range(level.pairs):
                at = slice(p * LANES, (p + 1) * LANES)
                tmp[0, 0:payload, :] = top(at)
                tmp[1, 0:payload, :] = low(at)
                gb[p, 0:g_margin, :] = tmp[0, x_margin : x_margin + g_margin, :]
                gb[p, g_margin : g_margin + row_count, :] = cot_ref[:, at].astype(F32)
                gb[p, g_margin + row_count : 2 * g_margin + row_count, :] = tmp[
                    1, x_margin : x_margin + g_margin, :
                ]
            mask_out = image_mask(level, -level.error, level.out_rows, strip, strips)

            def error(first, size, value):
                part = gb[first : first + size, 0 : level.out_rows, :]
                eo[first + 1 : first + 1 + size, 0 : level.out_rows, :] = jnp.where(
                    mask_out, rounded(part * value), 0.0
                )

            forward(
                level, xb, hb, [fwd_ref.at[0], fwd_ref.at[1]], twice(bias_ref[...]), db, error, strip, strips, chunk
            )
            backward(
                level, eo, ei, [back_ref.at[0], back_ref.at[1]], db, gb, 0, noise_ref, gu, bi, strip, strips, chunk
            )

            def emit(m, rows):
                flat[m * g_rows : (m + 1) * g_rows, :] = rows[0:g_rows]

            coarsen(fine, second, gu, rc, emit, strip, strips)
            value = flat[0:g_flat, :].astype(BF16)
            hop_ref[...] = value
            ship_ref[0:g_flat, :] = value
            rows = level.rows
            for p in range(level.pairs + 1):
                hid_ref[p, :, :] = hb[p, level.error : level.error + rows + 16, :].astype(BF16)
                ein_ref[p, :, :] = ei[p, level.error - 1 : level.error - 1 + rows, :].astype(BF16)
                if p < level.pairs:
                    eout_ref[p, :, :] = eo[p + 1, level.error : level.error + rows, :].astype(BF16)

        for level in (second, third):

            @pl.when(section == level.level)
            def _(level=level):
                fill_input(level, xb, act_ref, top, low, tmp, x_margin)
                for p in range(level.pairs):
                    flat[p * level.x_rows : (p + 1) * level.x_rows, :] = xb[p + 1, 0 : level.x_rows, :]
                used = up_to(level.pairs * level.x_rows, 16)
                ship_ref[0:used, :] = flat[0:used, :].astype(BF16)
                ship_ref[x_flat : x_flat + packed_rows, :] = packed_ref[...]
                rest = twice(bias_ref[...])
                for term in range(3):
                    part = rounded(rest)
                    bias_tmp[2 * term : 2 * term + 2, :] = part
                    rest = rest - part
                bias_tmp[6:16, :] = jnp.zeros((10, LANES), F32)
                ship_ref[x_flat + packed_rows : ship_rows, :] = bias_tmp[...].astype(BF16)

    hop_shape = sds((g_flat, LANES), BF16)
    ship_shape = sds((ship_rows, LANES), BF16)
    hop, ship, noise_first, hid_first, ein_first, eout_first = call(
        chain_body,
        [
            hop_shape,
            ship_shape,
            sds((row_count, flat_width), BF16),
            sds((fine.pairs + 1, row_count + 16, LANES), BF16),
            sds((fine.pairs + 1, row_count, LANES), BF16),
            sds((fine.pairs, row_count, LANES), BF16),
        ],
        [
            buffer(fine, 2),
            buffer(fine, 1),
            buffer(fine, 1),
            buffer(fine, 0),
            buffer(fine, 2),
            buffer(fine, 1),
            buffer(fine, 0),
            buffer(fine, 0),
            pltpu.VMEM((fine.pairs, 3 * fine.k_count, LANES), F32),
            pltpu.VMEM((up_to(max(g_flat, x_flat), 8) + 16, LANES), F32),
            pltpu.VMEM((2, max(payload, 32), LANES), F32),
            pltpu.VMEM((16, LANES), F32),
        ],
        [act, cot, from_swap, from_cross, fwd_own, back_own, packed_own, bias],
        3 * 10**9,
        4 * 10**6,
    )

    def across(value, pairs):
        return lax.ppermute(value, "section", pairs)

    got_hop = across(hop, [(0, 3)])
    got_far = across(ship, [(0, 2), (1, 3)])
    got_near = across(ship, [(0, 1), (1, 2), (2, 3)])

    def forward_body(
        act_ref, swap_ref, cross_ref, fwd_ref, back_ref, bias_ref, far_ref, near_ref,
        din1, dout1, din2, dout2, din3, dout3, back1, back2, hid_ref, xown_ref,
        xb, hb, flat, fwd_tmp, tmp,
    ):
        section, strip = ids()
        top, low = halo_readers(swap_ref, cross_ref, strip)
        slots = {1: (din1, dout1, back1), 2: (din2, dout2, back2), 3: (din3, dout3, None)}

        def run(level, kernels, bias_rows):
            d_in, d_out, _ = slots[level.level]

            def store(first, size, value):
                d_out[first : first + size, 0 : level.out_rows, :] = value

            forward(level, xb, hb, kernels, bias_rows, d_in, store, strip, strips, chunk)

        def own(level):
            fill_input(level, xb, act_ref, top, low, tmp, x_margin)
            run(level, [fwd_ref.at[0], fwd_ref.at[1]], twice(bias_ref[...]))
            hid_ref[0 : level.pairs + 1, 0 : level.alloc, :] = hb[0 : level.pairs + 1, 0 : level.alloc, :]
            xown_ref[0 : level.pairs + 2, 0 : level.alloc, :] = xb[0 : level.pairs + 2, 0 : level.alloc, :]
            back = slots[level.level][2]
            if back is not None:
                back[...] = back_ref[...]

        def shipped(level, source):
            half = channels // 2
            values = []
            for t in range(2 * TAPS):
                pack = source[x_flat + t * half : x_flat + (t + 1) * half, :].astype(F32)
                values.append(jnp.concatenate([pack[:, :channels], pack[:, channels:]], axis=0))
            expand(values, fwd_tmp, slots[level.level][2])
            used = up_to(level.pairs * level.x_rows, 16)
            flat[0:used, :] = source[0:used, :].astype(F32)
            flat_to_pairs(level, flat, xb)
            terms = source[x_flat + packed_rows : ship_rows, :].astype(F32)
            run(level, [fwd_tmp.at[0], fwd_tmp.at[1]], terms[0:2] + terms[2:4] + terms[4:6])

        @pl.when(section == 1)
        def _():
            own(second)

        @pl.when(section == 2)
        def _():
            own(third)
            shipped(second, near_ref)

        @pl.when(section == 3)
        def _():
            own(last)
            shipped(second, far_ref)
            shipped(third, near_ref)

    def field(level, extra):
        return sds((level.pairs + extra, level.alloc, LANES), F32)

    outs = call(
        forward_body,
        [
            field(second, 1), field(second, 0),
            field(third, 1), field(third, 0),
            field(last, 1), field(last, 0),
            matrix_shape, matrix_shape,
            field(second, 1), field(second, 2),
        ],
        [
            buffer(second, 2),
            buffer(second, 1),
            pltpu.VMEM((x_flat + 16, LANES), F32),
            pltpu.VMEM((2, 6 * LANES, LANES), BF16),
            pltpu.VMEM((2, max(payload, 32), LANES), F32),
        ],
        [act, from_swap, from_cross, fwd_own, back_own, bias, got_far, got_near],
        2 * 10**9,
        4 * 10**6,
    )
    din1, dout1, din2, dout2, din3, dout3, back1, back2, hid_own, x_own = outs

    grad_rows = up_to(TAPS * channels // 2 + 1, 16)

    def backward_body(
        act_ref, swap_ref, cross_ref, noise0, hid0, ein0, eout0,
        hop_ref, far_ref, near_ref,
        din1, dout1, din2, dout2, din3, dout3, back1, back2, back3, hid_ref, x_ref,
        noise_ref, keep_ref, send_ref,
        xb, hb, gb, eo, ei, bi, gu, rc, flat, tmp, pair_out,
    ):
        section, strip = ids()
        odd = lax.rem(strip, 2) == 1
        slots = {1: (din1, dout1, back1), 2: (din2, dout2, back2), 3: (din3, dout3, back3)}

        def gradients(level, source, hidden, err_in, err_out, rows_at):
            scale = np.float32(1.0 / math.sqrt(strips * level.rows * level.cols))
            first = kernel_terms(source, err_in, level.odd_pairs, rows_at[2], rows_at[0], level)
            pack_kernel_terms(pair_out.at[0], *first, scale)
            then = kernel_terms(hidden, err_out, level.pairs, rows_at[3], rows_at[1], level)
            pack_kernel_terms(pair_out.at[1], *then, scale)

        def step(level, grad_row, keep):
            d_in, d_out, back = slots[level.level]
            mask = image_mask(level, -level.error, level.out_rows, strip, strips)
            zero = jnp.zeros((level.alloc, LANES), F32)
            eo[0, 0 : level.alloc, :] = zero
            eo[level.pairs + 1, 0 : level.alloc, :] = zero
            for p in range(level.pairs):
                part = gb[p, grad_row : grad_row + level.out_rows, :] * d_out[p, 0 : level.out_rows, :]
                eo[p + 1, 0 : level.out_rows, :] = jnp.where(mask[0], rounded(part), 0.0)
            backward(
                level, eo, ei, [back.at[0], back.at[1]], d_in, gb, grad_row,
                noise_ref if keep else None, None if keep else gu, bi, strip, strips, chunk,
            )

        def take(source):
            flat[0:g_flat, :] = source[0:g_flat, :].astype(F32)
            for p in range(second.pairs):
                gb[p, 0:g_rows, :] = flat[p * g_rows : (p + 1) * g_rows, :]

        def down(upper, lower):
            def emit(m, rows):
                gb[m, 0 : 3 * upper.k_count, :] = rounded(rows)

            coarsen(upper, lower, gu, rc, emit, strip, strips)

        def finish(level):
            gradients(
                level, x_ref, hid_ref, ei, eo.at[1 : 1 + level.pairs],
                (level.error - 1, level.error, level.error + 1, level.error),
            )

        @pl.when(section == 0)
        def _():
            noise_ref[...] = noise0[...]
            top, low = halo_readers(swap_ref, cross_ref, strip)
            fill_input(fine, xb, act_ref, top, low, tmp, x_margin)
            rows = fine.rows
            for p in range(fine.pairs + 1):
                hb[p, 0 : rows + 16, :] = hid0[p, :, :].astype(F32)
                ei[p, 0:rows, :] = ein0[p, :, :].astype(F32)
                if p < fine.pairs:
                    eo[p, 0:rows, :] = eout0[p, :, :].astype(F32)
            gradients(fine, xb, hb, ei, eo, (0, 0, fine.error + 1, 0))

        @pl.when(section == 1)
        def _():
            take(near_ref)
            step(second, 0, True)
            finish(second)

        @pl.when(section == 2)
        def _():
            take(far_ref)
            step(second, 0, False)
            down(second, third)
            step(third, second.up_shift, True)
            finish(third)

        @pl.when(section == 3)
        def _():
            take(hop_ref)
            step(second, 0, False)
            down(second, third)
            step(third, second.up_shift, False)
            down(third, last)
            step(last, third.up_shift, True)
            finish(last)

        first, then = pair_out[0], pair_out[1]
        keep_ref[...] = jnp.where(odd, then, first)
        send_ref[...] = jnp.where(odd, first, then)

    half_shape = sds((grad_rows, LANES), F32)
    noise, keep, send = call(
        backward_body,
        [sds((row_count, flat_width), BF16), half_shape, half_shape],
        [
            buffer(fine, 2),
            buffer(fine, 1),
            buffer(fine, 0),
            buffer(fine, 2),
            buffer(fine, 1),
            buffer(fine, 0),
            buffer(fine, 0),
            pltpu.VMEM((second.pairs, 3 * second.k_count, LANES), F32),
            pltpu.VMEM((g_flat + 16, LANES), F32),
            pltpu.VMEM((2, max(payload, 32), LANES), F32),
            pltpu.VMEM((2, grad_rows, LANES), F32),
        ],
        [
            act, from_swap, from_cross, noise_first, hid_first, ein_first, eout_first,
            got_hop, got_far, got_near,
            din1, dout1, din2, dout2, din3, dout3, back1, back2, back_own, hid_own, x_own,
        ],
        3 * 10**9,
        6 * 10**6,
    )

    total = keep + lax.ppermute(send, "strip", swap_pairs)
    hop_size = 2
    while hop_size < strips:
        mine = lax.reduce_precision(total, 8, 7)
        other = lax.ppermute(mine.astype(BF16), "strip", [(i, i ^ hop_size) for i in range(strips)])
        total = mine + other.astype(F32)
        hop_size *= 2
    other = lax.ppermute(total, "strip", swap_pairs)

    def final_body(mine_ref, other_ref, kernel_ref, bias_ref):
        _, strip = ids()
        odd = lax.rem(strip, 2) == 1
        half = channels
        for c in range(2):
            if c == 0:
                value = jnp.where(odd, other_ref[...], mine_ref[...])
            else:
                value = jnp.where(odd, mine_ref[...], other_ref[...])
            swapped = half_swap(value)
            for dy in range(3):
                kernel_ref[c, dy * 192 : dy * 192 + 96, :] = value[dy * 96 : dy * 96 + 96, :half]
                kernel_ref[c, dy * 192 + 96 : dy * 192 + 192, :] = swapped[dy * 96 : dy * 96 + 96, :half]
            bias_ref[c : c + 1, :] = value[288:289, :half]

    kernel_sum, bias_sum = call(
        final_body,
        [sds((2, TAPS * channels, channels), F32), sds((2, channels), F32)],
        [],
        [total, other],
        10**6,
        10**6,
    )
    return (
        noise[None, None],
        kernel_sum.reshape(1, 2, 3, 3, channels, channels),
        bias_sum[None],
    )


def solution(mesh):
    strips = mesh.shape["strip"]
    sections = mesh.shape["section"]
    return jax.shard_map(
        functools.partial(local, strips, sections),
        mesh=mesh,
        in_specs=(
            P(None, "strip", None),
            P("section", None, "strip", None),
            P("section", None, None, None, None, None),
            P("section", None, None),
        ),
        out_specs=(
            P("section", None, "strip", None),
            P("section", None, None, None, None, None),
            P("section", None, None),
        ),
        check_vma=False,
    )
```

```python
import functools
import math

import jax
import jax.numpy as jnp
import numpy as np
from jax import lax
from jax.experimental import pallas as pl
from jax.experimental.pallas import tpu as pltpu
from jax.sharding import PartitionSpec as P

LEAK = 0.05
LANES = 128
F32 = jnp.float32
BF16 = jnp.bfloat16
TAPS = 9
VMEM_BYTES = 24 * 1024 * 1024


def up_to(value, step):
    return -(-value // step) * step


class Level:
    def __init__(self, level, rows, cols):
        self.level = level
        self.rows = rows * 3**level // 4**level
        self.cols = cols * 3**level // 4**level
        self.pairs = -(-self.cols // 2)
        self.odd_pairs = -(-(self.cols + 1) // 2)

    def margin(self, error):
        self.error = error
        self.x_margin = error + 2
        self.x_rows = self.rows + 2 * (error + 2)
        self.hidden_rows = up_to(self.rows + 2 * (error + 1), 16)
        self.out_rows = up_to(self.rows + 2 * error, 16)
        self.in_rows = up_to(self.rows + 2 * (error - 1), 16)
        self.back_rows = up_to(self.rows + 2 * (error - 2), 16)
        self.own_rows = up_to(self.rows, 16)
        self.alloc = up_to(max(self.hidden_rows, self.x_margin + self.own_rows + 2) + 2, 8)


def levels_of(rows, cols, count):
    levels = [Level(s, rows, cols) for s in range(count)]
    levels[-1].margin(2)
    for s in range(count - 2, -1, -1):
        fine, coarse = levels[s], levels[s + 1]
        first = -coarse.error
        last = coarse.rows + coarse.error - 1
        low = 4 * (first // 3) + (-1, 1, 2)[first % 3]
        high = 4 * (last // 3) + (1, 2, 4)[last % 3]
        fine.margin(max(-low, high - fine.rows + 1) + 2)
        fine.k_first = first // 3
        fine.k_count = up_to(last // 3 - fine.k_first + 1, 8)
        fine.up_shift = -3 * fine.k_first - coarse.error
        start = fine.error - 2 + 4 * fine.k_first - 1
        fine.gu_row = max(0, -start)
        fine.gu_start = start + fine.gu_row
        assert fine.rows % 4 == 0
    return levels


def column_weights(fine, coarse):
    matrix = np.zeros((coarse, fine), np.float32)
    for x in range(fine):
        num = max((2 * x + 1) * coarse - fine, 0)
        low = num // (2 * fine)
        frac = np.float32(num - 2 * fine * low) / np.float32(2 * fine)
        matrix[low, x] += np.float32(1.0) - frac
        matrix[min(low + 1, coarse - 1), x] += frac
    return matrix


def lane_index(shape):
    return lax.broadcasted_iota(jnp.int32, shape, len(shape) - 1)


def half_swap(value):
    return pltpu.roll(value, LANES // 2, value.ndim - 1)


def twice(bias):
    return jnp.concatenate([bias, bias], axis=1)


def rounded(value):
    return value.astype(BF16).astype(F32)


def image_mask(level, base, count, strip, strips):
    row = lax.broadcasted_iota(jnp.int32, (1, count, LANES), 1) + base
    low = jnp.where(strip == 0, 0, -(10**6))
    high = jnp.where(strip == strips - 1, level.rows, 10**6)
    return (row >= low) & (row < high)


def odd_column_mask(level, first, count, mask):
    if first > 0 and 2 * (first + count - 1) < level.cols:
        return mask
    shape = (count, mask.shape[1], LANES)
    half = lax.broadcasted_iota(jnp.int32, shape, 2) // (LANES // 2)
    col = 2 * (first + lax.broadcasted_iota(jnp.int32, shape, 0)) - 1 + half
    return mask & (col >= 0) & (col < level.cols)


def conv(source, kernel, count, rows, chunk, emit):
    for first in range(0, count, chunk):
        size = min(chunk, count - first)
        parts = []
        for dy in range(3):
            block = source[first : first + size + 1, dy : dy + rows, :].astype(BF16)
            parts.append(block[:size].reshape(size * rows, LANES))
            parts.append(block[1:].reshape(size * rows, LANES))
        stacked = jnp.concatenate(parts, axis=1)
        result = jnp.dot(stacked, kernel[...], preferred_element_type=F32)
        emit(first, size, result.reshape(size, rows, LANES))


def kernel_terms(source, error, count, source_row, error_row, level):
    rows = level.own_rows
    err = error[0:count, error_row : error_row + rows, :]
    if rows != level.rows:
        row = lax.broadcasted_iota(jnp.int32, (1, rows, LANES), 1)
        err = jnp.where(row < level.rows, err, 0.0)
    total = jnp.sum(err, axis=(0, 1)).reshape(1, LANES)
    parts = []
    for dy in range(3):
        block = source[0 : count + 1, source_row + dy : source_row + dy + rows, :].astype(BF16)
        parts.append(block[:count].reshape(count * rows, LANES))
        parts.append(block[1:].reshape(count * rows, LANES))
    stacked = jnp.concatenate(parts, axis=1)
    product = lax.dot_general(
        err.astype(BF16).reshape(count * rows, LANES),
        stacked,
        (((0,), (0,)), ((), ())),
        preferred_element_type=F32,
    )
    return product, total


def pack_kernel_terms(out_ref, product, total, scale):
    half = LANES // 2
    by_tap = product.T * scale
    lane = lane_index((1, LANES))
    for dy in range(3):
        block = by_tap[dy * 2 * LANES : (dy + 1) * 2 * LANES]
        folded = block[: 3 * half] + half_swap(block)[half:]
        out_ref[dy * 96 : dy * 96 + 96, :] = jnp.where(lane < half, folded[:96], half_swap(folded[96:]))
    bias = (total + half_swap(total)) * scale
    out_ref[288:304, :] = jnp.broadcast_to(bias, (16, LANES))


def toeplitz(taps):
    half = LANES // 2
    zero = jnp.zeros((half, half), F32)
    rows = []
    for dy in range(3):
        for k in range(4):
            left = taps[dy * 3 + k] if k < 3 else zero
            right = taps[dy * 3 + k - 1] if k > 0 else zero
            rows.append(jnp.concatenate([left, right], axis=1))
    return jnp.concatenate(rows, axis=0)


def toeplitz_back(taps):
    half = LANES // 2
    zero = jnp.zeros((half, half), F32)
    columns = []
    for dy in range(3):
        for k in range(4):
            top = taps[(2 - dy) * 3 + 2 - k] if k < 3 else zero
            bottom = taps[(2 - dy) * 3 + 3 - k] if k > 0 else zero
            columns.append(jnp.concatenate([top, bottom], axis=0))
    pairs = [jnp.concatenate(columns[i : i + 2], axis=1).T for i in range(0, 12, 2)]
    return jnp.concatenate(pairs, axis=0)


def forward(level, xb, hb, kernels, bias, d_in, d_out, strip, strips, chunk, hidden_out=None):
    base = -(level.error + 1)
    mask = image_mask(level, base, level.hidden_rows, strip, strips)
    if level.alloc > level.hidden_rows:
        hb[0 : level.pairs + 1, level.hidden_rows : level.alloc, :] = jnp.zeros(
            (level.pairs + 1, level.alloc - level.hidden_rows, LANES), F32
        )
    if level.odd_pairs < level.pairs + 1:
        hb[level.odd_pairs : level.pairs + 1, 0 : level.alloc, :] = jnp.zeros(
            (level.pairs + 1 - level.odd_pairs, level.alloc, LANES), F32
        )
    bias_in, bias_out = bias[0:1], bias[1:2]

    def first_layer(first, size, value):
        pre = value + bias_in
        small = jnp.exp(-jnp.abs(pre))
        soft = jnp.maximum(pre, 0.0) + jnp.log(1.0 + small)
        act = LEAK * pre + (1.0 - LEAK) * soft
        keep = odd_column_mask(level, first, size, mask)
        hb[first : first + size, 0 : level.hidden_rows, :] = jnp.where(keep, rounded(act), 0.0)
        d_in[first : first + size, 0 : level.hidden_rows, :] = slope(pre)

    conv(xb, kernels[0], level.odd_pairs, level.hidden_rows, chunk, first_layer)

    def second_layer(first, size, value):
        d_out(first, size, slope(value + bias_out))

    conv(hb, kernels[1], level.pairs, level.out_rows, chunk, second_layer)


def slope(value):
    return LEAK + (1.0 - LEAK) * (0.5 + 0.5 * jnp.tanh(0.5 * value))


def backward(level, eo, ei, kernels, d_in, grad, grad_row, noise, gu, bi, strip, strips, chunk):
    mask_in = image_mask(level, -(level.error - 1), level.in_rows, strip, strips)
    if level.odd_pairs < level.pairs + 1:
        ei[level.odd_pairs : level.pairs + 1, 0 : level.alloc, :] = jnp.zeros(
            (level.pairs + 1 - level.odd_pairs, level.alloc, LANES), F32
        )

    def inner(first, size, value):
        keep = odd_column_mask(level, first, size, mask_in)
        part = d_in[first : first + size, 2 : 2 + level.in_rows, :]
        ei[first : first + size, 0 : level.in_rows, :] = jnp.where(keep, rounded(value * part), 0.0)

    conv(eo, kernels[1], level.odd_pairs, level.in_rows, chunk, inner)
    mask_back = image_mask(level, -(level.error - 2), level.back_rows, strip, strips)

    def outer(first, size, value):
        if noise is not None:
            bi[first : first + size, 0 : level.back_rows, :] = value
        if gu is not None:
            part = grad[first : first + size, grad_row + 2 : grad_row + 2 + level.back_rows, :]
            gu[first : first + size, level.gu_row : level.gu_row + level.back_rows, :] = jnp.where(mask_back, rounded(part + value), 0.0)

    conv(ei, kernels[0], level.pairs, level.back_rows, chunk, outer)
    if noise is not None:
        total_rows = noise.shape[0]
        row = lax.broadcasted_iota(jnp.int32, (level.own_rows, LANES), 0)
        lane = lane_index((level.own_rows, LANES))
        for p in range(noise.shape[1] // LANES):
            at = slice(p * LANES, (p + 1) * LANES)
            if p < level.pairs:
                part = bi[p, level.error - 2 : level.error - 2 + level.own_rows, :]
                if level.own_rows != level.rows:
                    part = jnp.where(row < level.rows, part, 0.0)
                if 2 * p + 1 >= level.cols:
                    part = jnp.where(lane < LANES // 2, part, 0.0)
                noise[0 : level.own_rows, at] = part.astype(BF16)
                if level.own_rows < total_rows:
                    noise[level.own_rows : total_rows, at] = jnp.zeros((total_rows - level.own_rows, LANES), BF16)
            else:
                noise[:, at] = jnp.zeros((total_rows, LANES), BF16)


def coarsen(fine, coarse, gu, rc, emit, strip, strips):
    count = fine.k_count
    start = fine.gu_start
    for p in range(fine.pairs):
        f = [gu[p, pl.ds(start + a, count, stride=4), :] for a in range(6)]
        rc[p, pl.ds(0, count, stride=3), :] = 0.125 * f[0] + 0.875 * f[1] + 0.375 * f[2]
        rc[p, pl.ds(1, count, stride=3), :] = 0.625 * f[2] + 0.625 * f[3]
        rc[p, pl.ds(2, count, stride=3), :] = 0.375 * f[3] + 0.875 * f[4] + 0.125 * f[5]
    top = -3 * fine.k_first
    low = top + coarse.rows - 1
    on_top = jnp.where(strip == 0, 1.0, 0.0).astype(F32)
    on_low = jnp.where(strip == strips - 1, 1.0, 0.0).astype(F32)
    all_pairs = slice(0, fine.pairs)
    rc[all_pairs, top : top + 1, :] = rc[all_pairs, top : top + 1, :] + on_top * rc[all_pairs, top - 1 : top, :]
    rc[all_pairs, low : low + 1, :] = rc[all_pairs, low : low + 1, :] + on_low * rc[all_pairs, low + 1 : low + 2, :]
    matrix = column_weights(fine.cols, coarse.cols)
    matrix = np.pad(matrix, ((0, 2 * coarse.pairs - coarse.cols), (0, 2 * fine.pairs - fine.cols)))
    lane = lane_index((1, LANES))

    def weights(low_lanes, high_lanes):
        return jnp.where(lane < LANES // 2, np.float32(low_lanes), np.float32(high_lanes))

    for m in range(coarse.pairs):
        total = None
        for q in range(fine.pairs):
            same = (matrix[2 * m, 2 * q], matrix[2 * m + 1, 2 * q + 1])
            cross = (matrix[2 * m, 2 * q + 1], matrix[2 * m + 1, 2 * q])
            value = rc[q, 0 : 3 * count, :] if any(same) or any(cross) else None
            for pair, moved in ((same, False), (cross, True)):
                if any(pair):
                    term = (half_swap(value) if moved else value) * weights(*pair)
                    total = term if total is None else total + term
        emit(m, total)


def fill_input(level, xb, act, top, low, tmp, payload_rows):
    margin = level.x_margin
    zero = jnp.zeros((level.alloc, LANES), F32)
    xb[0, 0 : level.alloc, :] = zero
    xb[level.pairs + 1, 0 : level.alloc, :] = zero
    lane = lane_index((1, LANES))
    for p in range(level.pairs):
        at = slice(p * LANES, (p + 1) * LANES)
        upper, own, lower = top(at), act[0 : level.own_rows, at].astype(F32), low(at)
        if 2 * p + 1 >= level.cols:
            upper, own, lower = (jnp.where(lane < LANES // 2, v, 0.0) for v in (upper, own, lower))
        end = margin + level.rows
        if end + margin < level.alloc:
            xb[p + 1, end + margin : level.alloc, :] = jnp.zeros((level.alloc - end - margin, LANES), F32)
        tmp[0, 0:32, :] = upper
        tmp[1, 0:32, :] = lower
        xb[p + 1, 0:margin, :] = tmp[0, payload_rows - margin : payload_rows, :]
        xb[p + 1, margin : margin + level.own_rows, :] = own
        xb[p + 1, end : end + margin, :] = tmp[1, 0:margin, :]
        after = up_to(end + margin, 1)
        if margin + level.own_rows > after:
            xb[p + 1, after : margin + level.own_rows, :] = jnp.zeros((margin + level.own_rows - after, LANES), F32)


def flat_to_pairs(level, flat, xb):
    zero = jnp.zeros((level.alloc, LANES), F32)
    xb[0, 0 : level.alloc, :] = zero
    xb[level.pairs + 1, 0 : level.alloc, :] = zero
    for p in range(level.pairs):
        xb[p + 1, 0 : level.x_rows, :] = flat[p * level.x_rows : (p + 1) * level.x_rows, :]
        if level.alloc > level.x_rows:
            xb[p + 1, level.x_rows : level.alloc, :] = jnp.zeros((level.alloc - level.x_rows, LANES), F32)


def call(body, out_shape, scratch, operands, flops, nbytes, final=()):
    operands = [pltpu.with_memory_space_constraint(x, pltpu.VMEM) for x in operands]
    out_shape = [s if i in final else pltpu.VMEM(s.shape, s.dtype) for i, s in enumerate(out_shape)]
    return pl.pallas_call(
        body,
        out_shape=out_shape,
        in_specs=[pl.BlockSpec(memory_space=pltpu.VMEM)] * len(operands),
        out_specs=[pl.BlockSpec(memory_space=pltpu.VMEM)] * len(out_shape),
        scratch_shapes=scratch,
        compiler_params=pltpu.CompilerParams(vmem_limit_bytes=VMEM_BYTES),
        cost_estimate=pl.CostEstimate(flops=flops, bytes_accessed=nbytes, transcendentals=0),
    )(*operands)


def sds(shape, dtype):
    return jax.ShapeDtypeStruct(shape, dtype)


def buffer(level, extra):
    return pltpu.VMEM((level.pairs + extra, level.alloc, LANES), F32)


def local(strips, sections, cotangent, activations, weights, biases):
    row_count, flat_width = activations.shape[2:]
    channels = weights.shape[-1]
    cols = flat_width // channels
    assert 2 * channels == LANES and sections == 4 and cotangent.shape[0] == 1
    levels = levels_of(row_count, cols, sections)
    fine, second, third, last = levels
    x_margin, g_margin = fine.x_margin, fine.error
    payload = up_to(x_margin + g_margin, 16)
    pair_count = fine.pairs
    cot = cotangent[0]
    act = activations[0, 0]
    taps = weights.reshape(2 * TAPS, channels, channels)
    bias = biases[0]
    chunk = 4

    def ids():
        return lax.axis_index("section"), lax.axis_index("strip")

    def halo_body(act_ref, cot_ref, swap_ref, cross_ref, xs, cs, ts):
        section, strip = ids()
        odd = lax.rem(strip, 2) == 1
        live = jnp.int32(fine.rows)
        for level in levels[1:]:
            live = jnp.where(section == level.level, level.rows, live)
        for p in range(pair_count):
            at = slice(p * LANES, (p + 1) * LANES)
            xs[p, :, :] = act_ref[:, at].astype(F32)
            cs[p, :, :] = cot_ref[:, at].astype(F32)
            ts[0, p, 0:x_margin, :] = xs[p, 0:x_margin, :]
            ts[0, p, x_margin : x_margin + g_margin, :] = cs[p, 0:g_margin, :]
            ts[1, p, 0:x_margin, :] = xs[p, pl.ds(live - x_margin, x_margin), :]
            ts[1, p, x_margin : x_margin + g_margin, :] = cs[p, row_count - g_margin : row_count, :]
            upper = ts[0, p, 0:payload, :]
            lower = ts[1, p, 0:payload, :]
            swap_ref[:, at] = jnp.where(odd, upper, lower).astype(BF16)
            cross_ref[:, at] = jnp.where(odd, lower, upper).astype(BF16)

    halo_shape = sds((payload, flat_width), BF16)
    to_swap, to_cross = call(
        halo_body,
        [halo_shape, halo_shape],
        [
            pltpu.VMEM((pair_count, row_count, LANES), F32),
            pltpu.VMEM((pair_count, row_count, LANES), F32),
            pltpu.VMEM((2, pair_count, payload, LANES), F32),
        ],
        [act, cot],
        10**6,
        10**6,
    )
    swap_pairs = [(i, i ^ 1) for i in range(strips)]
    cross_pairs = [(i, i + 1) for i in range(1, strips - 1, 2)] + [(i + 1, i) for i in range(1, strips - 1, 2)]
    from_cross = lax.ppermute(to_cross, "strip", cross_pairs)
    from_swap = lax.ppermute(to_swap, "strip", swap_pairs)

    def expand(tap_list, forward_ref, back_ref):
        for c in range(2):
            chosen = tap_list[c * TAPS : (c + 1) * TAPS]
            forward_ref[c, :, :] = toeplitz(chosen).astype(BF16)
            back_ref[c, :, :] = toeplitz_back(chosen).astype(BF16)

    def matrix_body(taps_ref, forward_ref, back_ref, packed_ref):
        values = [taps_ref[t].astype(F32) for t in range(2 * TAPS)]
        expand(values, forward_ref, back_ref)
        half = channels // 2
        for t in range(2 * TAPS):
            packed_ref[t * half : (t + 1) * half, :] = jnp.concatenate(
                [values[t][:half], values[t][half:]], axis=1
            ).astype(BF16)

    matrix_shape = sds((2, 6 * LANES, LANES), BF16)
    packed_rows = TAPS * channels
    fwd_own, back_own, packed_own = call(
        matrix_body,
        [matrix_shape, matrix_shape, sds((packed_rows, LANES), BF16)],
        [],
        [taps],
        10**6,
        10**6,
    )

    g_rows = second.rows + 2 * second.error
    g_flat = up_to(second.pairs * g_rows, 16)
    x_flat = up_to(max(second.pairs * second.x_rows, third.pairs * third.x_rows), 16)
    g_flat = max(g_flat, 16)
    ship_rows = max(x_flat + packed_rows, g_flat) + 16

    def halo_readers(swap_ref, cross_ref, strip):
        odd = lax.rem(strip, 2) == 1

        def top(at):
            return jnp.where(odd, swap_ref[:, at].astype(F32), cross_ref[:, at].astype(F32))

        def low(at):
            return jnp.where(odd, cross_ref[:, at].astype(F32), swap_ref[:, at].astype(F32))

        return top, low

    def chain_body(
        act_ref, cot_ref, swap_ref, cross_ref, fwd_ref, back_ref, packed_ref, bias_ref,
        hop_ref, ship_ref, noise_ref, hid_ref, ein_ref, eout_ref,
        xb, hb, db, gb, eo, ei, bi, gu, rc, flat, tmp, bias_tmp,
    ):
        section, strip = ids()
        top, low = halo_readers(swap_ref, cross_ref, strip)

        @pl.when(section == 0)
        def _():
            level = fine
            fill_input(level, xb, act_ref, top, low, tmp, x_margin)
            zero = jnp.zeros((level.alloc, LANES), F32)
            eo[0, 0 : level.alloc, :] = zero
            eo[level.pairs + 1, 0 : level.alloc, :] = zero
            for p in range(level.pairs):
                at = slice(p * LANES, (p + 1) * LANES)
                tmp[0, 0:payload, :] = top(at)
                tmp[1, 0:payload, :] = low(at)
                gb[p, 0:g_margin, :] = tmp[0, x_margin : x_margin + g_margin, :]
                gb[p, g_margin : g_margin + row_count, :] = cot_ref[:, at].astype(F32)
                gb[p, g_margin + row_count : 2 * g_margin + row_count, :] = tmp[
                    1, x_margin : x_margin + g_margin, :
                ]
            mask_out = image_mask(level, -level.error, level.out_rows, strip, strips)

            def error(first, size, value):
                part = gb[first : first + size, 0 : level.out_rows, :]
                eo[first + 1 : first + 1 + size, 0 : level.out_rows, :] = jnp.where(
                    mask_out, rounded(part * value), 0.0
                )

            forward(
                level, xb, hb, [fwd_ref.at[0], fwd_ref.at[1]], twice(bias_ref[...]), db, error, strip, strips, chunk
            )
            backward(
                level, eo, ei, [back_ref.at[0], back_ref.at[1]], db, gb, 0, noise_ref, gu, bi, strip, strips, chunk
            )

            def emit(m, rows):
                flat[m * g_rows : (m + 1) * g_rows, :] = rows[0:g_rows]

            coarsen(fine, second, gu, rc, emit, strip, strips)
            value = flat[0:g_flat, :].astype(BF16)
            hop_ref[...] = value
            ship_ref[0:g_flat, :] = value
            rows = level.rows
            for p in range(level.pairs + 1):
                hid_ref[p, :, :] = hb[p, level.error : level.error + rows + 16, :].astype(BF16)
                ein_ref[p, :, :] = ei[p, level.error - 1 : level.error - 1 + rows, :].astype(BF16)
                if p < level.pairs:
                    eout_ref[p, :, :] = eo[p + 1, level.error : level.error + rows, :].astype(BF16)

        for level in (second, third):

            @pl.when(section == level.level)
            def _(level=level):
                fill_input(level, xb, act_ref, top, low, tmp, x_margin)
                for p in range(level.pairs):
                    flat[p * level.x_rows : (p + 1) * level.x_rows, :] = xb[p + 1, 0 : level.x_rows, :]
                used = up_to(level.pairs * level.x_rows, 16)
                ship_ref[0:used, :] = flat[0:used, :].astype(BF16)
                ship_ref[x_flat : x_flat + packed_rows, :] = packed_ref[...]
                rest = twice(bias_ref[...])
                for term in range(3):
                    part = rounded(rest)
                    bias_tmp[2 * term : 2 * term + 2, :] = part
                    rest = rest - part
                bias_tmp[6:16, :] = jnp.zeros((10, LANES), F32)
                ship_ref[x_flat + packed_rows : ship_rows, :] = bias_tmp[...].astype(BF16)

    hop_shape = sds((g_flat, LANES), BF16)
    ship_shape = sds((ship_rows, LANES), BF16)
    hop, ship, noise_first, hid_first, ein_first, eout_first = call(
        chain_body,
        [
            hop_shape,
            ship_shape,
            sds((row_count, flat_width), BF16),
            sds((fine.pairs + 1, row_count + 16, LANES), BF16),
            sds((fine.pairs + 1, row_count, LANES), BF16),
            sds((fine.pairs, row_count, LANES), BF16),
        ],
        [
            buffer(fine, 2),
            buffer(fine, 1),
            buffer(fine, 1),
            buffer(fine, 0),
            buffer(fine, 2),
            buffer(fine, 1),
            buffer(fine, 0),
            buffer(fine, 0),
            pltpu.VMEM((fine.pairs, 3 * fine.k_count, LANES), F32),
            pltpu.VMEM((up_to(max(g_flat, x_flat), 8) + 16, LANES), F32),
            pltpu.VMEM((2, max(payload, 32), LANES), F32),
            pltpu.VMEM((16, LANES), F32),
        ],
        [act, cot, from_swap, from_cross, fwd_own, back_own, packed_own, bias],
        3 * 10**9,
        4 * 10**6,
    )

    def across(value, pairs):
        return lax.ppermute(value, "section", pairs)

    got_hop = across(hop, [(0, 3)])
    got_far = across(ship, [(0, 2), (1, 3)])
    got_near = across(ship, [(0, 1), (1, 2), (2, 3)])

    def forward_body(
        act_ref, swap_ref, cross_ref, fwd_ref, back_ref, bias_ref, far_ref, near_ref,
        din1, dout1, din2, dout2, din3, dout3, back1, back2, hid_ref, xown_ref,
        xb, hb, flat, fwd_tmp, tmp,
    ):
        section, strip = ids()
        top, low = halo_readers(swap_ref, cross_ref, strip)
        slots = {1: (din1, dout1, back1), 2: (din2, dout2, back2), 3: (din3, dout3, None)}

        def run(level, kernels, bias_rows):
            d_in, d_out, _ = slots[level.level]

            def store(first, size, value):
                d_out[first : first + size, 0 : level.out_rows, :] = value

            forward(level, xb, hb, kernels, bias_rows, d_in, store, strip, strips, chunk)

        def own(level):
            fill_input(level, xb, act_ref, top, low, tmp, x_margin)
            run(level, [fwd_ref.at[0], fwd_ref.at[1]], twice(bias_ref[...]))
            hid_ref[0 : level.pairs + 1, 0 : level.alloc, :] = hb[0 : level.pairs + 1, 0 : level.alloc, :]
            xown_ref[0 : level.pairs + 2, 0 : level.alloc, :] = xb[0 : level.pairs + 2, 0 : level.alloc, :]
            back = slots[level.level][2]
            if back is not None:
                back[...] = back_ref[...]

        def shipped(level, source):
            half = channels // 2
            values = []
            for t in range(2 * TAPS):
                pack = source[x_flat + t * half : x_flat + (t + 1) * half, :].astype(F32)
                values.append(jnp.concatenate([pack[:, :channels], pack[:, channels:]], axis=0))
            expand(values, fwd_tmp, slots[level.level][2])
            used = up_to(level.pairs * level.x_rows, 16)
            flat[0:used, :] = source[0:used, :].astype(F32)
            flat_to_pairs(level, flat, xb)
            terms = source[x_flat + packed_rows : ship_rows, :].astype(F32)
            run(level, [fwd_tmp.at[0], fwd_tmp.at[1]], terms[0:2] + terms[2:4] + terms[4:6])

        @pl.when(section == 1)
        def _():
            own(second)

        @pl.when(section == 2)
        def _():
            own(third)
            shipped(second, near_ref)

        @pl.when(section == 3)
        def _():
            own(last)
            shipped(second, far_ref)
            shipped(third, near_ref)

    def field(level, extra):
        return sds((level.pairs + extra, level.alloc, LANES), F32)

    outs = call(
        forward_body,
        [
            field(second, 1), field(second, 0),
            field(third, 1), field(third, 0),
            field(last, 1), field(last, 0),
            matrix_shape, matrix_shape,
            field(second, 1), field(second, 2),
        ],
        [
            buffer(second, 2),
            buffer(second, 1),
            pltpu.VMEM((x_flat + 16, LANES), F32),
            pltpu.VMEM((2, 6 * LANES, LANES), BF16),
            pltpu.VMEM((2, max(payload, 32), LANES), F32),
        ],
        [act, from_swap, from_cross, fwd_own, back_own, bias, got_far, got_near],
        2 * 10**9,
        4 * 10**6,
    )
    din1, dout1, din2, dout2, din3, dout3, back1, back2, hid_own, x_own = outs

    grad_rows = up_to(TAPS * channels // 2 + 1, 16)

    def backward_body(
        act_ref, swap_ref, cross_ref, noise0, hid0, ein0, eout0,
        hop_ref, far_ref, near_ref,
        din1, dout1, din2, dout2, din3, dout3, back1, back2, back3, hid_ref, x_ref,
        noise_ref, keep_ref, send_ref,
        xb, hb, gb, eo, ei, bi, gu, rc, flat, tmp, pair_out,
    ):
        section, strip = ids()
        odd = lax.rem(strip, 2) == 1
        slots = {1: (din1, dout1, back1), 2: (din2, dout2, back2), 3: (din3, dout3, back3)}

        def gradients(level, source, hidden, err_in, err_out, rows_at):
            scale = np.float32(1.0 / math.sqrt(strips * level.rows * level.cols))
            first = kernel_terms(source, err_in, level.odd_pairs, rows_at[2], rows_at[0], level)
            pack_kernel_terms(pair_out.at[0], *first, scale)
            then = kernel_terms(hidden, err_out, level.pairs, rows_at[3], rows_at[1], level)
            pack_kernel_terms(pair_out.at[1], *then, scale)

        def step(level, grad_row, keep):
            d_in, d_out, back = slots[level.level]
            mask = image_mask(level, -level.error, level.out_rows, strip, strips)
            zero = jnp.zeros((level.alloc, LANES), F32)
            eo[0, 0 : level.alloc, :] = zero
            eo[level.pairs + 1, 0 : level.alloc, :] = zero
            for p in range(level.pairs):
                part = gb[p, grad_row : grad_row + level.out_rows, :] * d_out[p, 0 : level.out_rows, :]
                eo[p + 1, 0 : level.out_rows, :] = jnp.where(mask[0], rounded(part), 0.0)
            backward(
                level, eo, ei, [back.at[0], back.at[1]], d_in, gb, grad_row,
                noise_ref if keep else None, None if keep else gu, bi, strip, strips, chunk,
            )

        def take(source):
            flat[0:g_flat, :] = source[0:g_flat, :].astype(F32)
            for p in range(second.pairs):
                gb[p, 0:g_rows, :] = flat[p * g_rows : (p + 1) * g_rows, :]

        def down(upper, lower):
            def emit(m, rows):
                gb[m, 0 : 3 * upper.k_count, :] = rounded(rows)

            coarsen(upper, lower, gu, rc, emit, strip, strips)

        def finish(level):
            gradients(
                level, x_ref, hid_ref, ei, eo.at[1 : 1 + level.pairs],
                (level.error - 1, level.error, level.error + 1, level.error),
            )

        @pl.when(section == 0)
        def _():
            noise_ref[...] = noise0[...]
            top, low = halo_readers(swap_ref, cross_ref, strip)
            fill_input(fine, xb, act_ref, top, low, tmp, x_margin)
            rows = fine.rows
            for p in range(fine.pairs + 1):
                hb[p, 0 : rows + 16, :] = hid0[p, :, :].astype(F32)
                ei[p, 0:rows, :] = ein0[p, :, :].astype(F32)
                if p < fine.pairs:
                    eo[p, 0:rows, :] = eout0[p, :, :].astype(F32)
            gradients(fine, xb, hb, ei, eo, (0, 0, fine.error + 1, 0))

        @pl.when(section == 1)
        def _():
            take(near_ref)
            step(second, 0, True)
            finish(second)

        @pl.when(section == 2)
        def _():
            take(far_ref)
            step(second, 0, False)
            down(second, third)
            step(third, second.up_shift, True)
            finish(third)

        @pl.when(section == 3)
        def _():
            take(hop_ref)
            step(second, 0, False)
            down(second, third)
            step(third, second.up_shift, False)
            down(third, last)
            step(last, third.up_shift, True)
            finish(last)

        first, then = pair_out[0], pair_out[1]
        keep_ref[...] = jnp.where(odd, then, first)
        send_ref[...] = jnp.where(odd, first, then)

    half_shape = sds((grad_rows, LANES), F32)
    noise, keep, send = call(
        backward_body,
        [sds((row_count, flat_width), BF16), half_shape, half_shape],
        [
            buffer(fine, 2),
            buffer(fine, 1),
            buffer(fine, 0),
            buffer(fine, 2),
            buffer(fine, 1),
            buffer(fine, 0),
            buffer(fine, 0),
            pltpu.VMEM((second.pairs, 3 * second.k_count, LANES), F32),
            pltpu.VMEM((g_flat + 16, LANES), F32),
            pltpu.VMEM((2, max(payload, 32), LANES), F32),
            pltpu.VMEM((2, grad_rows, LANES), F32),
        ],
        [
            act, from_swap, from_cross, noise_first, hid_first, ein_first, eout_first,
            got_hop, got_far, got_near,
            din1, dout1, din2, dout2, din3, dout3, back1, back2, back_own, hid_own, x_own,
        ],
        3 * 10**9,
        6 * 10**6,
        final=(0,),
    )

    total = keep + lax.ppermute(send, "strip", swap_pairs)
    hop_size = 2
    while hop_size < strips:
        mine = lax.reduce_precision(total, 8, 7)
        other = lax.ppermute(mine.astype(BF16), "strip", [(i, i ^ hop_size) for i in range(strips)])
        total = mine + other.astype(F32)
        hop_size *= 2
    other = lax.ppermute(total, "strip", swap_pairs)

    def final_body(mine_ref, other_ref, kernel_ref, bias_ref):
        _, strip = ids()
        odd = lax.rem(strip, 2) == 1
        half = channels
        for c in range(2):
            if c == 0:
                value = jnp.where(odd, other_ref[...], mine_ref[...])
            else:
                value = jnp.where(odd, mine_ref[...], other_ref[...])
            swapped = half_swap(value)
            for dy in range(3):
                kernel_ref[c, dy * 192 : dy * 192 + 96, :] = value[dy * 96 : dy * 96 + 96, :half]
                kernel_ref[c, dy * 192 + 96 : dy * 192 + 192, :] = swapped[dy * 96 : dy * 96 + 96, :half]
            bias_ref[c : c + 1, :] = value[288:289, :half]

    kernel_sum, bias_sum = call(
        final_body,
        [sds((2, TAPS * channels, channels), F32), sds((2, channels), F32)],
        [],
        [total, other],
        10**6,
        10**6,
        final=(0, 1),
    )
    return (
        noise[None, None],
        kernel_sum.reshape(1, 2, 3, 3, channels, channels),
        bias_sum[None],
    )


def solution(mesh):
    strips = mesh.shape["strip"]
    sections = mesh.shape["section"]
    return jax.shard_map(
        functools.partial(local, strips, sections),
        mesh=mesh,
        in_specs=(
            P(None, "strip", None),
            P("section", None, "strip", None),
            P("section", None, None, None, None, None),
            P("section", None, None),
        ),
        out_specs=(
            P("section", None, "strip", None),
            P("section", None, None, None, None, None),
            P("section", None, None),
        ),
        check_vma=False,
    )
```

```python
import functools
import math

import jax
import jax.numpy as jnp
import numpy as np
from jax import lax
from jax.experimental import pallas as pl
from jax.experimental.pallas import tpu as pltpu
from jax.sharding import PartitionSpec as P

LEAK = 0.05
LANES = 128
F32 = jnp.float32
BF16 = jnp.bfloat16
TAPS = 9
VMEM_BYTES = 24 * 1024 * 1024


def up_to(value, step):
    return -(-value // step) * step


class Level:
    def __init__(self, level, rows, cols):
        self.level = level
        self.rows = rows * 3**level // 4**level
        self.cols = cols * 3**level // 4**level
        self.pairs = -(-self.cols // 2)
        self.odd_pairs = -(-(self.cols + 1) // 2)

    def margin(self, error):
        self.error = error
        self.x_margin = error + 2
        self.x_rows = self.rows + 2 * (error + 2)
        self.hidden_rows = up_to(self.rows + 2 * (error + 1), 16)
        self.out_rows = up_to(self.rows + 2 * error, 16)
        self.in_rows = up_to(self.rows + 2 * (error - 1), 16)
        self.back_rows = up_to(self.rows + 2 * (error - 2), 16)
        self.own_rows = up_to(self.rows, 16)
        self.alloc = up_to(max(self.hidden_rows, self.x_margin + self.own_rows + 2) + 2, 8)


def levels_of(rows, cols, count):
    levels = [Level(s, rows, cols) for s in range(count)]
    levels[-1].margin(2)
    for s in range(count - 2, -1, -1):
        fine, coarse = levels[s], levels[s + 1]
        first = -coarse.error
        last = coarse.rows + coarse.error - 1
        low = 4 * (first // 3) + (-1, 1, 2)[first % 3]
        high = 4 * (last // 3) + (1, 2, 4)[last % 3]
        fine.margin(max(-low, high - fine.rows + 1) + 2)
        fine.k_first = first // 3
        fine.k_count = up_to(last // 3 - fine.k_first + 1, 8)
        fine.up_shift = -3 * fine.k_first - coarse.error
        start = fine.error - 2 + 4 * fine.k_first - 1
        fine.gu_row = max(0, -start)
        fine.gu_start = start + fine.gu_row
        assert fine.rows % 4 == 0
    return levels


def column_weights(fine, coarse):
    matrix = np.zeros((coarse, fine), np.float32)
    for x in range(fine):
        num = max((2 * x + 1) * coarse - fine, 0)
        low = num // (2 * fine)
        frac = np.float32(num - 2 * fine * low) / np.float32(2 * fine)
        matrix[low, x] += np.float32(1.0) - frac
        matrix[min(low + 1, coarse - 1), x] += frac
    return matrix


def lane_index(shape):
    return lax.broadcasted_iota(jnp.int32, shape, len(shape) - 1)


def half_swap(value):
    return pltpu.roll(value, LANES // 2, value.ndim - 1)


def twice(bias):
    return jnp.concatenate([bias, bias], axis=1)


def rounded(value):
    return value.astype(BF16).astype(F32)


def image_mask(level, base, count, strip, strips):
    row = lax.broadcasted_iota(jnp.int32, (1, count, LANES), 1) + base
    low = jnp.where(strip == 0, 0, -(10**6))
    high = jnp.where(strip == strips - 1, level.rows, 10**6)
    return (row >= low) & (row < high)


def odd_column_mask(level, first, count, mask):
    if first > 0 and 2 * (first + count - 1) < level.cols:
        return mask
    shape = (count, mask.shape[1], LANES)
    half = lax.broadcasted_iota(jnp.int32, shape, 2) // (LANES // 2)
    col = 2 * (first + lax.broadcasted_iota(jnp.int32, shape, 0)) - 1 + half
    return mask & (col >= 0) & (col < level.cols)


def conv(source, kernel, count, segments, chunk, emit):
    total = sum(rows for _, rows in segments)
    for first in range(0, count, chunk):
        size = min(chunk, count - first)
        parts = []
        for dy in range(3):
            blocks = [source[first : first + size + 1, a + dy : a + dy + rows, :] for a, rows in segments]
            block = blocks[0] if len(blocks) == 1 else jnp.concatenate(blocks, axis=1)
            block = block.astype(BF16)
            parts.append(block[:size].reshape(size * total, LANES))
            parts.append(block[1:].reshape(size * total, LANES))
        stacked = jnp.concatenate(parts, axis=1)
        result = jnp.dot(stacked, kernel[...], preferred_element_type=F32).reshape(size, total, LANES)
        at = 0
        for a, rows in segments:
            emit(first, size, a, rows, result[:, at : at + rows])
            at += rows


def kernel_terms(source, error, count, source_row, error_row, level):
    rows = level.own_rows
    err = error[0:count, error_row : error_row + rows, :]
    if rows != level.rows:
        row = lax.broadcasted_iota(jnp.int32, (1, rows, LANES), 1)
        err = jnp.where(row < level.rows, err, 0.0)
    total = jnp.sum(err, axis=(0, 1)).reshape(1, LANES)
    parts = []
    for dy in range(3):
        block = source[0 : count + 1, source_row + dy : source_row + dy + rows, :].astype(BF16)
        parts.append(block[:count].reshape(count * rows, LANES))
        parts.append(block[1:].reshape(count * rows, LANES))
    stacked = jnp.concatenate(parts, axis=1)
    product = lax.dot_general(
        err.astype(BF16).reshape(count * rows, LANES),
        stacked,
        (((0,), (0,)), ((), ())),
        preferred_element_type=F32,
    )
    return product, total


def pack_kernel_terms(out_ref, product, total, scale):
    half = LANES // 2
    by_tap = product.T * scale
    lane = lane_index((1, LANES))
    for dy in range(3):
        block = by_tap[dy * 2 * LANES : (dy + 1) * 2 * LANES]
        folded = block[: 3 * half] + half_swap(block)[half:]
        out_ref[dy * 96 : dy * 96 + 96, :] = jnp.where(lane < half, folded[:96], half_swap(folded[96:]))
    bias = (total + half_swap(total)) * scale
    out_ref[288:304, :] = jnp.broadcast_to(bias, (16, LANES))


def toeplitz(taps):
    half = LANES // 2
    zero = jnp.zeros((half, half), F32)
    rows = []
    for dy in range(3):
        for k in range(4):
            left = taps[dy * 3 + k] if k < 3 else zero
            right = taps[dy * 3 + k - 1] if k > 0 else zero
            rows.append(jnp.concatenate([left, right], axis=1))
    return jnp.concatenate(rows, axis=0)


def toeplitz_back(taps):
    half = LANES // 2
    zero = jnp.zeros((half, half), F32)
    columns = []
    for dy in range(3):
        for k in range(4):
            top = taps[(2 - dy) * 3 + 2 - k] if k < 3 else zero
            bottom = taps[(2 - dy) * 3 + 3 - k] if k > 0 else zero
            columns.append(jnp.concatenate([top, bottom], axis=0))
    pairs = [jnp.concatenate(columns[i : i + 2], axis=1).T for i in range(0, 12, 2)]
    return jnp.concatenate(pairs, axis=0)


def zero_tail(ref, level, rows):
    if level.alloc > rows:
        ref[0 : level.pairs + 1, rows : level.alloc, :] = jnp.zeros((level.pairs + 1, level.alloc - rows, LANES), F32)
    if level.odd_pairs < level.pairs + 1:
        ref[level.odd_pairs : level.pairs + 1, 0 : level.alloc, :] = jnp.zeros(
            (level.pairs + 1 - level.odd_pairs, level.alloc, LANES), F32
        )


def zero_edges(ref, level):
    zero = jnp.zeros((level.alloc, LANES), F32)
    ref[0, 0 : level.alloc, :] = zero
    ref[level.pairs + 1, 0 : level.alloc, :] = zero


def slope(value):
    return LEAK + (1.0 - LEAK) * (0.5 + 0.5 * jnp.tanh(0.5 * value))


def forward(level, xb, hb, kernels, bias, d_in, d_out, place, chunk, hidden_parts=None, out_parts=None):
    strip, strips = place
    bias_in, bias_out = bias[0:1], bias[1:2]

    def first_layer(first, size, a, rows, value):
        mask = image_mask(level, a - (level.error + 1), rows, strip, strips)
        pre = value + bias_in
        small = jnp.exp(-jnp.abs(pre))
        soft = jnp.maximum(pre, 0.0) + jnp.log(1.0 + small)
        act = LEAK * pre + (1.0 - LEAK) * soft
        keep = odd_column_mask(level, first, size, mask)
        hb[first : first + size, a : a + rows, :] = jnp.where(keep, rounded(act), 0.0)
        d_in[first : first + size, a : a + rows, :] = slope(pre)

    conv(xb, kernels[0], level.odd_pairs, hidden_parts or [(0, level.hidden_rows)], chunk, first_layer)

    def second_layer(first, size, a, rows, value):
        d_out(first, size, a, rows, slope(value + bias_out))

    conv(hb, kernels[1], level.pairs, out_parts or [(0, level.out_rows)], chunk, second_layer)


def backward(level, eo, ei, kernels, d_in, grad, grad_row, bi, gu, place, chunk, in_parts=None, back_parts=None):
    strip, strips = place

    def inner(first, size, a, rows, value):
        mask = image_mask(level, a - (level.error - 1), rows, strip, strips)
        keep = odd_column_mask(level, first, size, mask)
        part = d_in[first : first + size, 2 + a : 2 + a + rows, :]
        ei[first : first + size, a : a + rows, :] = jnp.where(keep, rounded(value * part), 0.0)

    conv(eo, kernels[1], level.odd_pairs, in_parts or [(0, level.in_rows)], chunk, inner)

    def outer(first, size, a, rows, value):
        if bi is not None:
            bi[first : first + size, a : a + rows, :] = value
        if gu is not None:
            mask = image_mask(level, a - (level.error - 2), rows, strip, strips)
            part = grad[first : first + size, grad_row + 2 + a : grad_row + 2 + a + rows, :]
            at = level.gu_row + a
            gu[first : first + size, at : at + rows, :] = jnp.where(mask, rounded(part + value), 0.0)

    conv(ei, kernels[0], level.pairs, back_parts or [(0, level.back_rows)], chunk, outer)


def write_noise(level, bi, noise):
    total_rows = noise.shape[0]
    row = lax.broadcasted_iota(jnp.int32, (level.own_rows, LANES), 0)
    lane = lane_index((level.own_rows, LANES))
    for p in range(noise.shape[1] // LANES):
        at = slice(p * LANES, (p + 1) * LANES)
        if p < level.pairs:
            part = bi[p, level.error - 2 : level.error - 2 + level.own_rows, :]
            if level.own_rows != level.rows:
                part = jnp.where(row < level.rows, part, 0.0)
            if 2 * p + 1 >= level.cols:
                part = jnp.where(lane < LANES // 2, part, 0.0)
            noise[0 : level.own_rows, at] = part.astype(BF16)
            if level.own_rows < total_rows:
                noise[level.own_rows : total_rows, at] = jnp.zeros((total_rows - level.own_rows, LANES), BF16)
        else:
            noise[:, at] = jnp.zeros((total_rows, LANES), BF16)


def coarsen(fine, coarse, gu, rc, ranges, spans, emit, place, edges=True):
    strip, strips = place
    for k, count in ranges:
        start = fine.gu_start + 4 * (k - fine.k_first)
        at = 3 * (k - fine.k_first)
        for p in range(fine.pairs):
            f = [gu[p, pl.ds(start + a, count, stride=4), :] for a in range(6)]
            rc[p, pl.ds(at, count, stride=3), :] = 0.125 * f[0] + 0.875 * f[1] + 0.375 * f[2]
            rc[p, pl.ds(at + 1, count, stride=3), :] = 0.625 * f[2] + 0.625 * f[3]
            rc[p, pl.ds(at + 2, count, stride=3), :] = 0.375 * f[3] + 0.875 * f[4] + 0.125 * f[5]
    if edges:
        top = -3 * fine.k_first
        low = top + coarse.rows - 1
        on_top = jnp.where(strip == 0, 1.0, 0.0).astype(F32)
        on_low = jnp.where(strip == strips - 1, 1.0, 0.0).astype(F32)
        every = slice(0, fine.pairs)
        rc[every, top : top + 1, :] = rc[every, top : top + 1, :] + on_top * rc[every, top - 1 : top, :]
        rc[every, low : low + 1, :] = rc[every, low : low + 1, :] + on_low * rc[every, low + 1 : low + 2, :]
    matrix = column_weights(fine.cols, coarse.cols)
    matrix = np.pad(matrix, ((0, 2 * coarse.pairs - coarse.cols), (0, 2 * fine.pairs - fine.cols)))
    lane = lane_index((1, LANES))

    def weights(low_lanes, high_lanes):
        return jnp.where(lane < LANES // 2, np.float32(low_lanes), np.float32(high_lanes))

    for span, (row, rows) in enumerate(spans):
        at = row - 3 * fine.k_first
        for m in range(coarse.pairs):
            total = None
            for q in range(fine.pairs):
                same = (matrix[2 * m, 2 * q], matrix[2 * m + 1, 2 * q + 1])
                cross = (matrix[2 * m, 2 * q + 1], matrix[2 * m + 1, 2 * q])
                value = rc[q, at : at + rows, :] if any(same) or any(cross) else None
                for pair, moved in ((same, False), (cross, True)):
                    if any(pair):
                        term = (half_swap(value) if moved else value) * weights(*pair)
                        total = term if total is None else total + term
            emit(m, span, total)


def own_input(level, xb, act):
    zero_edges(xb, level)
    lane = lane_index((1, LANES))
    for p in range(level.pairs):
        own = act[0 : level.own_rows, p * LANES : (p + 1) * LANES].astype(F32)
        if 2 * p + 1 >= level.cols:
            own = jnp.where(lane < LANES // 2, own, 0.0)
        xb[p + 1, level.x_margin : level.x_margin + level.own_rows, :] = own


def zero_after(level, xb):
    end = level.x_rows
    if end < level.alloc:
        xb[1 : level.pairs + 1, end : level.alloc, :] = jnp.zeros((level.pairs, level.alloc - end, LANES), F32)


def halo_input(level, xb, top, low, tmp, payload_rows):
    margin = level.x_margin
    end = margin + level.rows
    lane = lane_index((1, LANES))
    for p in range(level.pairs):
        at = slice(p * LANES, (p + 1) * LANES)
        upper, lower = top(at), low(at)
        if 2 * p + 1 >= level.cols:
            upper, lower = (jnp.where(lane < LANES // 2, v, 0.0) for v in (upper, lower))
        tmp[0, 0 : upper.shape[0], :] = upper
        tmp[1, 0 : lower.shape[0], :] = lower
        xb[p + 1, 0:margin, :] = tmp[0, payload_rows - margin : payload_rows, :]
        xb[p + 1, end : end + margin, :] = tmp[1, 0:margin, :]
    zero_after(level, xb)


def shipped_input(level, xb, own):
    zero_edges(xb, level)
    for p in range(level.pairs):
        xb[p + 1, 0 : level.x_rows, :] = own[p * level.x_rows : (p + 1) * level.x_rows, :]
    zero_after(level, xb)


def call(body, out_shape, scratch, operands, final=(), outside=(), aliases=None, flops=1000):
    operands = [
        pltpu.with_memory_space_constraint(x, pltpu.HBM if i in outside else pltpu.VMEM)
        for i, x in enumerate(operands)
    ]
    out_shape = [s if i in final else pltpu.VMEM(s.shape, s.dtype) for i, s in enumerate(out_shape)]
    return pl.pallas_call(
        body,
        out_shape=out_shape,
        in_specs=[pl.BlockSpec(memory_space=pltpu.VMEM)] * len(operands),
        out_specs=[pl.BlockSpec(memory_space=pltpu.VMEM)] * len(out_shape),
        scratch_shapes=scratch,
        input_output_aliases=aliases or {},
        compiler_params=pltpu.CompilerParams(vmem_limit_bytes=VMEM_BYTES),
        cost_estimate=pl.CostEstimate(flops=flops, bytes_accessed=1000, transcendentals=0),
    )(*operands)


def sds(shape, dtype):
    return jax.ShapeDtypeStruct(shape, dtype)


def field(level, extra):
    return sds((level.pairs + extra, level.alloc, LANES), F32)


def buffer(level, extra):
    return pltpu.VMEM((level.pairs + extra, level.alloc, LANES), F32)


def local(strips, sections, cotangent, activations, weights, biases):
    row_count, flat_width = activations.shape[2:]
    channels = weights.shape[-1]
    half = channels // 2
    cols = flat_width // channels
    assert 2 * channels == LANES and sections == 4 and cotangent.shape[0] == 1
    levels = levels_of(row_count, cols, sections)
    fine, second, third, last = levels
    x_margin, g_margin = fine.x_margin, fine.error
    payload = up_to(x_margin + g_margin, 16)
    pair_count = fine.pairs
    chunk = 4

    def place():
        return lax.axis_index("strip"), strips

    def is_odd():
        return lax.rem(lax.axis_index("strip"), 2) == 1

    packed_rows = TAPS * channels
    own_flat = up_to(third.pairs * third.x_rows, 16)
    ship_rows = own_flat + packed_rows + 16

    def halo_body(
        act_hbm, cot_hbm, bias_hbm, act_ref, cot_ref, both_ref, swap_ref, cross_ref, xs, cs, ts
    ):
        both_ref[0:2, :] = twice(bias_hbm[...])
        section = lax.axis_index("section")
        odd = is_odd()

        live = jnp.int32(fine.rows)
        for level in levels[1:]:
            live = jnp.where(section == level.level, level.rows, live)
        for p in range(pair_count):
            at = slice(p * LANES, (p + 1) * LANES)
            act_ref[:, at] = act_hbm[:, at]
            cot_ref[:, at] = cot_hbm[:, at]
            xs[p, :, :] = act_hbm[:, at].astype(F32)
            cs[p, :, :] = cot_hbm[:, at].astype(F32)
            ts[0, p, 0:x_margin, :] = xs[p, 0:x_margin, :]
            ts[0, p, x_margin : x_margin + g_margin, :] = cs[p, 0:g_margin, :]
            ts[1, p, 0:x_margin, :] = xs[p, pl.ds(live - x_margin, x_margin), :]
            ts[1, p, x_margin : x_margin + g_margin, :] = cs[p, row_count - g_margin : row_count, :]
            upper = ts[0, p, 0:payload, :]
            lower = ts[1, p, 0:payload, :]
            swap_ref[:, at] = jnp.where(odd, upper, lower).astype(BF16)
            cross_ref[:, at] = jnp.where(odd, lower, upper).astype(BF16)

    strip_shape = sds((row_count, flat_width), BF16)
    halo_shape = sds((payload, flat_width), BF16)
    taps = weights.reshape(2 * TAPS, channels, channels)
    act, cot, bias_own, to_swap, to_cross = call(
        halo_body,
        [
            strip_shape, strip_shape, sds((8, LANES), F32), halo_shape, halo_shape,
        ],
        [
            pltpu.VMEM((pair_count, row_count, LANES), F32),
            pltpu.VMEM((pair_count, row_count, LANES), F32),
            pltpu.VMEM((2, pair_count, payload, LANES), F32),
        ],
        [activations[0, 0], cotangent[0], biases[0]],
        outside=(0, 1, 2),
    )
    swap_pairs = [(i, i ^ 1) for i in range(strips)]
    cross_pairs = [(i, i + 1) for i in range(1, strips - 1, 2)] + [(i + 1, i) for i in range(1, strips - 1, 2)]
    from_cross = lax.ppermute(to_cross, "strip", cross_pairs)
    from_swap = lax.ppermute(to_swap, "strip", swap_pairs)


    def expand(tap_list, forward_ref, back_ref):
        for c in range(2):
            chosen = tap_list[c * TAPS : (c + 1) * TAPS]
            forward_ref[c, :, :] = toeplitz(chosen).astype(BF16)
            back_ref[c, :, :] = toeplitz_back(chosen).astype(BF16)

    def matrix_body(taps_ref, bias_ref, forward_ref, back_ref):
        expand([taps_ref[t].astype(F32) for t in range(2 * TAPS)], forward_ref, back_ref)

    matrix_shape = sds((2, 6 * LANES, LANES), BF16)
    fwd_own, back_own = call(matrix_body, [matrix_shape, matrix_shape], [], [taps, bias_own])

    def across(value, pairs):
        return lax.ppermute(value, "section", pairs)

    def ends(count):
        return [(0, 24), (count - 24, 24)]

    inside = [(16, row_count)]
    assert fine.error == 15 and fine.hidden_rows == row_count + 32 == fine.back_rows
    g_in = (4, second.rows - 8)
    g_end = second.error + g_in[0]
    in_rows = up_to(second.pairs * g_in[1], 16)
    rim_rows = up_to(second.pairs * 2 * g_end, 16)

    def error_of(level, gb, eo, mask_place):
        def error(first, size, a, rows, value):
            mask = image_mask(level, a - level.error, rows, *mask_place)
            part = gb[first : first + size, a : a + rows, :]
            eo[first + 1 : first + 1 + size, a : a + rows, :] = jnp.where(mask, rounded(part * value), 0.0)

        return error

    def inside_body(
        act_ref, cot_ref, fwd_ref, back_ref, bias_ref, hop_ref, xb, hb, db, gb, eo, ei, bi, gu, rc, flat,
    ):
        section = lax.axis_index("section")

        @pl.when(section == 0)
        def _():
            level = fine
            own_input(level, xb, act_ref)
            zero_after(level, xb)
            zero_edges(eo, level)
            zero_tail(hb, level, level.hidden_rows)
            zero_tail(ei, level, level.alloc)
            for p in range(level.pairs):
                gb[p, g_margin : g_margin + row_count, :] = cot_ref[:, p * LANES : (p + 1) * LANES].astype(F32)
            forward(
                level, xb, hb, [fwd_ref.at[0], fwd_ref.at[1]], bias_ref, db, error_of(level, gb, eo, place()),
                place(), chunk, inside, inside,
            )
            backward(
                level, eo, ei, [back_ref.at[0], back_ref.at[1]], db, gb, 0, bi, gu, place(), chunk, inside, inside
            )

            def emit(m, span, rows):
                flat[m * g_in[1] : (m + 1) * g_in[1], :] = rows

            coarsen(fine, second, gu, rc, [(0, 16)], [g_in], emit, place(), edges=False)
            hop_ref[...] = flat[0:in_rows, :].astype(BF16)

    coarse_buffer = pltpu.VMEM((fine.pairs, 3 * fine.k_count + 8, LANES), F32)
    state_shapes = [
        field(fine, 2), field(fine, 1), field(fine, 1), field(fine, 0),
        field(fine, 2), field(fine, 1), field(fine, 0), field(fine, 0),
    ]
    hop_in, *state = call(
        inside_body,
        [sds((in_rows, LANES), BF16), *state_shapes],
        [coarse_buffer, pltpu.VMEM((in_rows + 16, LANES), F32)],
        [act, cot, fwd_own, back_own, bias_own],
    )
    in_near = across(hop_in, [(0, 1)])

    def halo_readers(swap_ref, cross_ref):
        odd = is_odd()

        def top(at):
            return jnp.where(odd, swap_ref[:, at].astype(F32), cross_ref[:, at].astype(F32))

        def low(at):
            return jnp.where(odd, cross_ref[:, at].astype(F32), swap_ref[:, at].astype(F32))

        return top, low

    def rim_body(
        swap_ref, cross_ref, fwd_ref, back_ref, bias_ref, xi, hi, di, gi, oi, ii, bii, ui,
        rim_ref, noise_ref, xb, hb, db, gb, eo, ei, bi, gu, rc, flat, tmp,
    ):
        section = lax.axis_index("section")
        top, low = halo_readers(swap_ref, cross_ref)

        @pl.when(section == 0)
        def _():
            level = fine
            halo_input(level, xb, top, low, tmp, x_margin)
            for p in range(level.pairs):
                at = slice(p * LANES, (p + 1) * LANES)
                tmp[0, 0:payload, :] = top(at)
                tmp[1, 0:payload, :] = low(at)
                gb[p, 0:g_margin, :] = tmp[0, x_margin : x_margin + g_margin, :]
                gb[p, g_margin + row_count : 2 * g_margin + row_count, :] = tmp[
                    1, x_margin : x_margin + g_margin, :
                ]
            parts = ends(level.hidden_rows)
            forward(
                level, xb, hb, [fwd_ref.at[0], fwd_ref.at[1]], bias_ref, db, error_of(level, gb, eo, place()),
                place(), chunk, parts, parts,
            )
            backward(
                level, eo, ei, [back_ref.at[0], back_ref.at[1]], db, gb, 0, bi, gu, place(), chunk, parts, parts
            )

            def emit(m, span, rows):
                at = m * 2 * g_end + span * g_end
                flat[at : at + g_end, :] = rows[0:g_end]

            last_k = (second.rows + second.error) // 3
            coarsen(
                fine, second, gu, rc,
                [(fine.k_first, 8), (last_k - 7, 8)],
                [(-second.error, up_to(g_end, 8)), (g_in[0] + g_in[1], up_to(g_end, 8))],
                emit, place(),
            )
            rim_ref[...] = flat[0:rim_rows, :].astype(BF16)
            write_noise(level, bi, noise_ref)

    tmp_buffer = pltpu.VMEM((2, payload, LANES), F32)
    rim, noise_first, *state = call(
        rim_body,
        [sds((rim_rows, LANES), BF16), strip_shape, *state_shapes],
        [coarse_buffer, pltpu.VMEM((rim_rows + 32, LANES), F32), tmp_buffer],
        [from_swap, from_cross, fwd_own, back_own, bias_own, *state],
        aliases={5 + i: 2 + i for i in range(len(state_shapes))},
        flops=2 * 10**9,
    )
    rim_near = across(rim, [(0, 1)])

    def ship_body(act_ref, swap_ref, cross_ref, taps_ref, both_ref, rim_ref, ship_ref, tmp, flat, bias_tmp):
        top, low = halo_readers(swap_ref, cross_ref)

        @pl.when(lax.axis_index("section") == 2)
        def _():
            level = third
            margin = level.x_margin
            for p in range(level.pairs):
                at = slice(p * LANES, (p + 1) * LANES)
                tmp[0, 0:payload, :] = top(at)
                tmp[1, 0:payload, :] = low(at)
                to = p * level.x_rows
                end = to + margin + level.rows
                flat[to : to + margin, :] = tmp[0, x_margin - margin : x_margin, :]
                flat[to + margin : to + margin + level.own_rows, :] = act_ref[0 : level.own_rows, at].astype(F32)
                flat[end : end + margin, :] = tmp[1, 0:margin, :]
            ship_ref[0:own_flat, :] = flat[0:own_flat, :].astype(BF16)
            for t in range(2 * TAPS):
                at = own_flat + t * half
                value = taps_ref[t].astype(F32)
                ship_ref[at : at + half, :] = jnp.concatenate([value[:half], value[half:]], axis=1).astype(BF16)
            rest = both_ref[0:2, :]
            for term in range(3):
                part = rounded(rest)
                bias_tmp[2 * term : 2 * term + 2, :] = part
                rest = rest - part
            bias_tmp[6:16, :] = jnp.zeros((10, LANES), F32)
            ship_ref[own_flat + packed_rows : ship_rows, :] = bias_tmp[...].astype(BF16)

    (ship,) = call(
        ship_body,
        [sds((ship_rows, LANES), BF16)],
        [tmp_buffer, pltpu.VMEM((own_flat + 32, LANES), F32), pltpu.VMEM((16, LANES), F32)],
        [act, from_swap, from_cross, taps, bias_own, rim],
    )
    shipped = across(ship, [(2, 3)])

    grad_rows = up_to(packed_rows // 2 + 1, 16)

    def gradients(level, source, hidden, err_in, err_out, rows_at, pair_out):
        scale = np.float32(1.0 / math.sqrt(strips * level.rows * level.cols))
        first = kernel_terms(source, err_in, level.odd_pairs, rows_at[2], rows_at[0], level)
        pack_kernel_terms(pair_out.at[0], *first, scale)
        then = kernel_terms(hidden, err_out, level.pairs, rows_at[3], rows_at[1], level)
        pack_kernel_terms(pair_out.at[1], *then, scale)

    def finish(level, source, hidden, ei, eo, pair_out):
        at = (level.error - 1, level.error, level.error + 1, level.error)
        gradients(level, source, hidden, ei, eo.at[1 : 1 + level.pairs], at, pair_out)

    def store_in(level, d_out):
        def store(first, size, a, rows, value):
            d_out[first : first + size, a : a + rows, :] = value

        return store

    def beside_body(
        act_ref, swap_ref, cross_ref, fwd_ref, bias_ref, x0, h0, o0, i0,
        din_ref, dout_ref, hid_ref, x_ref, pair_ref, tmp,
    ):
        section = lax.axis_index("section")
        top, low = halo_readers(swap_ref, cross_ref)

        @pl.when(section == 0)
        def _():
            finish(fine, x0, h0, i0, o0, pair_ref)

        for level in levels[1:]:

            @pl.when(section == level.level)
            def _(level=level):
                own_input(level, x_ref, act_ref)
                halo_input(level, x_ref, top, low, tmp, x_margin)
                zero_tail(hid_ref, level, level.hidden_rows)
                forward(
                    level, x_ref, hid_ref, [fwd_ref.at[0], fwd_ref.at[1]], bias_ref, din_ref,
                    store_in(level, dout_ref), place(), chunk,
                )

    pair_shape = sds((2, grad_rows, LANES), F32)
    din_own, dout_own, hid_own, x_own, pair_first = call(
        beside_body,
        [field(second, 1), field(second, 0), field(second, 1), field(second, 2), pair_shape],
        [tmp_buffer],
        [act, from_swap, from_cross, fwd_own, bias_own, state[0], state[1], state[4], state[5]],
    )

    def step(level, gb, grad_row, d_in, d_out, back, eo, ei, bi, gu):
        mask = image_mask(level, -level.error, level.out_rows, *place())
        zero_edges(eo, level)
        zero_tail(ei, level, level.alloc)
        for p in range(level.pairs):
            part = gb[p, grad_row : grad_row + level.out_rows, :] * d_out[p, 0 : level.out_rows, :]
            eo[p + 1, 0 : level.out_rows, :] = jnp.where(mask[0], rounded(part), 0.0)
        backward(level, eo, ei, [back.at[0], back.at[1]], d_in, gb, grad_row, bi, gu, place(), chunk)

    third_rows = third.rows + 2 * third.error
    third_flat = up_to(third.pairs * third_rows, 16)

    def hand_down(upper, lower, gu, rc, gb):
        def emit(m, span, value):
            gb[m, 0 : 3 * upper.k_count, :] = rounded(value)

        coarsen(
            upper, lower, gu, rc, [(upper.k_first, upper.k_count)], [(3 * upper.k_first, 3 * upper.k_count)],
            emit, place(),
        )

    def second_body(
        in_ref, rim_ref, din_o, dout_o, back_o, third_ref, eo, ei, bi, gb, gu, rc, mid, rims, flat
    ):
        @pl.when(lax.axis_index("section") == 1)
        def _():
            mid[...] = in_ref[...].astype(F32)
            rims[...] = rim_ref[...].astype(F32)
            low = g_end + g_in[1]
            for p in range(second.pairs):
                at = p * 2 * g_end
                gb[p, 0:g_end, :] = rims[at : at + g_end, :]
                gb[p, g_end:low, :] = mid[p * g_in[1] : (p + 1) * g_in[1], :]
                gb[p, low : low + g_end, :] = rims[at + g_end : at + 2 * g_end, :]
            step(second, gb, 0, din_o, dout_o, back_o, eo, ei, bi, gu)
            hand_down(second, third, gu, rc, gb)
            at = second.up_shift
            for p in range(third.pairs):
                flat[p * third_rows : (p + 1) * third_rows, :] = gb[p, at : at + third_rows, :]
            third_ref[...] = flat[0:third_flat, :].astype(BF16)

    coarse_tmp = pltpu.VMEM((second.pairs, 3 * second.k_count + 8, LANES), F32)
    third_grad, eo_own, ei_own, bi_own = call(
        second_body,
        [sds((third_flat, LANES), BF16), field(second, 2), field(second, 1), field(second, 0)],
        [
            buffer(second, 0),
            buffer(fine, 0),
            coarse_tmp,
            pltpu.VMEM((in_rows, LANES), F32),
            pltpu.VMEM((rim_rows, LANES), F32),
            pltpu.VMEM((third_flat + 16, LANES), F32),
        ],
        [in_near, rim_near, din_own, dout_own, back_own],
        flops=4 * 10**9,
    )
    third_to_last = across(third_grad, [(1, 3)])
    third_to_own = across(third_grad, [(1, 2)])

    def shipped_body(ship_ref, own_ref, din_s, dout_s, back_s, fwd_s, xb, hb, own):
        @pl.when(lax.axis_index("section") == 3)
        def _():
            level = third
            values = []
            for t in range(2 * TAPS):
                pack = ship_ref[own_flat + t * half : own_flat + (t + 1) * half, :].astype(F32)
                values.append(jnp.concatenate([pack[:, :channels], pack[:, channels:]], axis=0))
            expand(values, fwd_s, back_s)
            terms = ship_ref[own_flat + packed_rows : ship_rows, :].astype(F32)
            bias = terms[0:2] + terms[2:4] + terms[4:6]
            own[0:own_flat, :] = ship_ref[0:own_flat, :].astype(F32)
            shipped_input(level, xb, own)
            zero_tail(hb, level, level.hidden_rows)
            forward(level, xb, hb, [fwd_s.at[0], fwd_s.at[1]], bias, din_s, store_in(level, dout_s), place(), chunk)

    din_s, dout_s, back_s = call(
        shipped_body,
        [field(third, 1), field(third, 0), matrix_shape],
        [
            pltpu.VMEM((2, 6 * LANES, LANES), BF16),
            buffer(third, 2),
            buffer(third, 1),
            pltpu.VMEM((own_flat + 16, LANES), F32),
        ],
        [shipped, third_to_own],
    )

    def last_body(
        pair0, own_ref, last_ref, din_o, dout_o, hid_o, x_o, back_o, din_s, dout_s, back_s, eo_o, ei_o,
        keep_ref, send_ref, bi, pair_out, gb, eo, ei, gu, rc, flat,
    ):
        section = lax.axis_index("section")
        odd = is_odd()

        def take(source):
            flat[...] = source[...].astype(F32)
            for p in range(third.pairs):
                gb[p, 0:third_rows, :] = flat[p * third_rows : (p + 1) * third_rows, :]

        @pl.when(section == 0)
        def _():
            pair_out[...] = pair0[...]

        @pl.when(section == 1)
        def _():
            finish(second, x_o, hid_o, ei_o, eo_o, pair_out)

        @pl.when(section == 2)
        def _():
            take(own_ref)
            step(third, gb, 0, din_o, dout_o, back_o, eo, ei, bi, None)
            finish(third, x_o, hid_o, ei, eo, pair_out)

        @pl.when(section == 3)
        def _():
            take(last_ref)
            step(third, gb, 0, din_s, dout_s, back_s, eo, ei, None, gu)
            hand_down(third, last, gu, rc, gb)
            step(last, gb, third.up_shift, din_o, dout_o, back_o, eo, ei, bi, None)
            finish(last, x_o, hid_o, ei, eo, pair_out)

        first, then = pair_out[0], pair_out[1]
        keep_ref[...] = jnp.where(odd, then, first)
        send_ref[...] = jnp.where(odd, first, then)

    half_shape = sds((grad_rows, LANES), F32)
    keep, send, bi_last = call(
        last_body,
        [half_shape, half_shape, field(third, 0)],
        [
            pltpu.VMEM((2, grad_rows, LANES), F32),
            buffer(third, 0),
            buffer(third, 2),
            buffer(third, 1),
            buffer(fine, 0),
            coarse_tmp,
            pltpu.VMEM((third_flat, LANES), F32),
        ],
        [
            pair_first, third_to_own, third_to_last, din_own, dout_own, hid_own, x_own, back_own,
            din_s, dout_s, back_s, eo_own, ei_own,
        ],
    )

    total = keep + lax.ppermute(send, "strip", swap_pairs)
    hop_size = 2
    while hop_size < strips:
        mine = lax.reduce_precision(total, 8, 7)
        other = lax.ppermute(mine.astype(BF16), "strip", [(i, i ^ hop_size) for i in range(strips)])
        total = mine + other.astype(F32)
        hop_size *= 2
    other = lax.ppermute(total, "strip", swap_pairs)

    def noise_body(noise0, bi_o, bi_l, noise_ref):
        section = lax.axis_index("section")

        @pl.when(section == 0)
        def _():
            noise_ref[...] = noise0[...]

        for level, source in ((second, bi_o), (third, bi_l), (last, bi_l)):

            @pl.when(section == level.level)
            def _(level=level, source=source):
                write_noise(level, source, noise_ref)

    (noise,) = call(noise_body, [strip_shape], [], [noise_first, bi_own, bi_last], final=(0,))

    def final_body(mine_ref, other_ref, kernel_ref, bias_ref):
        odd = is_odd()
        for c in range(2):
            if c == 0:
                value = jnp.where(odd, other_ref[...], mine_ref[...])
            else:
                value = jnp.where(odd, mine_ref[...], other_ref[...])
            swapped = half_swap(value)
            for dy in range(3):
                kernel_ref[c, dy * 192 : dy * 192 + 96, :] = value[dy * 96 : dy * 96 + 96, :channels]
                kernel_ref[c, dy * 192 + 96 : dy * 192 + 192, :] = swapped[dy * 96 : dy * 96 + 96, :channels]
            bias_ref[c : c + 1, :] = value[288:289, :channels]

    kernel_sum, bias_sum = call(
        final_body,
        [sds((2, TAPS * channels, channels), F32), sds((2, channels), F32)],
        [],
        [total, other],
        final=(0, 1),
    )
    return (
        noise[None, None],
        kernel_sum.reshape(1, 2, 3, 3, channels, channels),
        bias_sum[None],
    )


def solution(mesh):
    strips = mesh.shape["strip"]
    sections = mesh.shape["section"]
    return jax.shard_map(
        functools.partial(local, strips, sections),
        mesh=mesh,
        in_specs=(
            P(None, "strip", None),
            P("section", None, "strip", None),
            P("section", None, None, None, None, None),
            P("section", None, None),
        ),
        out_specs=(
            P("section", None, "strip", None),
            P("section", None, None, None, None, None),
            P("section", None, None),
        ),
        check_vma=False,
    )
```

```python
import functools
import math

import jax
import jax.numpy as jnp
import numpy as np
from jax import lax
from jax.experimental import pallas as pl
from jax.experimental.pallas import tpu as pltpu
from jax.sharding import PartitionSpec as P

LEAK = 0.05
LANES = 128
F32 = jnp.float32
BF16 = jnp.bfloat16
TAPS = 9
VMEM_BYTES = 24 * 1024 * 1024


def up_to(value, step):
    return -(-value // step) * step


class Level:
    def __init__(self, level, rows, cols):
        self.level = level
        self.rows = rows * 3**level // 4**level
        self.cols = cols * 3**level // 4**level
        self.pairs = -(-self.cols // 2)
        self.odd_pairs = -(-(self.cols + 1) // 2)

    def margin(self, error):
        self.error = error
        self.x_margin = error + 2
        self.x_rows = self.rows + 2 * (error + 2)
        self.hidden_rows = up_to(self.rows + 2 * (error + 1) + 2, 8) - 2
        self.out_rows = up_to(self.rows + 2 * error + 2, 8) - 2
        self.in_rows = up_to(self.rows + 2 * (error - 1) + 2, 8) - 2
        self.back_rows = up_to(self.rows + 2 * (error - 2) + 2, 8) - 2
        self.own_rows = up_to(self.rows, 16)
        self.alloc = up_to(max(self.hidden_rows + 2, self.x_margin + self.own_rows + 2), 8)


def levels_of(rows, cols, count):
    levels = [Level(s, rows, cols) for s in range(count)]
    levels[-1].margin(2)
    for s in range(count - 2, -1, -1):
        fine, coarse = levels[s], levels[s + 1]
        first = -coarse.error
        last = coarse.rows + coarse.error - 1
        low = 4 * (first // 3) + (-1, 1, 2)[first % 3]
        high = 4 * (last // 3) + (1, 2, 4)[last % 3]
        fine.margin(max(-low, high - fine.rows + 1) + 2)
        fine.k_first = first // 3
        fine.k_count = up_to(last // 3 - fine.k_first + 1, 8)
        fine.up_shift = -3 * fine.k_first - coarse.error
        start = fine.error - 2 + 4 * fine.k_first - 1
        fine.gu_row = max(0, -start)
        fine.gu_start = start + fine.gu_row
        assert fine.rows % 4 == 0
    return levels


def column_weights(fine, coarse):
    matrix = np.zeros((coarse, fine), np.float32)
    for x in range(fine):
        num = max((2 * x + 1) * coarse - fine, 0)
        low = num // (2 * fine)
        frac = np.float32(num - 2 * fine * low) / np.float32(2 * fine)
        matrix[low, x] += np.float32(1.0) - frac
        matrix[min(low + 1, coarse - 1), x] += frac
    return matrix


def lane_index(shape):
    return lax.broadcasted_iota(jnp.int32, shape, len(shape) - 1)


def half_swap(value):
    return pltpu.roll(value, LANES // 2, value.ndim - 1)


def twice(bias):
    return jnp.concatenate([bias, bias], axis=1)


def rounded(value):
    return value.astype(BF16).astype(F32)


def image_mask(level, base, count, strip, strips):
    row = lax.broadcasted_iota(jnp.int32, (1, count, LANES), 1) + base
    low = jnp.where(strip == 0, 0, -(10**6))
    high = jnp.where(strip == strips - 1, level.rows, 10**6)
    return (row >= low) & (row < high)


def odd_column_mask(level, first, count, mask):
    if first > 0 and 2 * (first + count - 1) < level.cols:
        return mask
    shape = (count, mask.shape[1], LANES)
    half = lax.broadcasted_iota(jnp.int32, shape, 2) // (LANES // 2)
    col = 2 * (first + lax.broadcasted_iota(jnp.int32, shape, 0)) - 1 + half
    return mask & (col >= 0) & (col < level.cols)


def conv(source, kernel, count, segments, chunk, emit):
    total = sum(rows for _, rows in segments)
    for first in range(0, count, chunk):
        size = min(chunk, count - first)
        blocks = [source[first : first + size + 1, a : a + rows, :] for a, rows in segments]
        block = blocks[0] if len(blocks) == 1 else jnp.concatenate(blocks, axis=1)
        left = block[:size].reshape(size * total, LANES).astype(BF16)
        right = block[1:].reshape(size * total, LANES).astype(BF16)
        by_row = jnp.dot(jnp.concatenate([left, right], axis=1), kernel[...], preferred_element_type=F32)
        result = by_row[:, :LANES]
        for dy in (1, 2):
            part = by_row[:, dy * LANES : (dy + 1) * LANES]
            result = result + pltpu.roll(part, size * total - dy, 0)
        result = result.reshape(size, total, LANES)
        at = 0
        for a, rows in segments:
            emit(first, size, a, rows - 2, result[:, at : at + rows - 2])
            at += rows


def kernel_terms(source, error, count, source_row, error_row, level):
    rows = level.own_rows
    err = error[0:count, error_row : error_row + rows, :]
    if rows != level.rows:
        row = lax.broadcasted_iota(jnp.int32, (1, rows, LANES), 1)
        err = jnp.where(row < level.rows, err, 0.0)
    total = jnp.sum(err, axis=(0, 1)).reshape(1, LANES)
    parts = []
    for dy in range(3):
        block = source[0 : count + 1, source_row + dy : source_row + dy + rows, :].astype(BF16)
        parts.append(block[:count].reshape(count * rows, LANES))
        parts.append(block[1:].reshape(count * rows, LANES))
    stacked = jnp.concatenate(parts, axis=1)
    product = lax.dot_general(
        err.astype(BF16).reshape(count * rows, LANES),
        stacked,
        (((0,), (0,)), ((), ())),
        preferred_element_type=F32,
    )
    return product, total


def pack_kernel_terms(out_ref, product, total, scale):
    half = LANES // 2
    by_tap = product.T * scale
    lane = lane_index((1, LANES))
    for dy in range(3):
        block = by_tap[dy * 2 * LANES : (dy + 1) * 2 * LANES]
        folded = block[: 3 * half] + half_swap(block)[half:]
        out_ref[dy * 96 : dy * 96 + 96, :] = jnp.where(lane < half, folded[:96], half_swap(folded[96:]))
    bias = (total + half_swap(total)) * scale
    out_ref[288:304, :] = jnp.broadcast_to(bias, (16, LANES))


def toeplitz(taps):
    half = LANES // 2
    zero = jnp.zeros((half, half), F32)
    columns = []
    for dy in range(3):
        rows = []
        for k in range(4):
            left = taps[dy * 3 + k] if k < 3 else zero
            right = taps[dy * 3 + k - 1] if k > 0 else zero
            rows.append(jnp.concatenate([left, right], axis=1))
        columns.append(jnp.concatenate(rows, axis=0))
    return jnp.concatenate(columns, axis=1)


def toeplitz_back(taps):
    half = LANES // 2
    zero = jnp.zeros((half, half), F32)
    by_row = []
    for dy in range(3):
        columns = []
        for k in range(4):
            top = taps[(2 - dy) * 3 + 2 - k] if k < 3 else zero
            bottom = taps[(2 - dy) * 3 + 3 - k] if k > 0 else zero
            columns.append(jnp.concatenate([top, bottom], axis=0))
        by_row.append(jnp.concatenate([jnp.concatenate(columns[i : i + 2], axis=1).T for i in (0, 2)], axis=0))
    return jnp.concatenate(by_row, axis=1)


def zero_tail(ref, level, rows):
    if level.alloc > rows:
        ref[0 : level.pairs + 1, rows : level.alloc, :] = jnp.zeros((level.pairs + 1, level.alloc - rows, LANES), F32)
    if level.odd_pairs < level.pairs + 1:
        ref[level.odd_pairs : level.pairs + 1, 0 : level.alloc, :] = jnp.zeros(
            (level.pairs + 1 - level.odd_pairs, level.alloc, LANES), F32
        )


def zero_edges(ref, level):
    zero = jnp.zeros((level.alloc, LANES), F32)
    ref[0, 0 : level.alloc, :] = zero
    ref[level.pairs + 1, 0 : level.alloc, :] = zero


def slope(value):
    return LEAK + (1.0 - LEAK) * (0.5 + 0.5 * jnp.tanh(0.5 * value))


def forward(level, xb, hb, kernels, bias, d_in, d_out, place, chunk, hidden_parts=None, out_parts=None):
    strip, strips = place
    bias_in, bias_out = bias[0:1], bias[1:2]

    def first_layer(first, size, a, rows, value):
        mask = image_mask(level, a - (level.error + 1), rows, strip, strips)
        pre = value + bias_in
        small = jnp.exp(-jnp.abs(pre))
        soft = jnp.maximum(pre, 0.0) + jnp.log(1.0 + small)
        act = LEAK * pre + (1.0 - LEAK) * soft
        keep = odd_column_mask(level, first, size, mask)
        hb[first : first + size, a : a + rows, :] = jnp.where(keep, rounded(act), 0.0)
        d_in[first : first + size, a : a + rows, :] = slope(pre)

    conv(xb, kernels[0], level.odd_pairs, hidden_parts or [(0, level.hidden_rows + 2)], chunk, first_layer)

    def second_layer(first, size, a, rows, value):
        d_out(first, size, a, rows, slope(value + bias_out))

    conv(hb, kernels[1], level.pairs, out_parts or [(0, level.out_rows + 2)], chunk, second_layer)


def backward(level, eo, ei, kernels, d_in, grad, grad_row, bi, gu, place, chunk, in_parts=None, back_parts=None):
    strip, strips = place

    def inner(first, size, a, rows, value):
        mask = image_mask(level, a - (level.error - 1), rows, strip, strips)
        keep = odd_column_mask(level, first, size, mask)
        part = d_in[first : first + size, 2 + a : 2 + a + rows, :]
        ei[first : first + size, a : a + rows, :] = jnp.where(keep, rounded(value * part), 0.0)

    conv(eo, kernels[1], level.odd_pairs, in_parts or [(0, level.in_rows + 2)], chunk, inner)

    def outer(first, size, a, rows, value):
        if bi is not None:
            bi[first : first + size, a : a + rows, :] = value
        if gu is not None:
            mask = image_mask(level, a - (level.error - 2), rows, strip, strips)
            part = grad[first : first + size, grad_row + 2 + a : grad_row + 2 + a + rows, :]
            at = level.gu_row + a
            gu[first : first + size, at : at + rows, :] = jnp.where(mask, rounded(part + value), 0.0)

    conv(ei, kernels[0], level.pairs, back_parts or [(0, level.back_rows + 2)], chunk, outer)


def write_noise(level, bi, noise):
    total_rows = noise.shape[0]
    row = lax.broadcasted_iota(jnp.int32, (level.own_rows, LANES), 0)
    lane = lane_index((level.own_rows, LANES))
    for p in range(noise.shape[1] // LANES):
        at = slice(p * LANES, (p + 1) * LANES)
        if p < level.pairs:
            part = bi[p, level.error - 2 : level.error - 2 + level.own_rows, :]
            if level.own_rows != level.rows:
                part = jnp.where(row < level.rows, part, 0.0)
            if 2 * p + 1 >= level.cols:
                part = jnp.where(lane < LANES // 2, part, 0.0)
            noise[0 : level.own_rows, at] = part.astype(BF16)
            if level.own_rows < total_rows:
                noise[level.own_rows : total_rows, at] = jnp.zeros((total_rows - level.own_rows, LANES), BF16)
        else:
            noise[:, at] = jnp.zeros((total_rows, LANES), BF16)


def coarsen(fine, coarse, gu, rc, ranges, spans, emit, place, edges=True):
    strip, strips = place
    for k, count in ranges:
        start = fine.gu_start + 4 * (k - fine.k_first)
        at = 3 * (k - fine.k_first)
        for p in range(fine.pairs):
            f = [gu[p, pl.ds(start + a, count, stride=4), :] for a in range(6)]
            rc[p, pl.ds(at, count, stride=3), :] = 0.125 * f[0] + 0.875 * f[1] + 0.375 * f[2]
            rc[p, pl.ds(at + 1, count, stride=3), :] = 0.625 * f[2] + 0.625 * f[3]
            rc[p, pl.ds(at + 2, count, stride=3), :] = 0.375 * f[3] + 0.875 * f[4] + 0.125 * f[5]
    if edges:
        top = -3 * fine.k_first
        low = top + coarse.rows - 1
        on_top = jnp.where(strip == 0, 1.0, 0.0).astype(F32)
        on_low = jnp.where(strip == strips - 1, 1.0, 0.0).astype(F32)
        every = slice(0, fine.pairs)
        rc[every, top : top + 1, :] = rc[every, top : top + 1, :] + on_top * rc[every, top - 1 : top, :]
        rc[every, low : low + 1, :] = rc[every, low : low + 1, :] + on_low * rc[every, low + 1 : low + 2, :]
    matrix = column_weights(fine.cols, coarse.cols)
    matrix = np.pad(matrix, ((0, 2 * coarse.pairs - coarse.cols), (0, 2 * fine.pairs - fine.cols)))
    lane = lane_index((1, LANES))

    def weights(low_lanes, high_lanes):
        return jnp.where(lane < LANES // 2, np.float32(low_lanes), np.float32(high_lanes))

    for span, (row, rows) in enumerate(spans):
        at = row - 3 * fine.k_first
        for m in range(coarse.pairs):
            total = None
            for q in range(fine.pairs):
                same = (matrix[2 * m, 2 * q], matrix[2 * m + 1, 2 * q + 1])
                cross = (matrix[2 * m, 2 * q + 1], matrix[2 * m + 1, 2 * q])
                value = rc[q, at : at + rows, :] if any(same) or any(cross) else None
                for pair, moved in ((same, False), (cross, True)):
                    if any(pair):
                        term = (half_swap(value) if moved else value) * weights(*pair)
                        total = term if total is None else total + term
            emit(m, span, total)


def own_input(level, xb, act):
    zero_edges(xb, level)
    lane = lane_index((1, LANES))
    for p in range(level.pairs):
        own = act[0 : level.own_rows, p * LANES : (p + 1) * LANES].astype(F32)
        if 2 * p + 1 >= level.cols:
            own = jnp.where(lane < LANES // 2, own, 0.0)
        xb[p + 1, level.x_margin : level.x_margin + level.own_rows, :] = own


def zero_after(level, xb):
    end = level.x_rows
    if end < level.alloc:
        xb[1 : level.pairs + 1, end : level.alloc, :] = jnp.zeros((level.pairs, level.alloc - end, LANES), F32)


def halo_input(level, xb, top, low, tmp, payload_rows):
    margin = level.x_margin
    end = margin + level.rows
    lane = lane_index((1, LANES))
    for p in range(level.pairs):
        at = slice(p * LANES, (p + 1) * LANES)
        upper, lower = top(at), low(at)
        if 2 * p + 1 >= level.cols:
            upper, lower = (jnp.where(lane < LANES // 2, v, 0.0) for v in (upper, lower))
        tmp[0, 0 : upper.shape[0], :] = upper
        tmp[1, 0 : lower.shape[0], :] = lower
        xb[p + 1, 0:margin, :] = tmp[0, payload_rows - margin : payload_rows, :]
        xb[p + 1, end : end + margin, :] = tmp[1, 0:margin, :]
    zero_after(level, xb)


def shipped_input(level, xb, own):
    zero_edges(xb, level)
    for p in range(level.pairs):
        xb[p + 1, 0 : level.x_rows, :] = own[p * level.x_rows : (p + 1) * level.x_rows, :]
    zero_after(level, xb)


def call(body, out_shape, scratch, operands, final=(), outside=(), aliases=None, flops=1000):
    operands = [
        pltpu.with_memory_space_constraint(x, pltpu.HBM if i in outside else pltpu.VMEM)
        for i, x in enumerate(operands)
    ]
    out_shape = [s if i in final else pltpu.VMEM(s.shape, s.dtype) for i, s in enumerate(out_shape)]
    return pl.pallas_call(
        body,
        out_shape=out_shape,
        in_specs=[pl.BlockSpec(memory_space=pltpu.VMEM)] * len(operands),
        out_specs=[pl.BlockSpec(memory_space=pltpu.VMEM)] * len(out_shape),
        scratch_shapes=scratch,
        input_output_aliases=aliases or {},
        compiler_params=pltpu.CompilerParams(vmem_limit_bytes=VMEM_BYTES),
        cost_estimate=pl.CostEstimate(flops=flops, bytes_accessed=1000, transcendentals=0),
    )(*operands)


def sds(shape, dtype):
    return jax.ShapeDtypeStruct(shape, dtype)


def field(level, extra):
    return sds((level.pairs + extra, level.alloc, LANES), F32)


def buffer(level, extra):
    return pltpu.VMEM((level.pairs + extra, level.alloc, LANES), F32)


def local(strips, sections, cotangent, activations, weights, biases):
    row_count, flat_width = activations.shape[2:]
    channels = weights.shape[-1]
    half = channels // 2
    cols = flat_width // channels
    assert 2 * channels == LANES and sections == 4 and cotangent.shape[0] == 1
    levels = levels_of(row_count, cols, sections)
    fine, second, third, last = levels
    x_margin, g_margin = fine.x_margin, fine.error
    payload = up_to(x_margin + g_margin, 16)
    pair_count = fine.pairs
    chunk = 4

    def place():
        return lax.axis_index("strip"), strips

    def is_odd():
        return lax.rem(lax.axis_index("strip"), 2) == 1

    packed_rows = TAPS * channels
    own_flat = up_to(third.pairs * third.x_rows, 16)
    ship_rows = own_flat + packed_rows + 16

    def halo_body(
        act_hbm, cot_hbm, bias_hbm, act_ref, cot_ref, both_ref, swap_ref, cross_ref, xs, cs, ts
    ):
        both_ref[0:2, :] = twice(bias_hbm[...])
        section = lax.axis_index("section")
        odd = is_odd()

        live = jnp.int32(fine.rows)
        for level in levels[1:]:
            live = jnp.where(section == level.level, level.rows, live)
        for p in range(pair_count):
            at = slice(p * LANES, (p + 1) * LANES)
            act_ref[:, at] = act_hbm[:, at]
            cot_ref[:, at] = cot_hbm[:, at]
            xs[p, :, :] = act_hbm[:, at].astype(F32)
            cs[p, :, :] = cot_hbm[:, at].astype(F32)
            ts[0, p, 0:x_margin, :] = xs[p, 0:x_margin, :]
            ts[0, p, x_margin : x_margin + g_margin, :] = cs[p, 0:g_margin, :]
            ts[1, p, 0:x_margin, :] = xs[p, pl.ds(live - x_margin, x_margin), :]
            ts[1, p, x_margin : x_margin + g_margin, :] = cs[p, row_count - g_margin : row_count, :]
            upper = ts[0, p, 0:payload, :]
            lower = ts[1, p, 0:payload, :]
            swap_ref[:, at] = jnp.where(odd, upper, lower).astype(BF16)
            cross_ref[:, at] = jnp.where(odd, lower, upper).astype(BF16)

    strip_shape = sds((row_count, flat_width), BF16)
    halo_shape = sds((payload, flat_width), BF16)
    taps = weights.reshape(2 * TAPS, channels, channels)
    act, cot, bias_own, to_swap, to_cross = call(
        halo_body,
        [
            strip_shape, strip_shape, sds((8, LANES), F32), halo_shape, halo_shape,
        ],
        [
            pltpu.VMEM((pair_count, row_count, LANES), F32),
            pltpu.VMEM((pair_count, row_count, LANES), F32),
            pltpu.VMEM((2, pair_count, payload, LANES), F32),
        ],
        [activations[0, 0], cotangent[0], biases[0]],
        outside=(0, 1, 2),
    )
    swap_pairs = [(i, i ^ 1) for i in range(strips)]
    cross_pairs = [(i, i + 1) for i in range(1, strips - 1, 2)] + [(i + 1, i) for i in range(1, strips - 1, 2)]
    from_cross = lax.ppermute(to_cross, "strip", cross_pairs)
    from_swap = lax.ppermute(to_swap, "strip", swap_pairs)


    def expand(tap_list, forward_ref, back_ref):
        for c in range(2):
            chosen = tap_list[c * TAPS : (c + 1) * TAPS]
            forward_ref[c, :, :] = toeplitz(chosen).astype(BF16)
            back_ref[c, :, :] = toeplitz_back(chosen).astype(BF16)

    def matrix_body(taps_ref, bias_ref, forward_ref, back_ref):
        expand([taps_ref[t].astype(F32) for t in range(2 * TAPS)], forward_ref, back_ref)

    matrix_shape = sds((2, 2 * LANES, 3 * LANES), BF16)
    fwd_own, back_own = call(matrix_body, [matrix_shape, matrix_shape], [], [taps, bias_own])

    def across(value, pairs):
        return lax.ppermute(value, "section", pairs)

    inside = [[(17, row_count)], [(16, row_count)]]
    ends = [[(0, 24), (row_count + 10, 24)], [(0, 24), (row_count + 8, 24)]]
    assert fine.error == 15 and fine.x_margin == 17 and row_count >= 32
    g_in = (4, second.rows - 8)
    g_end = second.error + g_in[0]
    in_rows = up_to(second.pairs * g_in[1], 16)
    rim_rows = up_to(second.pairs * 2 * g_end, 16)

    def error_of(level, gb, eo, mask_place):
        def error(first, size, a, rows, value):
            mask = image_mask(level, a - level.error, rows, *mask_place)
            part = gb[first : first + size, a : a + rows, :]
            eo[first + 1 : first + 1 + size, a : a + rows, :] = jnp.where(mask, rounded(part * value), 0.0)

        return error

    def inside_body(
        act_ref, cot_ref, fwd_ref, back_ref, bias_ref, hop_ref, xb, hb, db, gb, eo, ei, bi, gu, rc, flat,
    ):
        section = lax.axis_index("section")

        @pl.when(section == 0)
        def _():
            level = fine
            own_input(level, xb, act_ref)
            zero_after(level, xb)
            zero_edges(eo, level)
            zero_tail(hb, level, level.hidden_rows)
            zero_tail(ei, level, level.alloc)
            for p in range(level.pairs):
                gb[p, g_margin : g_margin + row_count, :] = cot_ref[:, p * LANES : (p + 1) * LANES].astype(F32)
            forward(
                level, xb, hb, [fwd_ref.at[0], fwd_ref.at[1]], bias_ref, db, error_of(level, gb, eo, place()),
                place(), chunk, *inside,
            )
            backward(
                level, eo, ei, [back_ref.at[0], back_ref.at[1]], db, gb, 0, bi, gu, place(), chunk,
                inside[1], inside[1],
            )

            def emit(m, span, rows):
                flat[m * g_in[1] : (m + 1) * g_in[1], :] = rows

            coarsen(fine, second, gu, rc, [(0, 16)], [g_in], emit, place(), edges=False)
            hop_ref[...] = flat[0:in_rows, :].astype(BF16)

    coarse_buffer = pltpu.VMEM((fine.pairs, 3 * fine.k_count + 8, LANES), F32)
    state_shapes = [
        field(fine, 2), field(fine, 1), field(fine, 1), field(fine, 0),
        field(fine, 2), field(fine, 1), field(fine, 0), field(fine, 0),
    ]
    hop_in, *state = call(
        inside_body,
        [sds((in_rows, LANES), BF16), *state_shapes],
        [coarse_buffer, pltpu.VMEM((in_rows + 16, LANES), F32)],
        [act, cot, fwd_own, back_own, bias_own],
    )
    in_near = across(hop_in, [(0, 1), (1, 3), (3, 2), (2, 0)])

    def halo_readers(swap_ref, cross_ref):
        odd = is_odd()

        def top(at):
            return jnp.where(odd, swap_ref[:, at].astype(F32), cross_ref[:, at].astype(F32))

        def low(at):
            return jnp.where(odd, cross_ref[:, at].astype(F32), swap_ref[:, at].astype(F32))

        return top, low

    def rim_body(
        swap_ref, cross_ref, fwd_ref, back_ref, bias_ref, xi, hi, di, gi, oi, ii, bii, ui,
        rim_ref, xb, hb, db, gb, eo, ei, bi, gu, rc, flat, tmp,
    ):
        section = lax.axis_index("section")
        top, low = halo_readers(swap_ref, cross_ref)

        @pl.when(section == 0)
        def _():
            level = fine
            end = x_margin + row_count
            for p in range(level.pairs):
                at = slice(p * LANES, (p + 1) * LANES)
                tmp[0, 0:payload, :] = top(at)
                tmp[1, 0:payload, :] = low(at)
                xb[p + 1, 0:x_margin, :] = tmp[0, 0:x_margin, :]
                xb[p + 1, end : end + x_margin, :] = tmp[1, 0:x_margin, :]
                gb[p, 0:g_margin, :] = tmp[0, x_margin : x_margin + g_margin, :]
                gb[p, g_margin + row_count : 2 * g_margin + row_count, :] = tmp[
                    1, x_margin : x_margin + g_margin, :
                ]
            forward(
                level, xb, hb, [fwd_ref.at[0], fwd_ref.at[1]], bias_ref, db, error_of(level, gb, eo, place()),
                place(), chunk, ends[0], ends[0],
            )
            backward(
                level, eo, ei, [back_ref.at[0], back_ref.at[1]], db, gb, 0, bi, gu, place(), chunk, ends[1], ends[1]
            )

            def emit(m, span, rows):
                at = m * 2 * g_end + span * g_end
                flat[at : at + g_end, :] = rows[0:g_end]

            last_k = (second.rows + second.error) // 3
            coarsen(
                fine, second, gu, rc,
                [(fine.k_first, 8), (last_k - 7, 8)],
                [(-second.error, up_to(g_end, 8)), (g_in[0] + g_in[1], up_to(g_end, 8))],
                emit, place(),
            )
            rim_ref[...] = flat[0:rim_rows, :].astype(BF16)

    tmp_buffer = pltpu.VMEM((2, payload, LANES), F32)
    rim, *state = call(
        rim_body,
        [sds((rim_rows, LANES), BF16), *state_shapes],
        [coarse_buffer, pltpu.VMEM((rim_rows + 32, LANES), F32), tmp_buffer],
        [from_swap, from_cross, fwd_own, back_own, bias_own, *state],
        aliases={5 + i: 1 + i for i in range(len(state_shapes))},
        flops=2 * 10**9,
    )
    rim_near = across(rim, [(0, 1), (1, 3), (3, 2), (2, 0)])

    def ship_body(act_ref, swap_ref, cross_ref, taps_ref, both_ref, rim_ref, ship_ref, tmp, flat, bias_tmp):
        top, low = halo_readers(swap_ref, cross_ref)

        @pl.when(lax.axis_index("section") == 2)
        def _():
            level = third
            margin = level.x_margin
            for p in range(level.pairs):
                at = slice(p * LANES, (p + 1) * LANES)
                tmp[0, 0:payload, :] = top(at)
                tmp[1, 0:payload, :] = low(at)
                to = p * level.x_rows
                end = to + margin + level.rows
                flat[to : to + margin, :] = tmp[0, x_margin - margin : x_margin, :]
                flat[to + margin : to + margin + level.own_rows, :] = act_ref[0 : level.own_rows, at].astype(F32)
                flat[end : end + margin, :] = tmp[1, 0:margin, :]
            ship_ref[0:own_flat, :] = flat[0:own_flat, :].astype(BF16)
            for t in range(2 * TAPS):
                at = own_flat + t * half
                value = taps_ref[t].astype(F32)
                ship_ref[at : at + half, :] = jnp.concatenate([value[:half], value[half:]], axis=1).astype(BF16)
            rest = both_ref[0:2, :]
            for term in range(3):
                part = rounded(rest)
                bias_tmp[2 * term : 2 * term + 2, :] = part
                rest = rest - part
            bias_tmp[6:16, :] = jnp.zeros((10, LANES), F32)
            ship_ref[own_flat + packed_rows : ship_rows, :] = bias_tmp[...].astype(BF16)

    (ship,) = call(
        ship_body,
        [sds((ship_rows, LANES), BF16)],
        [tmp_buffer, pltpu.VMEM((own_flat + 32, LANES), F32), pltpu.VMEM((16, LANES), F32)],
        [act, from_swap, from_cross, taps, bias_own, rim],
    )
    shipped = across(ship, [(2, 3)])

    grad_rows = up_to(packed_rows // 2 + 1, 16)

    def gradients(level, source, hidden, err_in, err_out, rows_at, pair_out):
        scale = np.float32(1.0 / math.sqrt(strips * level.rows * level.cols))
        first = kernel_terms(source, err_in, level.odd_pairs, rows_at[2], rows_at[0], level)
        pack_kernel_terms(pair_out.at[0], *first, scale)
        then = kernel_terms(hidden, err_out, level.pairs, rows_at[3], rows_at[1], level)
        pack_kernel_terms(pair_out.at[1], *then, scale)

    def finish(level, source, hidden, ei, eo, pair_out):
        at = (level.error - 1, level.error, level.error + 1, level.error)
        gradients(level, source, hidden, ei, eo.at[1 : 1 + level.pairs], at, pair_out)

    def store_in(level, d_out):
        def store(first, size, a, rows, value):
            d_out[first : first + size, a : a + rows, :] = value

        return store

    def beside_body(
        act_ref, swap_ref, cross_ref, fwd_ref, bias_ref, x0, h0, o0, i0,
        din_ref, dout_ref, hid_ref, x_ref, pair_ref, tmp,
    ):
        section = lax.axis_index("section")
        top, low = halo_readers(swap_ref, cross_ref)

        @pl.when(section == 0)
        def _():
            finish(fine, x0, h0, i0, o0, pair_ref)

        for level in levels[1:]:

            @pl.when(section == level.level)
            def _(level=level):
                own_input(level, x_ref, act_ref)
                halo_input(level, x_ref, top, low, tmp, x_margin)
                zero_tail(hid_ref, level, level.hidden_rows)
                forward(
                    level, x_ref, hid_ref, [fwd_ref.at[0], fwd_ref.at[1]], bias_ref, din_ref,
                    store_in(level, dout_ref), place(), chunk,
                )

    pair_shape = sds((2, grad_rows, LANES), F32)
    din_own, dout_own, hid_own, x_own, pair_first = call(
        beside_body,
        [field(second, 1), field(second, 0), field(second, 1), field(second, 2), pair_shape],
        [tmp_buffer],
        [act, from_swap, from_cross, fwd_own, bias_own, state[0], state[1], state[4], state[5]],
    )

    def step(level, gb, grad_row, d_in, d_out, back, eo, ei, bi, gu):
        mask = image_mask(level, -level.error, level.out_rows, *place())
        zero_edges(eo, level)
        zero_tail(ei, level, level.alloc)
        for p in range(level.pairs):
            part = gb[p, grad_row : grad_row + level.out_rows, :] * d_out[p, 0 : level.out_rows, :]
            eo[p + 1, 0 : level.out_rows, :] = jnp.where(mask[0], rounded(part), 0.0)
        backward(level, eo, ei, [back.at[0], back.at[1]], d_in, gb, grad_row, bi, gu, place(), chunk)

    third_rows = third.rows + 2 * third.error
    third_flat = up_to(third.pairs * third_rows, 16)

    def hand_down(upper, lower, gu, rc, gb):
        def emit(m, span, value):
            gb[m, 0 : 3 * upper.k_count, :] = rounded(value)

        coarsen(
            upper, lower, gu, rc, [(upper.k_first, upper.k_count)], [(3 * upper.k_first, 3 * upper.k_count)],
            emit, place(),
        )

    def second_body(
        in_ref, rim_ref, din_o, dout_o, back_o, third_ref, eo, ei, bi, gb, gu, rc, mid, rims, flat
    ):
        @pl.when(lax.axis_index("section") == 1)
        def _():
            mid[...] = in_ref[...].astype(F32)
            rims[...] = rim_ref[...].astype(F32)
            low = g_end + g_in[1]
            for p in range(second.pairs):
                at = p * 2 * g_end
                gb[p, 0:g_end, :] = rims[at : at + g_end, :]
                gb[p, g_end:low, :] = mid[p * g_in[1] : (p + 1) * g_in[1], :]
                gb[p, low : low + g_end, :] = rims[at + g_end : at + 2 * g_end, :]
            step(second, gb, 0, din_o, dout_o, back_o, eo, ei, bi, gu)
            hand_down(second, third, gu, rc, gb)
            at = second.up_shift
            for p in range(third.pairs):
                flat[p * third_rows : (p + 1) * third_rows, :] = gb[p, at : at + third_rows, :]
            third_ref[...] = flat[0:third_flat, :].astype(BF16)

    coarse_tmp = pltpu.VMEM((second.pairs, 3 * second.k_count + 8, LANES), F32)
    third_grad, eo_own, ei_own, bi_own = call(
        second_body,
        [sds((third_flat, LANES), BF16), field(second, 2), field(second, 1), field(second, 0)],
        [
            buffer(second, 0),
            buffer(fine, 0),
            coarse_tmp,
            pltpu.VMEM((in_rows, LANES), F32),
            pltpu.VMEM((rim_rows, LANES), F32),
            pltpu.VMEM((third_flat + 16, LANES), F32),
        ],
        [in_near, rim_near, din_own, dout_own, back_own],
        flops=4 * 10**9,
    )
    third_to_last = across(third_grad, [(1, 3), (3, 2), (2, 0), (0, 1)])
    third_to_own = across(third_grad, [(1, 2)])

    def shipped_body(ship_ref, own_ref, din_s, dout_s, back_s, fwd_s, xb, hb, own):
        @pl.when(lax.axis_index("section") == 3)
        def _():
            level = third
            values = []
            for t in range(2 * TAPS):
                pack = ship_ref[own_flat + t * half : own_flat + (t + 1) * half, :].astype(F32)
                values.append(jnp.concatenate([pack[:, :channels], pack[:, channels:]], axis=0))
            expand(values, fwd_s, back_s)
            terms = ship_ref[own_flat + packed_rows : ship_rows, :].astype(F32)
            bias = terms[0:2] + terms[2:4] + terms[4:6]
            own[0:own_flat, :] = ship_ref[0:own_flat, :].astype(F32)
            shipped_input(level, xb, own)
            zero_tail(hb, level, level.hidden_rows)
            forward(level, xb, hb, [fwd_s.at[0], fwd_s.at[1]], bias, din_s, store_in(level, dout_s), place(), chunk)

    din_s, dout_s, back_s = call(
        shipped_body,
        [field(third, 1), field(third, 0), matrix_shape],
        [
            pltpu.VMEM((2, 2 * LANES, 3 * LANES), BF16),
            buffer(third, 2),
            buffer(third, 1),
            pltpu.VMEM((own_flat + 16, LANES), F32),
        ],
        [shipped, third_to_own],
    )

    def last_body(
        pair0, own_ref, last_ref, din_o, dout_o, hid_o, x_o, back_o, din_s, dout_s, back_s, eo_o, ei_o,
        keep_ref, send_ref, bi, pair_out, gb, eo, ei, gu, rc, flat,
    ):
        section = lax.axis_index("section")
        odd = is_odd()

        def take(source):
            flat[...] = source[...].astype(F32)
            for p in range(third.pairs):
                gb[p, 0:third_rows, :] = flat[p * third_rows : (p + 1) * third_rows, :]

        @pl.when(section == 0)
        def _():
            pair_out[...] = pair0[...]

        @pl.when(section == 1)
        def _():
            finish(second, x_o, hid_o, ei_o, eo_o, pair_out)

        @pl.when(section == 2)
        def _():
            take(own_ref)
            step(third, gb, 0, din_o, dout_o, back_o, eo, ei, bi, None)
            finish(third, x_o, hid_o, ei, eo, pair_out)

        @pl.when(section == 3)
        def _():
            take(last_ref)
            step(third, gb, 0, din_s, dout_s, back_s, eo, ei, None, gu)
            hand_down(third, last, gu, rc, gb)
            step(last, gb, third.up_shift, din_o, dout_o, back_o, eo, ei, bi, None)
            finish(last, x_o, hid_o, ei, eo, pair_out)

        first, then = pair_out[0], pair_out[1]
        keep_ref[...] = jnp.where(odd, then, first)
        send_ref[...] = jnp.where(odd, first, then)

    half_shape = sds((grad_rows, LANES), F32)
    keep, send, bi_last = call(
        last_body,
        [half_shape, half_shape, field(third, 0)],
        [
            pltpu.VMEM((2, grad_rows, LANES), F32),
            buffer(third, 0),
            buffer(third, 2),
            buffer(third, 1),
            buffer(fine, 0),
            coarse_tmp,
            pltpu.VMEM((third_flat, LANES), F32),
        ],
        [
            pair_first, third_to_own, third_to_last, din_own, dout_own, hid_own, x_own, back_own,
            din_s, dout_s, back_s, eo_own, ei_own,
        ],
    )

    total = keep + lax.ppermute(send, "strip", swap_pairs)
    step = 2
    while step < strips:
        mine = lax.reduce_precision(total, 8, 7)
        small = mine.astype(BF16)
        offsets = (step, 2 * step, 3 * step) if 2 * step < strips else (step,)
        got = [lax.ppermute(small, "strip", [(i, i ^ o) for i in range(strips)]).astype(F32) for o in offsets]
        total = mine + got[0]
        if len(got) == 3:
            total = total + (got[1] + got[2])
        step *= len(got) + 1
    other = lax.ppermute(total, "strip", swap_pairs)

    def noise_body(bi_f, bi_o, bi_l, noise_ref):
        section = lax.axis_index("section")

        for level, source in ((fine, bi_f), (second, bi_o), (third, bi_l), (last, bi_l)):

            @pl.when(section == level.level)
            def _(level=level, source=source):
                write_noise(level, source, noise_ref)

    (noise,) = call(noise_body, [strip_shape], [], [state[6], bi_own, bi_last], final=(0,))

    def final_body(mine_ref, other_ref, kernel_ref, bias_ref):
        odd = is_odd()
        for c in range(2):
            if c == 0:
                value = jnp.where(odd, other_ref[...], mine_ref[...])
            else:
                value = jnp.where(odd, mine_ref[...], other_ref[...])
            swapped = half_swap(value)
            for dy in range(3):
                kernel_ref[c, dy * 192 : dy * 192 + 96, :] = value[dy * 96 : dy * 96 + 96, :channels]
                kernel_ref[c, dy * 192 + 96 : dy * 192 + 192, :] = swapped[dy * 96 : dy * 96 + 96, :channels]
            bias_ref[c : c + 1, :] = value[288:289, :channels]

    kernel_sum, bias_sum = call(
        final_body,
        [sds((2, TAPS * channels, channels), F32), sds((2, channels), F32)],
        [],
        [total, other],
        final=(0, 1),
    )
    return (
        noise[None, None],
        kernel_sum.reshape(1, 2, 3, 3, channels, channels),
        bias_sum[None],
    )


def solution(mesh):
    strips = mesh.shape["strip"]
    sections = mesh.shape["section"]
    return jax.shard_map(
        functools.partial(local, strips, sections),
        mesh=mesh,
        in_specs=(
            P(None, "strip", None),
            P("section", None, "strip", None),
            P("section", None, None, None, None, None),
            P("section", None, None),
        ),
        out_specs=(
            P("section", None, "strip", None),
            P("section", None, None, None, None, None),
            P("section", None, None),
        ),
        check_vma=False,
    )
```

```python
import functools
import math

import jax
import jax.numpy as jnp
import numpy as np
from jax import lax
from jax.experimental import pallas as pl
from jax.experimental.pallas import tpu as pltpu
from jax.sharding import PartitionSpec as P

LEAK = 0.05
LANES = 128
F32 = jnp.float32
BF16 = jnp.bfloat16
TAPS = 9
VMEM_BYTES = 24 * 1024 * 1024


def up_to(value, step):
    return -(-value // step) * step


class Level:
    def __init__(self, level, rows, cols):
        self.level = level
        self.rows = rows * 3**level // 4**level
        self.cols = cols * 3**level // 4**level
        self.pairs = -(-self.cols // 2)
        self.odd_pairs = -(-(self.cols + 1) // 2)

    def margin(self, error):
        self.error = error
        self.x_margin = error + 2
        self.x_rows = self.rows + 2 * (error + 2)
        self.hidden_rows = up_to(self.rows + 2 * (error + 1) + 2, 8) - 2
        self.out_rows = up_to(self.rows + 2 * error + 2, 8) - 2
        self.in_rows = up_to(self.rows + 2 * (error - 1) + 2, 8) - 2
        self.back_rows = up_to(self.rows + 2 * (error - 2) + 2, 8) - 2
        self.own_rows = up_to(self.rows, 16)
        self.alloc = up_to(max(self.hidden_rows + 2, self.x_margin + self.own_rows + 2), 8)


def levels_of(rows, cols, count):
    levels = [Level(s, rows, cols) for s in range(count)]
    levels[-1].margin(2)
    for s in range(count - 2, -1, -1):
        fine, coarse = levels[s], levels[s + 1]
        first = -coarse.error
        last = coarse.rows + coarse.error - 1
        low = 4 * (first // 3) + (-1, 1, 2)[first % 3]
        high = 4 * (last // 3) + (1, 2, 4)[last % 3]
        fine.margin(max(-low, high - fine.rows + 1) + 2)
        fine.k_first = first // 3
        fine.k_count = up_to(last // 3 - fine.k_first + 1, 8)
        fine.up_shift = -3 * fine.k_first - coarse.error
        start = fine.error - 2 + 4 * fine.k_first - 1
        fine.gu_row = max(0, -start)
        fine.gu_start = start + fine.gu_row
        assert fine.rows % 4 == 0
    return levels


def column_weights(fine, coarse):
    matrix = np.zeros((coarse, fine), np.float32)
    for x in range(fine):
        num = max((2 * x + 1) * coarse - fine, 0)
        low = num // (2 * fine)
        frac = np.float32(num - 2 * fine * low) / np.float32(2 * fine)
        matrix[low, x] += np.float32(1.0) - frac
        matrix[min(low + 1, coarse - 1), x] += frac
    return matrix


def lane_index(shape):
    return lax.broadcasted_iota(jnp.int32, shape, len(shape) - 1)


def half_swap(value):
    return pltpu.roll(value, LANES // 2, value.ndim - 1)


def twice(bias):
    return jnp.concatenate([bias, bias], axis=1)


def rounded(value):
    return value.astype(BF16).astype(F32)


def image_mask(level, base, count, strip, strips):
    row = lax.broadcasted_iota(jnp.int32, (1, count, LANES), 1) + base
    low = jnp.where(strip == 0, 0, -(10**6))
    high = jnp.where(strip == strips - 1, level.rows, 10**6)
    return (row >= low) & (row < high)


def odd_column_mask(level, first, count, mask):
    if first > 0 and 2 * (first + count - 1) < level.cols:
        return mask
    shape = (count, mask.shape[1], LANES)
    half = lax.broadcasted_iota(jnp.int32, shape, 2) // (LANES // 2)
    col = 2 * (first + lax.broadcasted_iota(jnp.int32, shape, 0)) - 1 + half
    return mask & (col >= 0) & (col < level.cols)


def conv(source, kernel, count, segments, chunk, emit):
    total = sum(rows for _, rows in segments)
    for first in range(0, count, chunk):
        size = min(chunk, count - first)
        blocks = [source[first : first + size + 1, a : a + rows, :] for a, rows in segments]
        block = blocks[0] if len(blocks) == 1 else jnp.concatenate(blocks, axis=1)
        left = block[:size].reshape(size * total, LANES).astype(BF16)
        right = block[1:].reshape(size * total, LANES).astype(BF16)
        by_row = jnp.dot(jnp.concatenate([left, right], axis=1), kernel[...], preferred_element_type=F32)
        result = by_row[:, :LANES]
        for dy in (1, 2):
            part = by_row[:, dy * LANES : (dy + 1) * LANES]
            result = result + pltpu.roll(part, size * total - dy, 0)
        result = result.reshape(size, total, LANES)
        at = 0
        for a, rows in segments:
            emit(first, size, a, rows - 2, result[:, at : at + rows - 2])
            at += rows


def kernel_terms(source, error, count, source_row, error_row, level):
    rows = level.own_rows
    err = error[0:count, error_row : error_row + rows, :]
    if rows != level.rows:
        row = lax.broadcasted_iota(jnp.int32, (1, rows, LANES), 1)
        err = jnp.where(row < level.rows, err, 0.0)
    total = jnp.sum(err, axis=(0, 1)).reshape(1, LANES)
    parts = []
    for dy in range(3):
        block = source[0 : count + 1, source_row + dy : source_row + dy + rows, :].astype(BF16)
        parts.append(block[:count].reshape(count * rows, LANES))
        parts.append(block[1:].reshape(count * rows, LANES))
    stacked = jnp.concatenate(parts, axis=1)
    product = lax.dot_general(
        err.astype(BF16).reshape(count * rows, LANES),
        stacked,
        (((0,), (0,)), ((), ())),
        preferred_element_type=F32,
    )
    return product, total


def pack_kernel_terms(out_ref, product, total, scale):
    half = LANES // 2
    low = lane_index((1, LANES)) < half
    thirds = []
    for dy in range(3):
        first = product[:, 2 * dy * LANES : (2 * dy + 1) * LANES]
        then = product[:, (2 * dy + 1) * LANES : (2 * dy + 2) * LANES]
        moved = half_swap(then[half:])
        out_ref[dy * half : (dy + 1) * half, :] = (
            first[:half] + jnp.where(low, half_swap(first[half:]), moved)
        ) * scale
        thirds.append((then[:half] + moved) * scale)
    bias = (total + half_swap(total)) * scale
    out_ref[3 * half : 4 * half, :] = jnp.where(low, thirds[0], half_swap(thirds[1]))
    out_ref[4 * half : 5 * half, :] = jnp.where(low, thirds[2], bias)


def toeplitz(taps):
    half = LANES // 2
    zero = jnp.zeros((half, half), F32)
    columns = []
    for dy in range(3):
        rows = []
        for k in range(4):
            left = taps[dy * 3 + k] if k < 3 else zero
            right = taps[dy * 3 + k - 1] if k > 0 else zero
            rows.append(jnp.concatenate([left, right], axis=1))
        columns.append(jnp.concatenate(rows, axis=0))
    return jnp.concatenate(columns, axis=1)


def toeplitz_back(taps):
    half = LANES // 2
    zero = jnp.zeros((half, half), F32)
    by_row = []
    for dy in range(3):
        columns = []
        for k in range(4):
            top = taps[(2 - dy) * 3 + 2 - k] if k < 3 else zero
            bottom = taps[(2 - dy) * 3 + 3 - k] if k > 0 else zero
            columns.append(jnp.concatenate([top, bottom], axis=0))
        by_row.append(jnp.concatenate([jnp.concatenate(columns[i : i + 2], axis=1).T for i in (0, 2)], axis=0))
    return jnp.concatenate(by_row, axis=1)


def zero_tail(ref, level, rows):
    if level.alloc > rows:
        ref[0 : level.pairs + 1, rows : level.alloc, :] = jnp.zeros((level.pairs + 1, level.alloc - rows, LANES), F32)
    if level.odd_pairs < level.pairs + 1:
        ref[level.odd_pairs : level.pairs + 1, 0 : level.alloc, :] = jnp.zeros(
            (level.pairs + 1 - level.odd_pairs, level.alloc, LANES), F32
        )


def zero_edges(ref, level):
    zero = jnp.zeros((level.alloc, LANES), F32)
    ref[0, 0 : level.alloc, :] = zero
    ref[level.pairs + 1, 0 : level.alloc, :] = zero


def slope(value):
    return LEAK + (1.0 - LEAK) * (0.5 + 0.5 * jnp.tanh(0.5 * value))


def forward(level, xb, hb, kernels, bias, d_in, d_out, place, chunk, hidden_parts=None, out_parts=None):
    strip, strips = place
    bias_in, bias_out = bias[0:1], bias[1:2]

    def first_layer(first, size, a, rows, value):
        mask = image_mask(level, a - (level.error + 1), rows, strip, strips)
        pre = value + bias_in
        small = jnp.exp(-jnp.abs(pre))
        soft = jnp.maximum(pre, 0.0) + jnp.log(1.0 + small)
        act = LEAK * pre + (1.0 - LEAK) * soft
        keep = odd_column_mask(level, first, size, mask)
        hb[first : first + size, a : a + rows, :] = jnp.where(keep, rounded(act), 0.0)
        d_in[first : first + size, a : a + rows, :] = slope(pre)

    conv(xb, kernels[0], level.odd_pairs, hidden_parts or [(0, level.hidden_rows + 2)], chunk, first_layer)

    def second_layer(first, size, a, rows, value):
        d_out(first, size, a, rows, slope(value + bias_out))

    conv(hb, kernels[1], level.pairs, out_parts or [(0, level.out_rows + 2)], chunk, second_layer)


def backward(level, eo, ei, kernels, d_in, grad, grad_row, bi, gu, place, chunk, in_parts=None, back_parts=None):
    strip, strips = place

    def inner(first, size, a, rows, value):
        mask = image_mask(level, a - (level.error - 1), rows, strip, strips)
        keep = odd_column_mask(level, first, size, mask)
        part = d_in[first : first + size, 2 + a : 2 + a + rows, :]
        ei[first : first + size, a : a + rows, :] = jnp.where(keep, rounded(value * part), 0.0)

    conv(eo, kernels[1], level.odd_pairs, in_parts or [(0, level.in_rows + 2)], chunk, inner)

    def outer(first, size, a, rows, value):
        if bi is not None:
            bi[first : first + size, a : a + rows, :] = value
        if gu is not None:
            mask = image_mask(level, a - (level.error - 2), rows, strip, strips)
            part = grad[first : first + size, grad_row + 2 + a : grad_row + 2 + a + rows, :]
            at = level.gu_row + a
            gu[first : first + size, at : at + rows, :] = jnp.where(mask, rounded(part + value), 0.0)

    conv(ei, kernels[0], level.pairs, back_parts or [(0, level.back_rows + 2)], chunk, outer)


def write_noise(level, bi, noise):
    total_rows = noise.shape[0]
    row = lax.broadcasted_iota(jnp.int32, (level.own_rows, LANES), 0)
    lane = lane_index((level.own_rows, LANES))
    for p in range(noise.shape[1] // LANES):
        at = slice(p * LANES, (p + 1) * LANES)
        if p < level.pairs:
            part = bi[p, level.error - 2 : level.error - 2 + level.own_rows, :]
            if level.own_rows != level.rows:
                part = jnp.where(row < level.rows, part, 0.0)
            if 2 * p + 1 >= level.cols:
                part = jnp.where(lane < LANES // 2, part, 0.0)
            noise[0 : level.own_rows, at] = part.astype(BF16)
            if level.own_rows < total_rows:
                noise[level.own_rows : total_rows, at] = jnp.zeros((total_rows - level.own_rows, LANES), BF16)
        else:
            noise[:, at] = jnp.zeros((total_rows, LANES), BF16)


def coarsen(fine, coarse, gu, rc, ranges, spans, emit, place, edges=True):
    strip, strips = place
    for k, count in ranges:
        start = fine.gu_start + 4 * (k - fine.k_first)
        at = 3 * (k - fine.k_first)
        for p in range(fine.pairs):
            f = [gu[p, pl.ds(start + a, count, stride=4), :] for a in range(6)]
            rc[p, pl.ds(at, count, stride=3), :] = 0.125 * f[0] + 0.875 * f[1] + 0.375 * f[2]
            rc[p, pl.ds(at + 1, count, stride=3), :] = 0.625 * f[2] + 0.625 * f[3]
            rc[p, pl.ds(at + 2, count, stride=3), :] = 0.375 * f[3] + 0.875 * f[4] + 0.125 * f[5]
    if edges:
        top = -3 * fine.k_first
        low = top + coarse.rows - 1
        on_top = jnp.where(strip == 0, 1.0, 0.0).astype(F32)
        on_low = jnp.where(strip == strips - 1, 1.0, 0.0).astype(F32)
        every = slice(0, fine.pairs)
        rc[every, top : top + 1, :] = rc[every, top : top + 1, :] + on_top * rc[every, top - 1 : top, :]
        rc[every, low : low + 1, :] = rc[every, low : low + 1, :] + on_low * rc[every, low + 1 : low + 2, :]
    matrix = column_weights(fine.cols, coarse.cols)
    matrix = np.pad(matrix, ((0, 2 * coarse.pairs - coarse.cols), (0, 2 * fine.pairs - fine.cols)))
    lane = lane_index((1, LANES))

    def weights(low_lanes, high_lanes):
        return jnp.where(lane < LANES // 2, np.float32(low_lanes), np.float32(high_lanes))

    for span, (row, rows) in enumerate(spans):
        at = row - 3 * fine.k_first
        for m in range(coarse.pairs):
            total = None
            for q in range(fine.pairs):
                same = (matrix[2 * m, 2 * q], matrix[2 * m + 1, 2 * q + 1])
                cross = (matrix[2 * m, 2 * q + 1], matrix[2 * m + 1, 2 * q])
                value = rc[q, at : at + rows, :] if any(same) or any(cross) else None
                for pair, moved in ((same, False), (cross, True)):
                    if any(pair):
                        term = (half_swap(value) if moved else value) * weights(*pair)
                        total = term if total is None else total + term
            emit(m, span, total)


def own_input(level, xb, act):
    zero_edges(xb, level)
    lane = lane_index((1, LANES))
    for p in range(level.pairs):
        own = act[0 : level.own_rows, p * LANES : (p + 1) * LANES].astype(F32)
        if 2 * p + 1 >= level.cols:
            own = jnp.where(lane < LANES // 2, own, 0.0)
        xb[p + 1, level.x_margin : level.x_margin + level.own_rows, :] = own


def zero_after(level, xb):
    end = level.x_rows
    if end < level.alloc:
        xb[1 : level.pairs + 1, end : level.alloc, :] = jnp.zeros((level.pairs, level.alloc - end, LANES), F32)


def halo_input(level, xb, top, low, tmp, payload_rows):
    margin = level.x_margin
    end = margin + level.rows
    lane = lane_index((1, LANES))
    for p in range(level.pairs):
        at = slice(p * LANES, (p + 1) * LANES)
        upper, lower = top(at), low(at)
        if 2 * p + 1 >= level.cols:
            upper, lower = (jnp.where(lane < LANES // 2, v, 0.0) for v in (upper, lower))
        tmp[0, 0 : upper.shape[0], :] = upper
        tmp[1, 0 : lower.shape[0], :] = lower
        xb[p + 1, 0:margin, :] = tmp[0, payload_rows - margin : payload_rows, :]
        xb[p + 1, end : end + margin, :] = tmp[1, 0:margin, :]
    zero_after(level, xb)


def shipped_input(level, xb, own):
    zero_edges(xb, level)
    for p in range(level.pairs):
        xb[p + 1, 0 : level.x_rows, :] = own[p * level.x_rows : (p + 1) * level.x_rows, :]
    zero_after(level, xb)


def call(body, out_shape, scratch, operands, final=(), outside=(), aliases=None, flops=1000):
    operands = [
        pltpu.with_memory_space_constraint(x, pltpu.HBM if i in outside else pltpu.VMEM)
        for i, x in enumerate(operands)
    ]
    out_shape = [s if i in final else pltpu.VMEM(s.shape, s.dtype) for i, s in enumerate(out_shape)]
    return pl.pallas_call(
        body,
        out_shape=out_shape,
        in_specs=[pl.BlockSpec(memory_space=pltpu.VMEM)] * len(operands),
        out_specs=[pl.BlockSpec(memory_space=pltpu.VMEM)] * len(out_shape),
        scratch_shapes=scratch,
        input_output_aliases=aliases or {},
        compiler_params=pltpu.CompilerParams(vmem_limit_bytes=VMEM_BYTES),
        cost_estimate=pl.CostEstimate(flops=flops, bytes_accessed=1000, transcendentals=0),
    )(*operands)


def sds(shape, dtype):
    return jax.ShapeDtypeStruct(shape, dtype)


def field(level, extra):
    return sds((level.pairs + extra, level.alloc, LANES), F32)


def buffer(level, extra):
    return pltpu.VMEM((level.pairs + extra, level.alloc, LANES), F32)


def local(strips, sections, cotangent, activations, weights, biases):
    row_count, flat_width = activations.shape[2:]
    channels = weights.shape[-1]
    half = channels // 2
    cols = flat_width // channels
    assert 2 * channels == LANES and sections == 4 and cotangent.shape[0] == 1
    levels = levels_of(row_count, cols, sections)
    fine, second, third, last = levels
    x_margin, g_margin = fine.x_margin, fine.error
    payload = up_to(x_margin + g_margin, 16)
    pair_count = fine.pairs
    chunk = 4

    def place():
        return lax.axis_index("strip"), strips

    def is_odd():
        return lax.rem(lax.axis_index("strip"), 2) == 1

    packed_rows = TAPS * channels
    own_flat = up_to(third.pairs * third.x_rows, 16)
    ship_rows = own_flat + packed_rows + 16

    def halo_body(
        act_hbm, cot_hbm, bias_hbm, act_ref, cot_ref, both_ref, swap_ref, cross_ref, xs, cs, ts
    ):
        both_ref[0:2, :] = twice(bias_hbm[...])
        section = lax.axis_index("section")
        odd = is_odd()

        live = jnp.int32(fine.rows)
        for level in levels[1:]:
            live = jnp.where(section == level.level, level.rows, live)
        for p in range(pair_count):
            at = slice(p * LANES, (p + 1) * LANES)
            act_ref[:, at] = act_hbm[:, at]
            cot_ref[:, at] = cot_hbm[:, at]
            xs[p, :, :] = act_hbm[:, at].astype(F32)
            cs[p, :, :] = cot_hbm[:, at].astype(F32)
            ts[0, p, 0:x_margin, :] = xs[p, 0:x_margin, :]
            ts[0, p, x_margin : x_margin + g_margin, :] = cs[p, 0:g_margin, :]
            ts[1, p, 0:x_margin, :] = xs[p, pl.ds(live - x_margin, x_margin), :]
            ts[1, p, x_margin : x_margin + g_margin, :] = cs[p, row_count - g_margin : row_count, :]
            upper = ts[0, p, 0:payload, :]
            lower = ts[1, p, 0:payload, :]
            swap_ref[:, at] = jnp.where(odd, upper, lower).astype(BF16)
            cross_ref[:, at] = jnp.where(odd, lower, upper).astype(BF16)

    strip_shape = sds((row_count, flat_width), BF16)
    halo_shape = sds((payload, flat_width), BF16)
    taps = weights.reshape(2 * TAPS, channels, channels)
    act, cot, bias_own, to_swap, to_cross = call(
        halo_body,
        [
            strip_shape, strip_shape, sds((8, LANES), F32), halo_shape, halo_shape,
        ],
        [
            pltpu.VMEM((pair_count, row_count, LANES), F32),
            pltpu.VMEM((pair_count, row_count, LANES), F32),
            pltpu.VMEM((2, pair_count, payload, LANES), F32),
        ],
        [activations[0, 0], cotangent[0], biases[0]],
        outside=(0, 1, 2),
    )
    swap_pairs = [(i, i ^ 1) for i in range(strips)]
    cross_pairs = [(i, i + 1) for i in range(1, strips - 1, 2)] + [(i + 1, i) for i in range(1, strips - 1, 2)]
    from_cross = lax.ppermute(to_cross, "strip", cross_pairs)
    from_swap = lax.ppermute(to_swap, "strip", swap_pairs)


    def expand(tap_list, forward_ref, back_ref):
        for c in range(2):
            chosen = tap_list[c * TAPS : (c + 1) * TAPS]
            forward_ref[c, :, :] = toeplitz(chosen).astype(BF16)
            back_ref[c, :, :] = toeplitz_back(chosen).astype(BF16)

    def matrix_body(taps_ref, bias_ref, forward_ref, back_ref):
        expand([taps_ref[t].astype(F32) for t in range(2 * TAPS)], forward_ref, back_ref)

    matrix_shape = sds((2, 2 * LANES, 3 * LANES), BF16)
    fwd_own, back_own = call(matrix_body, [matrix_shape, matrix_shape], [], [taps, bias_own])

    def across(value, pairs):
        return lax.ppermute(value, "section", pairs)

    inside = [[(17, row_count)], [(16, row_count)]]
    ends = [[(0, 24), (row_count + 10, 24)], [(0, 24), (row_count + 8, 24)]]
    assert fine.error == 15 and fine.x_margin == 17 and row_count >= 32
    g_in = (4, second.rows - 8)
    g_end = second.error + g_in[0]
    in_rows = up_to(second.pairs * g_in[1], 16)
    rim_rows = up_to(second.pairs * 2 * g_end, 16)

    def error_of(level, gb, eo, mask_place):
        def error(first, size, a, rows, value):
            mask = image_mask(level, a - level.error, rows, *mask_place)
            part = gb[first : first + size, a : a + rows, :]
            eo[first + 1 : first + 1 + size, a : a + rows, :] = jnp.where(mask, rounded(part * value), 0.0)

        return error

    def inside_body(
        act_ref, cot_ref, fwd_ref, back_ref, bias_ref, hop_ref, xb, hb, db, gb, eo, ei, bi, gu, rc, flat,
    ):
        section = lax.axis_index("section")

        @pl.when(section == 0)
        def _():
            level = fine
            own_input(level, xb, act_ref)
            zero_after(level, xb)
            zero_edges(eo, level)
            zero_tail(hb, level, level.hidden_rows)
            zero_tail(ei, level, level.alloc)
            for p in range(level.pairs):
                gb[p, g_margin : g_margin + row_count, :] = cot_ref[:, p * LANES : (p + 1) * LANES].astype(F32)
            forward(
                level, xb, hb, [fwd_ref.at[0], fwd_ref.at[1]], bias_ref, db, error_of(level, gb, eo, place()),
                place(), chunk, *inside,
            )
            backward(
                level, eo, ei, [back_ref.at[0], back_ref.at[1]], db, gb, 0, bi, gu, place(), chunk,
                inside[1], inside[1],
            )

            def emit(m, span, rows):
                flat[m * g_in[1] : (m + 1) * g_in[1], :] = rows

            coarsen(fine, second, gu, rc, [(0, 16)], [g_in], emit, place(), edges=False)
            hop_ref[...] = flat[0:in_rows, :].astype(BF16)

    coarse_buffer = pltpu.VMEM((fine.pairs, 3 * fine.k_count + 8, LANES), F32)
    state_shapes = [
        field(fine, 2), field(fine, 1), field(fine, 1), field(fine, 0),
        field(fine, 2), field(fine, 1), field(fine, 0), field(fine, 0),
    ]
    hop_in, *state = call(
        inside_body,
        [sds((in_rows, LANES), BF16), *state_shapes],
        [coarse_buffer, pltpu.VMEM((in_rows + 16, LANES), F32)],
        [act, cot, fwd_own, back_own, bias_own],
    )
    in_near = across(hop_in, [(0, 1), (1, 3), (3, 2), (2, 0)])

    def halo_readers(swap_ref, cross_ref):
        odd = is_odd()

        def top(at):
            return jnp.where(odd, swap_ref[:, at].astype(F32), cross_ref[:, at].astype(F32))

        def low(at):
            return jnp.where(odd, cross_ref[:, at].astype(F32), swap_ref[:, at].astype(F32))

        return top, low

    def rim_body(
        swap_ref, cross_ref, fwd_ref, back_ref, bias_ref, xi, hi, di, gi, oi, ii, bii, ui,
        rim_ref, xb, hb, db, gb, eo, ei, bi, gu, rc, flat, tmp,
    ):
        section = lax.axis_index("section")
        top, low = halo_readers(swap_ref, cross_ref)

        @pl.when(section == 0)
        def _():
            level = fine
            end = x_margin + row_count
            for p in range(level.pairs):
                at = slice(p * LANES, (p + 1) * LANES)
                tmp[0, 0:payload, :] = top(at)
                tmp[1, 0:payload, :] = low(at)
                xb[p + 1, 0:x_margin, :] = tmp[0, 0:x_margin, :]
                xb[p + 1, end : end + x_margin, :] = tmp[1, 0:x_margin, :]
                gb[p, 0:g_margin, :] = tmp[0, x_margin : x_margin + g_margin, :]
                gb[p, g_margin + row_count : 2 * g_margin + row_count, :] = tmp[
                    1, x_margin : x_margin + g_margin, :
                ]
            forward(
                level, xb, hb, [fwd_ref.at[0], fwd_ref.at[1]], bias_ref, db, error_of(level, gb, eo, place()),
                place(), chunk, ends[0], ends[0],
            )
            backward(
                level, eo, ei, [back_ref.at[0], back_ref.at[1]], db, gb, 0, bi, gu, place(), chunk, ends[1], ends[1]
            )

            def emit(m, span, rows):
                at = m * 2 * g_end + span * g_end
                flat[at : at + g_end, :] = rows[0:g_end]

            last_k = (second.rows + second.error) // 3
            coarsen(
                fine, second, gu, rc,
                [(fine.k_first, 8), (last_k - 7, 8)],
                [(-second.error, up_to(g_end, 8)), (g_in[0] + g_in[1], up_to(g_end, 8))],
                emit, place(),
            )
            rim_ref[...] = flat[0:rim_rows, :].astype(BF16)

    tmp_buffer = pltpu.VMEM((2, payload, LANES), F32)
    rim, *state = call(
        rim_body,
        [sds((rim_rows, LANES), BF16), *state_shapes],
        [coarse_buffer, pltpu.VMEM((rim_rows + 32, LANES), F32), tmp_buffer],
        [from_swap, from_cross, fwd_own, back_own, bias_own, *state],
        aliases={5 + i: 1 + i for i in range(len(state_shapes))},
        flops=2 * 10**9,
    )
    rim_near = across(rim, [(0, 1), (1, 3), (3, 2), (2, 0)])

    def ship_body(act_ref, swap_ref, cross_ref, taps_ref, both_ref, rim_ref, ship_ref, tmp, flat, bias_tmp):
        top, low = halo_readers(swap_ref, cross_ref)

        @pl.when(lax.axis_index("section") == 2)
        def _():
            level = third
            margin = level.x_margin
            for p in range(level.pairs):
                at = slice(p * LANES, (p + 1) * LANES)
                tmp[0, 0:payload, :] = top(at)
                tmp[1, 0:payload, :] = low(at)
                to = p * level.x_rows
                end = to + margin + level.rows
                flat[to : to + margin, :] = tmp[0, x_margin - margin : x_margin, :]
                flat[to + margin : to + margin + level.own_rows, :] = act_ref[0 : level.own_rows, at].astype(F32)
                flat[end : end + margin, :] = tmp[1, 0:margin, :]
            ship_ref[0:own_flat, :] = flat[0:own_flat, :].astype(BF16)
            for t in range(2 * TAPS):
                at = own_flat + t * half
                value = taps_ref[t].astype(F32)
                ship_ref[at : at + half, :] = jnp.concatenate([value[:half], value[half:]], axis=1).astype(BF16)
            rest = both_ref[0:2, :]
            for term in range(3):
                part = rounded(rest)
                bias_tmp[2 * term : 2 * term + 2, :] = part
                rest = rest - part
            bias_tmp[6:16, :] = jnp.zeros((10, LANES), F32)
            ship_ref[own_flat + packed_rows : ship_rows, :] = bias_tmp[...].astype(BF16)

    (ship,) = call(
        ship_body,
        [sds((ship_rows, LANES), BF16)],
        [tmp_buffer, pltpu.VMEM((own_flat + 32, LANES), F32), pltpu.VMEM((16, LANES), F32)],
        [act, from_swap, from_cross, taps, bias_own, rim],
    )
    shipped = across(ship, [(2, 3)])

    grad_rows = 5 * channels

    def gradients(level, source, hidden, err_in, err_out, rows_at, pair_out):
        scale = np.float32(1.0 / math.sqrt(strips * level.rows * level.cols))
        first = kernel_terms(source, err_in, level.odd_pairs, rows_at[2], rows_at[0], level)
        pack_kernel_terms(pair_out.at[0], *first, scale)
        then = kernel_terms(hidden, err_out, level.pairs, rows_at[3], rows_at[1], level)
        pack_kernel_terms(pair_out.at[1], *then, scale)

    def finish(level, source, hidden, ei, eo, pair_out):
        at = (level.error - 1, level.error, level.error + 1, level.error)
        gradients(level, source, hidden, ei, eo.at[1 : 1 + level.pairs], at, pair_out)

    def store_in(level, d_out):
        def store(first, size, a, rows, value):
            d_out[first : first + size, a : a + rows, :] = value

        return store

    def beside_body(
        act_ref, swap_ref, cross_ref, fwd_ref, bias_ref, x0, h0, o0, i0,
        din_ref, dout_ref, hid_ref, x_ref, pair_ref, tmp,
    ):
        section = lax.axis_index("section")
        top, low = halo_readers(swap_ref, cross_ref)

        @pl.when(section == 0)
        def _():
            finish(fine, x0, h0, i0, o0, pair_ref)

        for level in levels[1:]:

            @pl.when(section == level.level)
            def _(level=level):
                own_input(level, x_ref, act_ref)
                halo_input(level, x_ref, top, low, tmp, x_margin)
                zero_tail(hid_ref, level, level.hidden_rows)
                forward(
                    level, x_ref, hid_ref, [fwd_ref.at[0], fwd_ref.at[1]], bias_ref, din_ref,
                    store_in(level, dout_ref), place(), chunk,
                )

    pair_shape = sds((2, grad_rows, LANES), F32)
    din_own, dout_own, hid_own, x_own, pair_first = call(
        beside_body,
        [field(second, 1), field(second, 0), field(second, 1), field(second, 2), pair_shape],
        [tmp_buffer],
        [act, from_swap, from_cross, fwd_own, bias_own, state[0], state[1], state[4], state[5]],
    )

    def step(level, gb, grad_row, d_in, d_out, back, eo, ei, bi, gu):
        mask = image_mask(level, -level.error, level.out_rows, *place())
        zero_edges(eo, level)
        zero_tail(ei, level, level.alloc)
        for p in range(level.pairs):
            part = gb[p, grad_row : grad_row + level.out_rows, :] * d_out[p, 0 : level.out_rows, :]
            eo[p + 1, 0 : level.out_rows, :] = jnp.where(mask[0], rounded(part), 0.0)
        backward(level, eo, ei, [back.at[0], back.at[1]], d_in, gb, grad_row, bi, gu, place(), chunk)

    third_rows = third.rows + 2 * third.error
    third_flat = up_to(third.pairs * third_rows, 16)

    def hand_down(upper, lower, gu, rc, gb):
        def emit(m, span, value):
            gb[m, 0 : 3 * upper.k_count, :] = rounded(value)

        coarsen(
            upper, lower, gu, rc, [(upper.k_first, upper.k_count)], [(3 * upper.k_first, 3 * upper.k_count)],
            emit, place(),
        )

    def second_error(gb, d_out, eo, first, rows):
        mask = image_mask(second, first - second.error, rows, *place())
        for p in range(second.pairs):
            part = gb[p, first : first + rows, :] * d_out[p, first : first + rows, :]
            eo[p + 1, first : first + rows, :] = jnp.where(mask[0], rounded(part), 0.0)

    def second_inside_body(in_ref, din_o, dout_o, back_o, eo, ei, bi, gu, gb, mid):
        @pl.when(lax.axis_index("section") == 1)
        def _():
            mid[...] = in_ref[...].astype(F32)
            for p in range(second.pairs):
                gb[p, g_end : g_end + g_in[1], :] = mid[p * g_in[1] : (p + 1) * g_in[1], :]
            zero_edges(eo, second)
            zero_tail(ei, second, second.alloc)
            second_error(gb, dout_o, eo, g_end, g_in[1])
            parts = [(g_end, g_in[1])]
            backward(second, eo, ei, [back_o.at[0], back_o.at[1]], din_o, gb, 0, bi, gu, place(), chunk, parts, parts)

    inside_shapes = [
        field(second, 2), field(second, 1), field(second, 0),
        sds((second.pairs, second.alloc + 8, LANES), F32), field(second, 0),
    ]
    inside_state = call(
        second_inside_body,
        inside_shapes,
        [pltpu.VMEM((in_rows, LANES), F32)],
        [in_near, din_own, dout_own, back_own],
    )

    def second_rim_body(
        rim_ref, din_o, dout_o, back_o, eo_i, ei_i, bi_i, gu_i, gb_i, third_ref, eo, ei, bi, gu, gb, rc, rims, flat
    ):
        @pl.when(lax.axis_index("section") == 1)
        def _():
            rims[...] = rim_ref[...].astype(F32)
            low = g_end + g_in[1]
            for p in range(second.pairs):
                at = p * 2 * g_end
                gb[p, 0:g_end, :] = rims[at : at + g_end, :]
                gb[p, low : low + g_end, :] = rims[at + g_end : at + 2 * g_end, :]
            second_error(gb, dout_o, eo, 0, g_end)
            second_error(gb, dout_o, eo, low, g_end)
            rows = up_to(g_end + 2, 8)
            in_parts = [(0, rows), (low + g_end - rows, rows)]
            back_parts = [(0, rows), (low + g_end - 2 - rows, rows)]
            backward(
                second, eo, ei, [back_o.at[0], back_o.at[1]], din_o, gb, 0, bi, gu, place(), chunk,
                in_parts, back_parts,
            )
            hand_down(second, third, gu, rc, gb)
            at = second.up_shift
            for p in range(third.pairs):
                flat[p * third_rows : (p + 1) * third_rows, :] = gb[p, at : at + third_rows, :]
            third_ref[...] = flat[0:third_flat, :].astype(BF16)

    coarse_tmp = pltpu.VMEM((second.pairs, 3 * second.k_count + 8, LANES), F32)
    third_grad, eo_own, ei_own, bi_own, *_ = call(
        second_rim_body,
        [sds((third_flat, LANES), BF16), *inside_shapes],
        [coarse_tmp, pltpu.VMEM((rim_rows, LANES), F32), pltpu.VMEM((third_flat + 16, LANES), F32)],
        [rim_near, din_own, dout_own, back_own, *inside_state],
        aliases={4 + i: 1 + i for i in range(len(inside_shapes))},
        flops=4 * 10**9,
    )
    third_to_last = across(third_grad, [(1, 3), (3, 2), (2, 0), (0, 1)])
    third_to_own = across(third_grad, [(1, 2)])

    def shipped_body(ship_ref, own_ref, x_o, hid_o, eo_o, ei_o, din_s, dout_s, back_s, pair_ref, fwd_s, xb, hb, own):
        @pl.when(lax.axis_index("section") == 1)
        def _():
            finish(second, x_o, hid_o, ei_o, eo_o, pair_ref)

        @pl.when(lax.axis_index("section") == 3)
        def _():
            level = third
            values = []
            for t in range(2 * TAPS):
                pack = ship_ref[own_flat + t * half : own_flat + (t + 1) * half, :].astype(F32)
                values.append(jnp.concatenate([pack[:, :channels], pack[:, channels:]], axis=0))
            expand(values, fwd_s, back_s)
            terms = ship_ref[own_flat + packed_rows : ship_rows, :].astype(F32)
            bias = terms[0:2] + terms[2:4] + terms[4:6]
            own[0:own_flat, :] = ship_ref[0:own_flat, :].astype(F32)
            shipped_input(level, xb, own)
            zero_tail(hb, level, level.hidden_rows)
            forward(level, xb, hb, [fwd_s.at[0], fwd_s.at[1]], bias, din_s, store_in(level, dout_s), place(), chunk)

    din_s, dout_s, back_s, pair_second = call(
        shipped_body,
        [field(third, 1), field(third, 0), matrix_shape, pair_shape],
        [
            pltpu.VMEM((2, 2 * LANES, 3 * LANES), BF16),
            buffer(third, 2),
            buffer(third, 1),
            pltpu.VMEM((own_flat + 16, LANES), F32),
        ],
        [shipped, third_to_own, x_own, hid_own, eo_own, ei_own],
    )

    def last_body(
        pair0, pair1, own_ref, last_ref, din_o, dout_o, hid_o, x_o, back_o, din_s, dout_s, back_s,
        keep_ref, send_ref, bi, pair_out, gb, eo, ei, gu, rc, flat,
    ):
        section = lax.axis_index("section")
        odd = is_odd()

        def take(source):
            flat[...] = source[...].astype(F32)
            for p in range(third.pairs):
                gb[p, 0:third_rows, :] = flat[p * third_rows : (p + 1) * third_rows, :]

        @pl.when(section == 0)
        def _():
            pair_out[...] = pair0[...]

        @pl.when(section == 1)
        def _():
            pair_out[...] = pair1[...]

        @pl.when(section == 2)
        def _():
            take(own_ref)
            step(third, gb, 0, din_o, dout_o, back_o, eo, ei, bi, None)
            finish(third, x_o, hid_o, ei, eo, pair_out)

        @pl.when(section == 3)
        def _():
            take(last_ref)
            step(third, gb, 0, din_s, dout_s, back_s, eo, ei, None, gu)
            hand_down(third, last, gu, rc, gb)
            step(last, gb, third.up_shift, din_o, dout_o, back_o, eo, ei, bi, None)
            finish(last, x_o, hid_o, ei, eo, pair_out)

        first, then = pair_out[0], pair_out[1]
        keep_ref[...] = jnp.where(odd, then, first)
        send_ref[...] = jnp.where(odd, first, then)

    half_shape = sds((grad_rows, LANES), F32)
    keep, send, bi_last = call(
        last_body,
        [half_shape, half_shape, field(third, 0)],
        [
            pltpu.VMEM((2, grad_rows, LANES), F32),
            buffer(third, 0),
            buffer(third, 2),
            buffer(third, 1),
            buffer(fine, 0),
            coarse_tmp,
            pltpu.VMEM((third_flat, LANES), F32),
        ],
        [
            pair_first, pair_second, third_to_own, third_to_last, din_own, dout_own, hid_own, x_own, back_own,
            din_s, dout_s, back_s,
        ],
    )

    total = keep + lax.ppermute(send, "strip", swap_pairs)
    step = 2
    while step < strips:
        mine = lax.reduce_precision(total, 8, 7)
        small = mine.astype(BF16)
        offsets = (step, 2 * step, 3 * step) if 2 * step < strips else (step,)
        got = [lax.ppermute(small, "strip", [(i, i ^ o) for i in range(strips)]).astype(F32) for o in offsets]
        total = mine + got[0]
        if len(got) == 3:
            total = total + (got[1] + got[2])
        step *= len(got) + 1
    other = lax.ppermute(total, "strip", swap_pairs)

    def noise_body(bi_f, bi_o, bi_l, noise_ref):
        section = lax.axis_index("section")

        for level, source in ((fine, bi_f), (second, bi_o), (third, bi_l), (last, bi_l)):

            @pl.when(section == level.level)
            def _(level=level, source=source):
                write_noise(level, source, noise_ref)

    (noise,) = call(noise_body, [strip_shape], [], [state[6], bi_own, bi_last], final=(0,))

    def final_body(mine_ref, other_ref, kernel_ref, bias_ref):
        odd = is_odd()
        half = channels
        for c in range(2):
            if c == 0:
                value = jnp.where(odd, other_ref[...], mine_ref[...])
            else:
                value = jnp.where(odd, mine_ref[...], other_ref[...])
            for dy in range(3):
                kernel_ref[c, dy * 192 : dy * 192 + 128, :] = value[dy * half : (dy + 1) * half].T
            pair = value[3 * half : 4 * half].T
            kernel_ref[c, 128:192, :] = pair[:half]
            kernel_ref[c, 320:384, :] = pair[half:]
            kernel_ref[c, 512:576, :] = value[4 * half : 5 * half].T[:half]
            bias_ref[c : c + 1, :] = half_swap(value[4 * half : 4 * half + 1])[:, :half]

    kernel_sum, bias_sum = call(
        final_body,
        [sds((2, TAPS * channels, channels), F32), sds((2, channels), F32)],
        [],
        [total, other],
        final=(0, 1),
    )
    return (
        noise[None, None],
        kernel_sum.reshape(1, 2, 3, 3, channels, channels),
        bias_sum[None],
    )


def solution(mesh):
    strips = mesh.shape["strip"]
    sections = mesh.shape["section"]
    return jax.shard_map(
        functools.partial(local, strips, sections),
        mesh=mesh,
        in_specs=(
            P(None, "strip", None),
            P("section", None, "strip", None),
            P("section", None, None, None, None, None),
            P("section", None, None),
        ),
        out_specs=(
            P("section", None, "strip", None),
            P("section", None, None, None, None, None),
            P("section", None, None),
        ),
        check_vma=False,
    )
```

```python
import functools
import math

import jax
import jax.numpy as jnp
import numpy as np
from jax import lax
from jax.experimental import pallas as pl
from jax.experimental.pallas import tpu as pltpu
from jax.sharding import PartitionSpec as P

LEAK = 0.05
LANES = 128
F32 = jnp.float32
BF16 = jnp.bfloat16
TAPS = 9
VMEM_BYTES = 24 * 1024 * 1024


def up_to(value, step):
    return -(-value // step) * step


class Level:
    def __init__(self, level, rows, cols):
        self.level = level
        self.rows = rows * 3**level // 4**level
        self.cols = cols * 3**level // 4**level
        self.pairs = -(-self.cols // 2)
        self.odd_pairs = -(-(self.cols + 1) // 2)

    def margin(self, error):
        self.error = error
        self.x_margin = error + 2
        self.x_rows = self.rows + 2 * (error + 2)
        self.hidden_rows = up_to(self.rows + 2 * (error + 1) + 2, 8) - 2
        self.out_rows = up_to(self.rows + 2 * error + 2, 8) - 2
        self.in_rows = up_to(self.rows + 2 * (error - 1) + 2, 8) - 2
        self.back_rows = up_to(self.rows + 2 * (error - 2) + 2, 8) - 2
        self.own_rows = up_to(self.rows, 16)
        self.alloc = up_to(max(self.hidden_rows + 2, self.x_margin + self.own_rows + 2), 8) + 8


def levels_of(rows, cols, count):
    levels = [Level(s, rows, cols) for s in range(count)]
    levels[-1].margin(2)
    for s in range(count - 2, -1, -1):
        fine, coarse = levels[s], levels[s + 1]
        first = -coarse.error
        last = coarse.rows + coarse.error - 1
        low = 4 * (first // 3) + (-1, 1, 2)[first % 3]
        high = 4 * (last // 3) + (1, 2, 4)[last % 3]
        fine.margin(max(-low, high - fine.rows + 1) + 2)
        fine.k_first = first // 3
        fine.k_count = up_to(last // 3 - fine.k_first + 1, 8)
        fine.up_shift = -3 * fine.k_first - coarse.error
        start = fine.error - 2 + 4 * fine.k_first - 1
        fine.gu_row = max(0, -start)
        fine.gu_start = start + fine.gu_row
        assert fine.rows % 4 == 0
    return levels


def column_weights(fine, coarse):
    matrix = np.zeros((coarse, fine), np.float32)
    for x in range(fine):
        num = max((2 * x + 1) * coarse - fine, 0)
        low = num // (2 * fine)
        frac = np.float32(num - 2 * fine * low) / np.float32(2 * fine)
        matrix[low, x] += np.float32(1.0) - frac
        matrix[min(low + 1, coarse - 1), x] += frac
    return matrix


def lane_index(shape):
    return lax.broadcasted_iota(jnp.int32, shape, len(shape) - 1)


def half_swap(value):
    return pltpu.roll(value, LANES // 2, value.ndim - 1)


def twice(bias):
    return jnp.concatenate([bias, bias], axis=1)


def rounded(value):
    return value.astype(BF16).astype(F32)


def image_mask(level, base, count, strip, strips):
    row = lax.broadcasted_iota(jnp.int32, (1, count, LANES), 1) + base
    low = jnp.where(strip == 0, 0, -(10**6))
    high = jnp.where(strip == strips - 1, level.rows, 10**6)
    return (row >= low) & (row < high)


def odd_column_mask(level, first, count, mask):
    if first > 0 and 2 * (first + count - 1) < level.cols:
        return mask
    shape = (count, mask.shape[1], LANES)
    half = lax.broadcasted_iota(jnp.int32, shape, 2) // (LANES // 2)
    col = 2 * (first + lax.broadcasted_iota(jnp.int32, shape, 0)) - 1 + half
    return mask & (col >= 0) & (col < level.cols)


def conv(source, kernel, count, segments, chunk, emit):
    total = sum(rows for _, rows in segments)
    for first in range(0, count, chunk):
        size = min(chunk, count - first)
        blocks = [source[first : first + size + 1, a : a + rows, :] for a, rows in segments]
        block = blocks[0] if len(blocks) == 1 else jnp.concatenate(blocks, axis=1)
        left = block[:size].reshape(size * total, LANES).astype(BF16)
        right = block[1:].reshape(size * total, LANES).astype(BF16)
        by_row = jnp.dot(jnp.concatenate([left, right], axis=1), kernel[...], preferred_element_type=F32)
        result = by_row[:, :LANES]
        for dy in (1, 2):
            part = by_row[:, dy * LANES : (dy + 1) * LANES]
            result = result + pltpu.roll(part, size * total - dy, 0)
        result = result.reshape(size, total, LANES)
        at = 0
        for a, rows in segments:
            emit(first, size, a, rows - 2, result[:, at : at + rows - 2])
            at += rows


def kernel_terms(source, error, count, source_row, error_row, level):
    rows = level.own_rows
    err = error[0:count, error_row : error_row + rows, :]
    if rows != level.rows:
        row = lax.broadcasted_iota(jnp.int32, (1, rows, LANES), 1)
        err = jnp.where(row < level.rows, err, 0.0)
    total = jnp.sum(err, axis=(0, 1)).reshape(1, LANES)
    parts = []
    for dy in range(3):
        block = source[0 : count + 1, source_row + dy : source_row + dy + rows, :].astype(BF16)
        parts.append(block[:count].reshape(count * rows, LANES))
        parts.append(block[1:].reshape(count * rows, LANES))
    stacked = jnp.concatenate(parts, axis=1)
    product = lax.dot_general(
        err.astype(BF16).reshape(count * rows, LANES),
        stacked,
        (((0,), (0,)), ((), ())),
        preferred_element_type=F32,
    )
    return product, total


def pack_kernel_terms(out_ref, product, total, scale):
    half = LANES // 2
    low = lane_index((1, LANES)) < half
    thirds = []
    for dy in range(3):
        first = product[:, 2 * dy * LANES : (2 * dy + 1) * LANES]
        then = product[:, (2 * dy + 1) * LANES : (2 * dy + 2) * LANES]
        moved = half_swap(then[half:])
        out_ref[dy * half : (dy + 1) * half, :] = (
            first[:half] + jnp.where(low, half_swap(first[half:]), moved)
        ) * scale
        thirds.append((then[:half] + moved) * scale)
    bias = (total + half_swap(total)) * scale
    out_ref[3 * half : 4 * half, :] = jnp.where(low, thirds[0], half_swap(thirds[1]))
    out_ref[4 * half : 5 * half, :] = jnp.where(low, thirds[2], bias)


def toeplitz(taps):
    half = LANES // 2
    zero = jnp.zeros((half, half), F32)
    columns = []
    for dy in range(3):
        rows = []
        for k in range(4):
            left = taps[dy * 3 + k] if k < 3 else zero
            right = taps[dy * 3 + k - 1] if k > 0 else zero
            rows.append(jnp.concatenate([left, right], axis=1))
        columns.append(jnp.concatenate(rows, axis=0))
    return jnp.concatenate(columns, axis=1)


def toeplitz_back(taps):
    half = LANES // 2
    zero = jnp.zeros((half, half), F32)
    by_row = []
    for dy in range(3):
        columns = []
        for k in range(4):
            top = taps[(2 - dy) * 3 + 2 - k] if k < 3 else zero
            bottom = taps[(2 - dy) * 3 + 3 - k] if k > 0 else zero
            columns.append(jnp.concatenate([top, bottom], axis=0))
        by_row.append(jnp.concatenate([jnp.concatenate(columns[i : i + 2], axis=1).T for i in (0, 2)], axis=0))
    return jnp.concatenate(by_row, axis=1)


def zero_tail(ref, level, rows):
    if level.alloc > rows:
        ref[0 : level.pairs + 1, rows : level.alloc, :] = jnp.zeros((level.pairs + 1, level.alloc - rows, LANES), F32)
    if level.odd_pairs < level.pairs + 1:
        ref[level.odd_pairs : level.pairs + 1, 0 : level.alloc, :] = jnp.zeros(
            (level.pairs + 1 - level.odd_pairs, level.alloc, LANES), F32
        )


def zero_edges(ref, level):
    zero = jnp.zeros((level.alloc, LANES), F32)
    ref[0, 0 : level.alloc, :] = zero
    ref[level.pairs + 1, 0 : level.alloc, :] = zero


def slope(value):
    return LEAK + (1.0 - LEAK) * (0.5 + 0.5 * jnp.tanh(0.5 * value))


def forward(level, xb, hb, kernels, bias, d_in, d_out, place, chunk, hidden_parts=None, out_parts=None):
    strip, strips = place
    bias_in, bias_out = bias[0:1], bias[1:2]

    def first_layer(first, size, a, rows, value):
        mask = image_mask(level, a - (level.error + 1), rows, strip, strips)
        pre = value + bias_in
        small = jnp.exp(-jnp.abs(pre))
        soft = jnp.maximum(pre, 0.0) + jnp.log(1.0 + small)
        act = LEAK * pre + (1.0 - LEAK) * soft
        keep = odd_column_mask(level, first, size, mask)
        hb[first : first + size, a : a + rows, :] = jnp.where(keep, rounded(act), 0.0)
        d_in[first : first + size, a : a + rows, :] = slope(pre)

    conv(xb, kernels[0], level.odd_pairs, hidden_parts or [(0, level.hidden_rows + 2)], chunk, first_layer)

    def second_layer(first, size, a, rows, value):
        d_out(first, size, a, rows, slope(value + bias_out))

    conv(hb, kernels[1], level.pairs, out_parts or [(0, level.out_rows + 2)], chunk, second_layer)


def backward(level, eo, ei, kernels, d_in, grad, grad_row, bi, gu, place, chunk, in_parts=None, back_parts=None):
    strip, strips = place

    def inner(first, size, a, rows, value):
        mask = image_mask(level, a - (level.error - 1), rows, strip, strips)
        keep = odd_column_mask(level, first, size, mask)
        part = d_in[first : first + size, 2 + a : 2 + a + rows, :]
        ei[first : first + size, a : a + rows, :] = jnp.where(keep, rounded(value * part), 0.0)

    conv(eo, kernels[1], level.odd_pairs, in_parts or [(0, level.in_rows + 2)], chunk, inner)

    def outer(first, size, a, rows, value):
        if bi is not None:
            bi[first : first + size, a : a + rows, :] = value
        if gu is not None:
            mask = image_mask(level, a - (level.error - 2), rows, strip, strips)
            part = grad[first : first + size, grad_row + 2 + a : grad_row + 2 + a + rows, :]
            at = level.gu_row + a
            gu[first : first + size, at : at + rows, :] = jnp.where(mask, rounded(part + value), 0.0)

    conv(ei, kernels[0], level.pairs, back_parts or [(0, level.back_rows + 2)], chunk, outer)


def write_noise(level, bi, noise):
    total_rows = noise.shape[0]
    row = lax.broadcasted_iota(jnp.int32, (level.own_rows, LANES), 0)
    lane = lane_index((level.own_rows, LANES))
    for p in range(noise.shape[1] // LANES):
        at = slice(p * LANES, (p + 1) * LANES)
        if p < level.pairs:
            part = bi[p, level.error - 2 : level.error - 2 + level.own_rows, :]
            if level.own_rows != level.rows:
                part = jnp.where(row < level.rows, part, 0.0)
            if 2 * p + 1 >= level.cols:
                part = jnp.where(lane < LANES // 2, part, 0.0)
            noise[0 : level.own_rows, at] = part.astype(BF16)
            if level.own_rows < total_rows:
                noise[level.own_rows : total_rows, at] = jnp.zeros((total_rows - level.own_rows, LANES), BF16)
        else:
            noise[:, at] = jnp.zeros((total_rows, LANES), BF16)


def coarsen(fine, coarse, gu, rc, ranges, spans, emit, place, edges=True):
    strip, strips = place
    for k, count in ranges:
        start = fine.gu_start + 4 * (k - fine.k_first)
        at = 3 * (k - fine.k_first)
        for p in range(fine.pairs):
            f = [gu[p, pl.ds(start + a, count, stride=4), :] for a in range(6)]
            rc[p, pl.ds(at, count, stride=3), :] = 0.125 * f[0] + 0.875 * f[1] + 0.375 * f[2]
            rc[p, pl.ds(at + 1, count, stride=3), :] = 0.625 * f[2] + 0.625 * f[3]
            rc[p, pl.ds(at + 2, count, stride=3), :] = 0.375 * f[3] + 0.875 * f[4] + 0.125 * f[5]
    if edges:
        top = -3 * fine.k_first
        low = top + coarse.rows - 1
        on_top = jnp.where(strip == 0, 1.0, 0.0).astype(F32)
        on_low = jnp.where(strip == strips - 1, 1.0, 0.0).astype(F32)
        every = slice(0, fine.pairs)
        rc[every, top : top + 1, :] = rc[every, top : top + 1, :] + on_top * rc[every, top - 1 : top, :]
        rc[every, low : low + 1, :] = rc[every, low : low + 1, :] + on_low * rc[every, low + 1 : low + 2, :]
    matrix = column_weights(fine.cols, coarse.cols)
    matrix = np.pad(matrix, ((0, 2 * coarse.pairs - coarse.cols), (0, 2 * fine.pairs - fine.cols)))
    lane = lane_index((1, LANES))

    def weights(low_lanes, high_lanes):
        return jnp.where(lane < LANES // 2, np.float32(low_lanes), np.float32(high_lanes))

    for span, (row, rows) in enumerate(spans):
        at = row - 3 * fine.k_first
        for m in range(coarse.pairs):
            total = None
            for q in range(fine.pairs):
                same = (matrix[2 * m, 2 * q], matrix[2 * m + 1, 2 * q + 1])
                cross = (matrix[2 * m, 2 * q + 1], matrix[2 * m + 1, 2 * q])
                value = rc[q, at : at + rows, :] if any(same) or any(cross) else None
                for pair, moved in ((same, False), (cross, True)):
                    if any(pair):
                        term = (half_swap(value) if moved else value) * weights(*pair)
                        total = term if total is None else total + term
            emit(m, span, total)


def own_input(level, xb, act):
    zero_edges(xb, level)
    lane = lane_index((1, LANES))
    for p in range(level.pairs):
        own = act[0 : level.own_rows, p * LANES : (p + 1) * LANES].astype(F32)
        if 2 * p + 1 >= level.cols:
            own = jnp.where(lane < LANES // 2, own, 0.0)
        xb[p + 1, level.x_margin : level.x_margin + level.own_rows, :] = own


def zero_after(level, xb):
    end = level.x_rows
    if end < level.alloc:
        xb[1 : level.pairs + 1, end : level.alloc, :] = jnp.zeros((level.pairs, level.alloc - end, LANES), F32)


def halo_input(level, xb, top, low, tmp, payload_rows):
    margin = level.x_margin
    end = margin + level.rows
    lane = lane_index((1, LANES))
    for p in range(level.pairs):
        at = slice(p * LANES, (p + 1) * LANES)
        upper, lower = top(at), low(at)
        if 2 * p + 1 >= level.cols:
            upper, lower = (jnp.where(lane < LANES // 2, v, 0.0) for v in (upper, lower))
        tmp[0, 0 : upper.shape[0], :] = upper
        tmp[1, 0 : lower.shape[0], :] = lower
        xb[p + 1, 0:margin, :] = tmp[0, payload_rows - margin : payload_rows, :]
        xb[p + 1, end : end + margin, :] = tmp[1, 0:margin, :]
    zero_after(level, xb)


def shipped_input(level, xb, own):
    zero_edges(xb, level)
    for p in range(level.pairs):
        xb[p + 1, 0 : level.x_rows, :] = own[p * level.x_rows : (p + 1) * level.x_rows, :]
    zero_after(level, xb)


def call(body, out_shape, scratch, operands, final=(), outside=(), aliases=None, flops=1000):
    operands = [
        pltpu.with_memory_space_constraint(x, pltpu.HBM if i in outside else pltpu.VMEM)
        for i, x in enumerate(operands)
    ]
    out_shape = [s if i in final else pltpu.VMEM(s.shape, s.dtype) for i, s in enumerate(out_shape)]
    return pl.pallas_call(
        body,
        out_shape=out_shape,
        in_specs=[pl.BlockSpec(memory_space=pltpu.VMEM)] * len(operands),
        out_specs=[pl.BlockSpec(memory_space=pltpu.VMEM)] * len(out_shape),
        scratch_shapes=scratch,
        input_output_aliases=aliases or {},
        compiler_params=pltpu.CompilerParams(vmem_limit_bytes=VMEM_BYTES),
        cost_estimate=pl.CostEstimate(flops=flops, bytes_accessed=1000, transcendentals=0),
    )(*operands)


def sds(shape, dtype):
    return jax.ShapeDtypeStruct(shape, dtype)


def field(level, extra):
    return sds((level.pairs + extra, level.alloc, LANES), F32)


def buffer(level, extra):
    return pltpu.VMEM((level.pairs + extra, level.alloc, LANES), F32)


def local(strips, sections, cotangent, activations, weights, biases):
    row_count, flat_width = activations.shape[2:]
    channels = weights.shape[-1]
    half = channels // 2
    cols = flat_width // channels
    assert 2 * channels == LANES and sections == 4 and cotangent.shape[0] == 1
    levels = levels_of(row_count, cols, sections)
    fine, second, third, last = levels
    x_margin, g_margin = fine.x_margin, fine.error
    payload = up_to(x_margin + g_margin, 16)
    pair_count = fine.pairs
    chunk = 4

    def place():
        return lax.axis_index("strip"), strips

    def is_odd():
        return lax.rem(lax.axis_index("strip"), 2) == 1

    packed_rows = TAPS * channels
    own_flat = up_to(third.pairs * third.x_rows, 16)
    ship_rows = own_flat + packed_rows + 16

    def halo_body(
        act_hbm, cot_hbm, bias_hbm, act_ref, cot_ref, both_ref, swap_ref, cross_ref, xs, cs, ts
    ):
        both_ref[0:2, :] = twice(bias_hbm[...])
        section = lax.axis_index("section")
        odd = is_odd()

        live = jnp.int32(fine.rows)
        for level in levels[1:]:
            live = jnp.where(section == level.level, level.rows, live)
        for p in range(pair_count):
            at = slice(p * LANES, (p + 1) * LANES)
            act_ref[:, at] = act_hbm[:, at]
            cot_ref[:, at] = cot_hbm[:, at]
            xs[p, 0:row_count, :] = act_hbm[:, at].astype(F32)
            cs[p, 0:row_count, :] = cot_hbm[:, at].astype(F32)
            ts[0, p, 0:x_margin, :] = xs[p, 0:x_margin, :]
            ts[0, p, x_margin : x_margin + g_margin, :] = cs[p, 0:g_margin, :]
            ts[1, p, 0:x_margin, :] = xs[p, pl.ds(live - x_margin, x_margin), :]
            ts[1, p, x_margin : x_margin + g_margin, :] = cs[p, row_count - g_margin : row_count, :]
            upper = ts[0, p, 0:payload, :]
            lower = ts[1, p, 0:payload, :]
            swap_ref[:, at] = jnp.where(odd, upper, lower).astype(BF16)
            cross_ref[:, at] = jnp.where(odd, lower, upper).astype(BF16)

    strip_shape = sds((row_count, flat_width), BF16)
    halo_shape = sds((payload, flat_width), BF16)
    taps = weights.reshape(2 * TAPS, channels, channels)
    act, cot, bias_own, to_swap, to_cross = call(
        halo_body,
        [
            strip_shape, strip_shape, sds((8, LANES), F32), halo_shape, halo_shape,
        ],
        [
            pltpu.VMEM((pair_count, row_count + 16, LANES), F32),
            pltpu.VMEM((pair_count, row_count + 16, LANES), F32),
            pltpu.VMEM((2, pair_count, payload + 16, LANES), F32),
        ],
        [activations[0, 0], cotangent[0], biases[0]],
        outside=(0, 1, 2),
    )
    swap_pairs = [(i, i ^ 1) for i in range(strips)]
    cross_pairs = [(i, i + 1) for i in range(1, strips - 1, 2)] + [(i + 1, i) for i in range(1, strips - 1, 2)]
    from_cross = lax.ppermute(to_cross, "strip", cross_pairs)
    from_swap = lax.ppermute(to_swap, "strip", swap_pairs)


    def expand(tap_list, forward_ref, back_ref):
        for c in range(2):
            chosen = tap_list[c * TAPS : (c + 1) * TAPS]
            forward_ref[c, :, :] = toeplitz(chosen).astype(BF16)
            back_ref[c, :, :] = toeplitz_back(chosen).astype(BF16)

    def matrix_body(taps_ref, bias_ref, forward_ref, back_ref):
        expand([taps_ref[t].astype(F32) for t in range(2 * TAPS)], forward_ref, back_ref)

    matrix_shape = sds((2, 2 * LANES, 3 * LANES), BF16)
    fwd_own, back_own = call(matrix_body, [matrix_shape, matrix_shape], [], [taps, bias_own])

    def across(value, pairs):
        return lax.ppermute(value, "section", pairs)

    inside = [[(17, row_count)], [(16, row_count)]]
    ends = [[(0, 24), (row_count + 10, 24)], [(0, 24), (row_count + 8, 24)]]
    assert fine.error == 15 and fine.x_margin == 17 and row_count >= 32
    g_in = (4, second.rows - 8)
    g_end = second.error + g_in[0]
    in_rows = up_to(second.pairs * g_in[1], 16)
    rim_rows = up_to(second.pairs * 2 * g_end, 16)

    def error_of(level, gb, eo, mask_place):
        def error(first, size, a, rows, value):
            mask = image_mask(level, a - level.error, rows, *mask_place)
            part = gb[first : first + size, a : a + rows, :]
            eo[first + 1 : first + 1 + size, a : a + rows, :] = jnp.where(mask, rounded(part * value), 0.0)

        return error

    def inside_body(
        act_ref, cot_ref, fwd_ref, back_ref, bias_ref, hop_ref, xb, hb, db, gb, eo, ei, bi, gu, rc, flat,
    ):
        section = lax.axis_index("section")

        @pl.when(section == 0)
        def _():
            level = fine
            own_input(level, xb, act_ref)
            zero_after(level, xb)
            zero_edges(eo, level)
            zero_tail(hb, level, level.hidden_rows)
            zero_tail(ei, level, level.alloc)
            for p in range(level.pairs):
                gb[p, g_margin : g_margin + row_count, :] = cot_ref[:, p * LANES : (p + 1) * LANES].astype(F32)
            forward(
                level, xb, hb, [fwd_ref.at[0], fwd_ref.at[1]], bias_ref, db, error_of(level, gb, eo, place()),
                place(), chunk, *inside,
            )
            backward(
                level, eo, ei, [back_ref.at[0], back_ref.at[1]], db, gb, 0, bi, gu, place(), chunk,
                inside[1], inside[1],
            )

            def emit(m, span, rows):
                flat[m * g_in[1] : (m + 1) * g_in[1], :] = rows

            coarsen(fine, second, gu, rc, [(0, 16)], [g_in], emit, place(), edges=False)
            hop_ref[...] = flat[0:in_rows, :].astype(BF16)

    coarse_buffer = pltpu.VMEM((fine.pairs, 3 * fine.k_count + 8, LANES), F32)
    state_shapes = [
        field(fine, 2), field(fine, 1), field(fine, 1), field(fine, 0),
        field(fine, 2), field(fine, 1), field(fine, 0), field(fine, 0),
    ]
    hop_in, *state = call(
        inside_body,
        [sds((in_rows, LANES), BF16), *state_shapes],
        [coarse_buffer, pltpu.VMEM((in_rows + 16, LANES), F32)],
        [act, cot, fwd_own, back_own, bias_own],
    )
    in_near = across(hop_in, [(0, 1), (1, 3), (3, 2), (2, 0)])

    def halo_readers(swap_ref, cross_ref):
        odd = is_odd()

        def top(at):
            return jnp.where(odd, swap_ref[:, at].astype(F32), cross_ref[:, at].astype(F32))

        def low(at):
            return jnp.where(odd, cross_ref[:, at].astype(F32), swap_ref[:, at].astype(F32))

        return top, low

    def rim_body(
        swap_ref, cross_ref, fwd_ref, back_ref, bias_ref, xi, hi, di, gi, oi, ii, bii, ui,
        rim_ref, xb, hb, db, gb, eo, ei, bi, gu, rc, flat, tmp,
    ):
        section = lax.axis_index("section")
        top, low = halo_readers(swap_ref, cross_ref)

        @pl.when(section == 0)
        def _():
            level = fine
            end = x_margin + row_count
            for p in range(level.pairs):
                at = slice(p * LANES, (p + 1) * LANES)
                tmp[0, 0:payload, :] = top(at)
                tmp[1, 0:payload, :] = low(at)
                xb[p + 1, 0:x_margin, :] = tmp[0, 0:x_margin, :]
                xb[p + 1, end : end + x_margin, :] = tmp[1, 0:x_margin, :]
                gb[p, 0:g_margin, :] = tmp[0, x_margin : x_margin + g_margin, :]
                gb[p, g_margin + row_count : 2 * g_margin + row_count, :] = tmp[
                    1, x_margin : x_margin + g_margin, :
                ]
            forward(
                level, xb, hb, [fwd_ref.at[0], fwd_ref.at[1]], bias_ref, db, error_of(level, gb, eo, place()),
                place(), chunk, ends[0], ends[0],
            )
            backward(
                level, eo, ei, [back_ref.at[0], back_ref.at[1]], db, gb, 0, bi, gu, place(), chunk, ends[1], ends[1]
            )

            def emit(m, span, rows):
                at = m * 2 * g_end + span * g_end
                flat[at : at + g_end, :] = rows[0:g_end]

            last_k = (second.rows + second.error) // 3
            coarsen(
                fine, second, gu, rc,
                [(fine.k_first, 8), (last_k - 7, 8)],
                [(-second.error, up_to(g_end, 8)), (g_in[0] + g_in[1], up_to(g_end, 8))],
                emit, place(),
            )
            rim_ref[...] = flat[0:rim_rows, :].astype(BF16)

    tmp_buffer = pltpu.VMEM((2, payload + 16, LANES), F32)
    rim, *state = call(
        rim_body,
        [sds((rim_rows, LANES), BF16), *state_shapes],
        [coarse_buffer, pltpu.VMEM((rim_rows + 32, LANES), F32), tmp_buffer],
        [from_swap, from_cross, fwd_own, back_own, bias_own, *state],
        aliases={5 + i: 1 + i for i in range(len(state_shapes))},
        flops=2 * 10**9,
    )
    rim_near = across(rim, [(0, 1), (1, 3), (3, 2), (2, 0)])

    def ship_body(act_ref, swap_ref, cross_ref, taps_ref, both_ref, rim_ref, ship_ref, tmp, flat, bias_tmp):
        top, low = halo_readers(swap_ref, cross_ref)

        @pl.when(lax.axis_index("section") == 2)
        def _():
            level = third
            margin = level.x_margin
            for p in range(level.pairs):
                at = slice(p * LANES, (p + 1) * LANES)
                tmp[0, 0:payload, :] = top(at)
                tmp[1, 0:payload, :] = low(at)
                to = p * level.x_rows
                end = to + margin + level.rows
                flat[to : to + margin, :] = tmp[0, x_margin - margin : x_margin, :]
                flat[to + margin : to + margin + level.own_rows, :] = act_ref[0 : level.own_rows, at].astype(F32)
                flat[end : end + margin, :] = tmp[1, 0:margin, :]
            ship_ref[0:own_flat, :] = flat[0:own_flat, :].astype(BF16)
            for t in range(2 * TAPS):
                at = own_flat + t * half
                value = taps_ref[t].astype(F32)
                ship_ref[at : at + half, :] = jnp.concatenate([value[:half], value[half:]], axis=1).astype(BF16)
            rest = both_ref[0:2, :]
            for term in range(3):
                part = rounded(rest)
                bias_tmp[2 * term : 2 * term + 2, :] = part
                rest = rest - part
            bias_tmp[6:16, :] = jnp.zeros((10, LANES), F32)
            ship_ref[own_flat + packed_rows : ship_rows, :] = bias_tmp[0:16, :].astype(BF16)

    (ship,) = call(
        ship_body,
        [sds((ship_rows, LANES), BF16)],
        [tmp_buffer, pltpu.VMEM((own_flat + 32, LANES), F32), pltpu.VMEM((32, LANES), F32)],
        [act, from_swap, from_cross, taps, bias_own, rim],
    )
    shipped = across(ship, [(2, 3)])

    grad_rows = 5 * channels

    def gradients(level, source, hidden, err_in, err_out, rows_at, pair_out):
        scale = np.float32(1.0 / math.sqrt(strips * level.rows * level.cols))
        first = kernel_terms(source, err_in, level.odd_pairs, rows_at[2], rows_at[0], level)
        pack_kernel_terms(pair_out.at[0], *first, scale)
        then = kernel_terms(hidden, err_out, level.pairs, rows_at[3], rows_at[1], level)
        pack_kernel_terms(pair_out.at[1], *then, scale)

    def finish(level, source, hidden, ei, eo, pair_out):
        at = (level.error - 1, level.error, level.error + 1, level.error)
        gradients(level, source, hidden, ei, eo.at[1 : 1 + level.pairs], at, pair_out)

    def store_in(level, d_out):
        def store(first, size, a, rows, value):
            d_out[first : first + size, a : a + rows, :] = value

        return store

    def beside_body(
        act_ref, swap_ref, cross_ref, fwd_ref, bias_ref, x0, h0, o0, i0,
        din_ref, dout_ref, hid_ref, x_ref, pair_ref, tmp,
    ):
        section = lax.axis_index("section")
        top, low = halo_readers(swap_ref, cross_ref)

        @pl.when(section == 0)
        def _():
            finish(fine, x0, h0, i0, o0, pair_ref)

        for level in levels[1:]:

            @pl.when(section == level.level)
            def _(level=level):
                own_input(level, x_ref, act_ref)
                halo_input(level, x_ref, top, low, tmp, x_margin)
                zero_tail(hid_ref, level, level.hidden_rows)
                forward(
                    level, x_ref, hid_ref, [fwd_ref.at[0], fwd_ref.at[1]], bias_ref, din_ref,
                    store_in(level, dout_ref), place(), chunk,
                )

    pair_shape = sds((2, grad_rows, LANES), F32)
    din_own, dout_own, hid_own, x_own, pair_first = call(
        beside_body,
        [field(second, 1), field(second, 0), field(second, 1), field(second, 2), pair_shape],
        [tmp_buffer],
        [act, from_swap, from_cross, fwd_own, bias_own, state[0], state[1], state[4], state[5]],
    )

    def step(level, gb, grad_row, d_in, d_out, back, eo, ei, bi, gu):
        mask = image_mask(level, -level.error, level.out_rows, *place())
        zero_edges(eo, level)
        zero_tail(ei, level, level.alloc)
        for p in range(level.pairs):
            part = gb[p, grad_row : grad_row + level.out_rows, :] * d_out[p, 0 : level.out_rows, :]
            eo[p + 1, 0 : level.out_rows, :] = jnp.where(mask[0], rounded(part), 0.0)
        backward(level, eo, ei, [back.at[0], back.at[1]], d_in, gb, grad_row, bi, gu, place(), chunk)

    third_rows = third.rows + 2 * third.error
    third_flat = up_to(third.pairs * third_rows, 16)

    def hand_down(upper, lower, gu, rc, gb):
        def emit(m, span, value):
            gb[m, 0 : 3 * upper.k_count, :] = rounded(value)

        coarsen(
            upper, lower, gu, rc, [(upper.k_first, upper.k_count)], [(3 * upper.k_first, 3 * upper.k_count)],
            emit, place(),
        )

    def second_error(gb, d_out, eo, first, rows):
        mask = image_mask(second, first - second.error, rows, *place())
        for p in range(second.pairs):
            part = gb[p, first : first + rows, :] * d_out[p, first : first + rows, :]
            eo[p + 1, first : first + rows, :] = jnp.where(mask[0], rounded(part), 0.0)

    def second_inside_body(in_ref, din_o, dout_o, back_o, eo, ei, bi, gu, gb, mid):
        @pl.when(lax.axis_index("section") == 1)
        def _():
            mid[...] = in_ref[...].astype(F32)
            for p in range(second.pairs):
                gb[p, g_end : g_end + g_in[1], :] = mid[p * g_in[1] : (p + 1) * g_in[1], :]
            zero_edges(eo, second)
            zero_tail(ei, second, second.alloc)
            second_error(gb, dout_o, eo, g_end, g_in[1])
            parts = [(g_end, g_in[1])]
            backward(second, eo, ei, [back_o.at[0], back_o.at[1]], din_o, gb, 0, bi, gu, place(), chunk, parts, parts)

    inside_shapes = [
        field(second, 2), field(second, 1), field(second, 0),
        sds((second.pairs, second.alloc + 8, LANES), F32), field(second, 0),
    ]
    inside_state = call(
        second_inside_body,
        inside_shapes,
        [pltpu.VMEM((in_rows, LANES), F32)],
        [in_near, din_own, dout_own, back_own],
    )

    def second_rim_body(
        rim_ref, din_o, dout_o, back_o, eo_i, ei_i, bi_i, gu_i, gb_i, third_ref, eo, ei, bi, gu, gb, rc, rims, flat
    ):
        @pl.when(lax.axis_index("section") == 1)
        def _():
            rims[...] = rim_ref[...].astype(F32)
            low = g_end + g_in[1]
            for p in range(second.pairs):
                at = p * 2 * g_end
                gb[p, 0:g_end, :] = rims[at : at + g_end, :]
                gb[p, low : low + g_end, :] = rims[at + g_end : at + 2 * g_end, :]
            second_error(gb, dout_o, eo, 0, g_end)
            second_error(gb, dout_o, eo, low, g_end)
            rows = up_to(g_end + 2, 8)
            in_parts = [(0, rows), (low + g_end - rows, rows)]
            back_parts = [(0, rows), (low + g_end - 2 - rows, rows)]
            backward(
                second, eo, ei, [back_o.at[0], back_o.at[1]], din_o, gb, 0, bi, gu, place(), chunk,
                in_parts, back_parts,
            )
            hand_down(second, third, gu, rc, gb)
            at = second.up_shift
            for p in range(third.pairs):
                flat[p * third_rows : (p + 1) * third_rows, :] = gb[p, at : at + third_rows, :]
            third_ref[...] = flat[0:third_flat, :].astype(BF16)

    coarse_tmp = pltpu.VMEM((second.pairs, 3 * second.k_count + 8, LANES), F32)
    third_grad, eo_own, ei_own, bi_own, *_ = call(
        second_rim_body,
        [sds((third_flat, LANES), BF16), *inside_shapes],
        [coarse_tmp, pltpu.VMEM((rim_rows, LANES), F32), pltpu.VMEM((third_flat + 16, LANES), F32)],
        [rim_near, din_own, dout_own, back_own, *inside_state],
        aliases={4 + i: 1 + i for i in range(len(inside_shapes))},
        flops=4 * 10**9,
    )
    third_to_last = across(third_grad, [(1, 3), (3, 2), (2, 0), (0, 1)])
    third_to_own = across(third_grad, [(1, 2)])

    def shipped_body(ship_ref, own_ref, x_o, hid_o, eo_o, ei_o, din_s, dout_s, back_s, pair_ref, fwd_s, xb, hb, own):
        @pl.when(lax.axis_index("section") == 1)
        def _():
            finish(second, x_o, hid_o, ei_o, eo_o, pair_ref)

        @pl.when(lax.axis_index("section") == 3)
        def _():
            level = third
            values = []
            for t in range(2 * TAPS):
                pack = ship_ref[own_flat + t * half : own_flat + (t + 1) * half, :].astype(F32)
                values.append(jnp.concatenate([pack[:, :channels], pack[:, channels:]], axis=0))
            expand(values, fwd_s, back_s)
            terms = ship_ref[own_flat + packed_rows : ship_rows, :].astype(F32)
            bias = terms[0:2] + terms[2:4] + terms[4:6]
            own[0:own_flat, :] = ship_ref[0:own_flat, :].astype(F32)
            shipped_input(level, xb, own)
            zero_tail(hb, level, level.hidden_rows)
            forward(level, xb, hb, [fwd_s.at[0], fwd_s.at[1]], bias, din_s, store_in(level, dout_s), place(), chunk)

    din_s, dout_s, back_s, pair_second = call(
        shipped_body,
        [field(third, 1), field(third, 0), matrix_shape, pair_shape],
        [
            pltpu.VMEM((2, 2 * LANES, 3 * LANES), BF16),
            buffer(third, 2),
            buffer(third, 1),
            pltpu.VMEM((own_flat + 16, LANES), F32),
        ],
        [shipped, third_to_own, x_own, hid_own, eo_own, ei_own],
    )

    def last_body(
        pair0, pair1, own_ref, last_ref, din_o, dout_o, hid_o, x_o, back_o, din_s, dout_s, back_s,
        keep_ref, send_ref, bi, pair_out, gb, eo, ei, gu, rc, flat,
    ):
        section = lax.axis_index("section")
        odd = is_odd()

        def take(source):
            flat[0:third_flat, :] = source[...].astype(F32)
            for p in range(third.pairs):
                gb[p, 0:third_rows, :] = flat[p * third_rows : (p + 1) * third_rows, :]

        @pl.when(section == 0)
        def _():
            pair_out[...] = pair0[...]

        @pl.when(section == 1)
        def _():
            pair_out[...] = pair1[...]

        @pl.when(section == 2)
        def _():
            take(own_ref)
            step(third, gb, 0, din_o, dout_o, back_o, eo, ei, bi, None)
            finish(third, x_o, hid_o, ei, eo, pair_out)

        @pl.when(section == 3)
        def _():
            take(last_ref)
            step(third, gb, 0, din_s, dout_s, back_s, eo, ei, None, gu)
            hand_down(third, last, gu, rc, gb)
            step(last, gb, third.up_shift, din_o, dout_o, back_o, eo, ei, bi, None)
            finish(last, x_o, hid_o, ei, eo, pair_out)

        first, then = pair_out[0], pair_out[1]
        keep_ref[...] = jnp.where(odd, then, first)
        send_ref[...] = jnp.where(odd, first, then)

    half_shape = sds((grad_rows, LANES), F32)
    keep, send, bi_last = call(
        last_body,
        [half_shape, half_shape, field(third, 0)],
        [
            pltpu.VMEM((2, grad_rows, LANES), F32),
            buffer(third, 0),
            buffer(third, 2),
            buffer(third, 1),
            buffer(fine, 0),
            coarse_tmp,
            pltpu.VMEM((third_flat + 16, LANES), F32),
        ],
        [
            pair_first, pair_second, third_to_own, third_to_last, din_own, dout_own, hid_own, x_own, back_own,
            din_s, dout_s, back_s,
        ],
    )

    total = keep + lax.ppermute(send, "strip", swap_pairs)
    step = 2
    while step < strips:
        mine = lax.reduce_precision(total, 8, 7)
        small = mine.astype(BF16)
        offsets = (step, 2 * step, 3 * step) if 2 * step < strips else (step,)
        got = [lax.ppermute(small, "strip", [(i, i ^ o) for i in range(strips)]).astype(F32) for o in offsets]
        total = mine + got[0]
        if len(got) == 3:
            total = total + (got[1] + got[2])
        step *= len(got) + 1
    other = lax.ppermute(total, "strip", swap_pairs)

    def noise_body(bi_f, bi_o, bi_l, noise_ref):
        section = lax.axis_index("section")

        for level, source in ((fine, bi_f), (second, bi_o), (third, bi_l), (last, bi_l)):

            @pl.when(section == level.level)
            def _(level=level, source=source):
                write_noise(level, source, noise_ref)

    (noise,) = call(noise_body, [strip_shape], [], [state[6], bi_own, bi_last], final=(0,))

    def final_body(mine_ref, other_ref, kernel_ref, bias_ref):
        odd = is_odd()
        half = channels
        bias_rows = []
        for c in range(2):
            if c == 0:
                value = jnp.where(odd, other_ref[...], mine_ref[...])
            else:
                value = jnp.where(odd, mine_ref[...], other_ref[...])
            for dy in range(3):
                kernel_ref[c, dy * 192 : dy * 192 + 128, :] = value[dy * half : (dy + 1) * half].T
            pair = value[3 * half : 4 * half].T
            kernel_ref[c, 128:192, :] = pair[:half]
            kernel_ref[c, 320:384, :] = pair[half:]
            kernel_ref[c, 512:576, :] = value[4 * half : 5 * half].T[:half]
            bias_rows.append(half_swap(value[4 * half : 4 * half + 1])[:, :half])
        bias_ref[...] = jnp.concatenate(bias_rows, axis=0)

    kernel_sum, bias_sum = call(
        final_body,
        [sds((2, TAPS * channels, channels), F32), sds((2, channels), F32)],
        [],
        [total, other],
        final=(0, 1),
    )
    return (
        noise[None, None],
        kernel_sum.reshape(1, 2, 3, 3, channels, channels),
        bias_sum[None],
    )


def solution(mesh):
    strips = mesh.shape["strip"]
    sections = mesh.shape["section"]
    return jax.shard_map(
        functools.partial(local, strips, sections),
        mesh=mesh,
        in_specs=(
            P(None, "strip", None),
            P("section", None, "strip", None),
            P("section", None, None, None, None, None),
            P("section", None, None),
        ),
        out_specs=(
            P("section", None, "strip", None),
            P("section", None, None, None, None, None),
            P("section", None, None),
        ),
        check_vma=False,
    )
```

```python
import functools
import math

import jax
import jax.numpy as jnp
import numpy as np
from jax import lax
from jax.experimental import pallas as pl
from jax.experimental.pallas import tpu as pltpu
from jax.sharding import PartitionSpec as P

LEAK = 0.05
LANES = 128
F32 = jnp.float32
BF16 = jnp.bfloat16
TAPS = 9
VMEM_BYTES = 24 * 1024 * 1024


def up_to(value, step):
    return -(-value // step) * step


class Level:
    def __init__(self, level, rows, cols):
        self.level = level
        self.rows = rows * 3**level // 4**level
        self.cols = cols * 3**level // 4**level
        self.pairs = -(-self.cols // 2)
        self.odd_pairs = -(-(self.cols + 1) // 2)

    def margin(self, error):
        self.error = error
        self.x_margin = error + 2
        self.x_rows = self.rows + 2 * (error + 2)
        self.hidden_rows = up_to(self.rows + 2 * (error + 1) + 2, 8) - 2
        self.out_rows = up_to(self.rows + 2 * error + 2, 8) - 2
        self.in_rows = up_to(self.rows + 2 * (error - 1) + 2, 8) - 2
        self.back_rows = up_to(self.rows + 2 * (error - 2) + 2, 8) - 2
        self.own_rows = up_to(self.rows, 16)
        self.alloc = up_to(max(self.hidden_rows + 2, self.x_margin + self.own_rows + 2), 8) + 8


def levels_of(rows, cols, count):
    levels = [Level(s, rows, cols) for s in range(count)]
    levels[-1].margin(2)
    for s in range(count - 2, -1, -1):
        fine, coarse = levels[s], levels[s + 1]
        first = -coarse.error
        last = coarse.rows + coarse.error - 1
        low = 4 * (first // 3) + (-1, 1, 2)[first % 3]
        high = 4 * (last // 3) + (1, 2, 4)[last % 3]
        fine.margin(max(-low, high - fine.rows + 1) + 2)
        fine.k_first = first // 3
        fine.k_count = up_to(last // 3 - fine.k_first + 1, 8)
        fine.up_shift = -3 * fine.k_first - coarse.error
        start = fine.error - 2 + 4 * fine.k_first - 1
        fine.gu_row = max(0, -start)
        fine.gu_start = start + fine.gu_row
        assert fine.rows % 4 == 0
    return levels


def column_weights(fine, coarse):
    matrix = np.zeros((coarse, fine), np.float32)
    for x in range(fine):
        num = max((2 * x + 1) * coarse - fine, 0)
        low = num // (2 * fine)
        frac = np.float32(num - 2 * fine * low) / np.float32(2 * fine)
        matrix[low, x] += np.float32(1.0) - frac
        matrix[min(low + 1, coarse - 1), x] += frac
    return matrix


def lane_index(shape):
    return lax.broadcasted_iota(jnp.int32, shape, len(shape) - 1)


def half_swap(value):
    return pltpu.roll(value, LANES // 2, value.ndim - 1)


def twice(bias):
    return jnp.concatenate([bias, bias], axis=1)


def rounded(value):
    return value.astype(BF16).astype(F32)


def image_mask(level, base, count, strip, strips):
    row = lax.broadcasted_iota(jnp.int32, (1, count, LANES), 1) + base
    low = jnp.where(strip == 0, 0, -(10**6))
    high = jnp.where(strip == strips - 1, level.rows, 10**6)
    return (row >= low) & (row < high)


def odd_column_mask(level, first, count, mask):
    if first > 0 and 2 * (first + count - 1) < level.cols:
        return mask
    shape = (count, mask.shape[1], LANES)
    half = lax.broadcasted_iota(jnp.int32, shape, 2) // (LANES // 2)
    col = 2 * (first + lax.broadcasted_iota(jnp.int32, shape, 0)) - 1 + half
    return mask & (col >= 0) & (col < level.cols)


def conv(source, kernel, count, segments, chunk, emit):
    total = sum(rows for _, rows in segments)
    for first in range(0, count, chunk):
        size = min(chunk, count - first)
        blocks = [source[first : first + size + 1, a : a + rows, :] for a, rows in segments]
        block = blocks[0] if len(blocks) == 1 else jnp.concatenate(blocks, axis=1)
        left = block[:size].reshape(size * total, LANES).astype(BF16)
        right = block[1:].reshape(size * total, LANES).astype(BF16)
        by_row = jnp.dot(jnp.concatenate([left, right], axis=1), kernel[...], preferred_element_type=F32)
        result = by_row[:, :LANES]
        for dy in (1, 2):
            part = by_row[:, dy * LANES : (dy + 1) * LANES]
            result = result + pltpu.roll(part, size * total - dy, 0)
        result = result.reshape(size, total, LANES)
        at = 0
        for a, rows in segments:
            emit(first, size, a, rows - 2, result[:, at : at + rows - 2])
            at += rows


def kernel_terms(source, error, count, source_row, error_row, level):
    rows = level.own_rows
    err = error[0:count, error_row : error_row + rows, :]
    if rows != level.rows:
        row = lax.broadcasted_iota(jnp.int32, (1, rows, LANES), 1)
        err = jnp.where(row < level.rows, err, 0.0)
    total = jnp.sum(err, axis=(0, 1)).reshape(1, LANES)
    parts = []
    for dy in range(3):
        block = source[0 : count + 1, source_row + dy : source_row + dy + rows, :].astype(BF16)
        parts.append(block[:count].reshape(count * rows, LANES))
        parts.append(block[1:].reshape(count * rows, LANES))
    stacked = jnp.concatenate(parts, axis=1)
    product = lax.dot_general(
        err.astype(BF16).reshape(count * rows, LANES),
        stacked,
        (((0,), (0,)), ((), ())),
        preferred_element_type=F32,
    )
    return product, total


def pack_kernel_terms(out_ref, product, total, scale):
    half = LANES // 2
    low = lane_index((1, LANES)) < half
    thirds = []
    for dy in range(3):
        first = product[:, 2 * dy * LANES : (2 * dy + 1) * LANES]
        then = product[:, (2 * dy + 1) * LANES : (2 * dy + 2) * LANES]
        moved = half_swap(then[half:])
        out_ref[dy * half : (dy + 1) * half, :] = (
            first[:half] + jnp.where(low, half_swap(first[half:]), moved)
        ) * scale
        thirds.append((then[:half] + moved) * scale)
    bias = (total + half_swap(total)) * scale
    out_ref[3 * half : 4 * half, :] = jnp.where(low, thirds[0], half_swap(thirds[1]))
    at = 4 * half + half // 2
    out_ref[4 * half : at, :] = jnp.where(low, thirds[2][: half // 2], half_swap(thirds[2][half // 2 :]))
    out_ref[at : at + 16, :] = jnp.broadcast_to(bias, (16, LANES))


def toeplitz(taps):
    half = LANES // 2
    zero = jnp.zeros((half, half), F32)
    columns = []
    for dy in range(3):
        rows = []
        for k in range(4):
            left = taps[dy * 3 + k] if k < 3 else zero
            right = taps[dy * 3 + k - 1] if k > 0 else zero
            rows.append(jnp.concatenate([left, right], axis=1))
        columns.append(jnp.concatenate(rows, axis=0))
    return jnp.concatenate(columns, axis=1)


def toeplitz_back(taps):
    half = LANES // 2
    zero = jnp.zeros((half, half), F32)
    by_row = []
    for dy in range(3):
        columns = []
        for k in range(4):
            top = taps[(2 - dy) * 3 + 2 - k] if k < 3 else zero
            bottom = taps[(2 - dy) * 3 + 3 - k] if k > 0 else zero
            columns.append(jnp.concatenate([top, bottom], axis=0))
        by_row.append(jnp.concatenate([jnp.concatenate(columns[i : i + 2], axis=1).T for i in (0, 2)], axis=0))
    return jnp.concatenate(by_row, axis=1)


def zero_tail(ref, level, rows):
    if level.alloc > rows:
        ref[0 : level.pairs + 1, rows : level.alloc, :] = jnp.zeros((level.pairs + 1, level.alloc - rows, LANES), F32)
    if level.odd_pairs < level.pairs + 1:
        ref[level.odd_pairs : level.pairs + 1, 0 : level.alloc, :] = jnp.zeros(
            (level.pairs + 1 - level.odd_pairs, level.alloc, LANES), F32
        )


def zero_edges(ref, level):
    zero = jnp.zeros((level.alloc, LANES), F32)
    ref[0, 0 : level.alloc, :] = zero
    ref[level.pairs + 1, 0 : level.alloc, :] = zero


def slope(value):
    return LEAK + (1.0 - LEAK) * (0.5 + 0.5 * jnp.tanh(0.5 * value))


def forward(level, xb, hb, kernels, bias, d_in, d_out, place, chunk, hidden_parts=None, out_parts=None):
    strip, strips = place
    bias_in, bias_out = bias[0:1], bias[1:2]

    def first_layer(first, size, a, rows, value):
        mask = image_mask(level, a - (level.error + 1), rows, strip, strips)
        pre = value + bias_in
        small = jnp.exp(-jnp.abs(pre))
        soft = jnp.maximum(pre, 0.0) + jnp.log(1.0 + small)
        act = LEAK * pre + (1.0 - LEAK) * soft
        keep = odd_column_mask(level, first, size, mask)
        hb[first : first + size, a : a + rows, :] = jnp.where(keep, rounded(act), 0.0)
        d_in[first : first + size, a : a + rows, :] = slope(pre)

    conv(xb, kernels[0], level.odd_pairs, hidden_parts or [(0, level.hidden_rows + 2)], chunk, first_layer)

    def second_layer(first, size, a, rows, value):
        d_out(first, size, a, rows, slope(value + bias_out))

    conv(hb, kernels[1], level.pairs, out_parts or [(0, level.out_rows + 2)], chunk, second_layer)


def backward(level, eo, ei, kernels, d_in, grad, grad_row, bi, gu, place, chunk, in_parts=None, back_parts=None):
    strip, strips = place

    def inner(first, size, a, rows, value):
        mask = image_mask(level, a - (level.error - 1), rows, strip, strips)
        keep = odd_column_mask(level, first, size, mask)
        part = d_in[first : first + size, 2 + a : 2 + a + rows, :]
        ei[first : first + size, a : a + rows, :] = jnp.where(keep, rounded(value * part), 0.0)

    conv(eo, kernels[1], level.odd_pairs, in_parts or [(0, level.in_rows + 2)], chunk, inner)

    def outer(first, size, a, rows, value):
        if bi is not None:
            bi[first : first + size, a : a + rows, :] = value
        if gu is not None:
            mask = image_mask(level, a - (level.error - 2), rows, strip, strips)
            part = grad[first : first + size, grad_row + 2 + a : grad_row + 2 + a + rows, :]
            at = level.gu_row + a
            gu[first : first + size, at : at + rows, :] = jnp.where(mask, rounded(part + value), 0.0)

    conv(ei, kernels[0], level.pairs, back_parts or [(0, level.back_rows + 2)], chunk, outer)


def write_noise(level, bi, noise):
    total_rows = noise.shape[0]
    row = lax.broadcasted_iota(jnp.int32, (level.own_rows, LANES), 0)
    lane = lane_index((level.own_rows, LANES))
    for p in range(noise.shape[1] // LANES):
        at = slice(p * LANES, (p + 1) * LANES)
        if p < level.pairs:
            part = bi[p, level.error - 2 : level.error - 2 + level.own_rows, :]
            if level.own_rows != level.rows:
                part = jnp.where(row < level.rows, part, 0.0)
            if 2 * p + 1 >= level.cols:
                part = jnp.where(lane < LANES // 2, part, 0.0)
            noise[0 : level.own_rows, at] = part.astype(BF16)
            if level.own_rows < total_rows:
                noise[level.own_rows : total_rows, at] = jnp.zeros((total_rows - level.own_rows, LANES), BF16)
        else:
            noise[:, at] = jnp.zeros((total_rows, LANES), BF16)


def coarsen(fine, coarse, gu, rc, ranges, spans, emit, place, edges=True):
    strip, strips = place
    for k, count in ranges:
        start = fine.gu_start + 4 * (k - fine.k_first)
        at = 3 * (k - fine.k_first)
        for p in range(fine.pairs):
            f = [gu[p, pl.ds(start + a, count, stride=4), :] for a in range(6)]
            rc[p, pl.ds(at, count, stride=3), :] = 0.125 * f[0] + 0.875 * f[1] + 0.375 * f[2]
            rc[p, pl.ds(at + 1, count, stride=3), :] = 0.625 * f[2] + 0.625 * f[3]
            rc[p, pl.ds(at + 2, count, stride=3), :] = 0.375 * f[3] + 0.875 * f[4] + 0.125 * f[5]
    if edges:
        top = -3 * fine.k_first
        low = top + coarse.rows - 1
        on_top = jnp.where(strip == 0, 1.0, 0.0).astype(F32)
        on_low = jnp.where(strip == strips - 1, 1.0, 0.0).astype(F32)
        every = slice(0, fine.pairs)
        rc[every, top : top + 1, :] = rc[every, top : top + 1, :] + on_top * rc[every, top - 1 : top, :]
        rc[every, low : low + 1, :] = rc[every, low : low + 1, :] + on_low * rc[every, low + 1 : low + 2, :]
    matrix = column_weights(fine.cols, coarse.cols)
    matrix = np.pad(matrix, ((0, 2 * coarse.pairs - coarse.cols), (0, 2 * fine.pairs - fine.cols)))
    lane = lane_index((1, LANES))

    def weights(low_lanes, high_lanes):
        return jnp.where(lane < LANES // 2, np.float32(low_lanes), np.float32(high_lanes))

    for span, (row, rows) in enumerate(spans):
        at = row - 3 * fine.k_first
        for m in range(coarse.pairs):
            total = None
            for q in range(fine.pairs):
                same = (matrix[2 * m, 2 * q], matrix[2 * m + 1, 2 * q + 1])
                cross = (matrix[2 * m, 2 * q + 1], matrix[2 * m + 1, 2 * q])
                value = rc[q, at : at + rows, :] if any(same) or any(cross) else None
                for pair, moved in ((same, False), (cross, True)):
                    if any(pair):
                        term = (half_swap(value) if moved else value) * weights(*pair)
                        total = term if total is None else total + term
            emit(m, span, total)


def own_input(level, xb, act):
    zero_edges(xb, level)
    lane = lane_index((1, LANES))
    for p in range(level.pairs):
        own = act[0 : level.own_rows, p * LANES : (p + 1) * LANES].astype(F32)
        if 2 * p + 1 >= level.cols:
            own = jnp.where(lane < LANES // 2, own, 0.0)
        xb[p + 1, level.x_margin : level.x_margin + level.own_rows, :] = own


def zero_after(level, xb):
    end = level.x_rows
    if end < level.alloc:
        xb[1 : level.pairs + 1, end : level.alloc, :] = jnp.zeros((level.pairs, level.alloc - end, LANES), F32)


def halo_input(level, xb, top, low, tmp, payload_rows):
    margin = level.x_margin
    end = margin + level.rows
    lane = lane_index((1, LANES))
    for p in range(level.pairs):
        at = slice(p * LANES, (p + 1) * LANES)
        upper, lower = top(at), low(at)
        if 2 * p + 1 >= level.cols:
            upper, lower = (jnp.where(lane < LANES // 2, v, 0.0) for v in (upper, lower))
        tmp[0, 0 : upper.shape[0], :] = upper
        tmp[1, 0 : lower.shape[0], :] = lower
        xb[p + 1, 0:margin, :] = tmp[0, payload_rows - margin : payload_rows, :]
        xb[p + 1, end : end + margin, :] = tmp[1, 0:margin, :]
    zero_after(level, xb)


def shipped_input(level, xb, own):
    zero_edges(xb, level)
    for p in range(level.pairs):
        xb[p + 1, 0 : level.x_rows, :] = own[p * level.x_rows : (p + 1) * level.x_rows, :]
    zero_after(level, xb)


def call(body, out_shape, scratch, operands, final=(), outside=(), aliases=None, flops=1000):
    operands = [
        pltpu.with_memory_space_constraint(x, pltpu.HBM if i in outside else pltpu.VMEM)
        for i, x in enumerate(operands)
    ]
    out_shape = [s if i in final else pltpu.VMEM(s.shape, s.dtype) for i, s in enumerate(out_shape)]
    return pl.pallas_call(
        body,
        out_shape=out_shape,
        in_specs=[pl.BlockSpec(memory_space=pltpu.VMEM)] * len(operands),
        out_specs=[pl.BlockSpec(memory_space=pltpu.VMEM)] * len(out_shape),
        scratch_shapes=scratch,
        input_output_aliases=aliases or {},
        compiler_params=pltpu.CompilerParams(vmem_limit_bytes=VMEM_BYTES),
        cost_estimate=pl.CostEstimate(flops=flops, bytes_accessed=1000, transcendentals=0),
    )(*operands)


def sds(shape, dtype):
    return jax.ShapeDtypeStruct(shape, dtype)


def field(level, extra):
    return sds((level.pairs + extra, level.alloc, LANES), F32)


def buffer(level, extra):
    return pltpu.VMEM((level.pairs + extra, level.alloc, LANES), F32)


def local(strips, sections, cotangent, activations, weights, biases):
    row_count, flat_width = activations.shape[2:]
    channels = weights.shape[-1]
    half = channels // 2
    cols = flat_width // channels
    assert 2 * channels == LANES and sections == 4 and cotangent.shape[0] == 1
    levels = levels_of(row_count, cols, sections)
    fine, second, third, last = levels
    x_margin, g_margin = fine.x_margin, fine.error
    payload = up_to(x_margin + g_margin, 16)
    pair_count = fine.pairs
    chunk = 4

    def place():
        return lax.axis_index("strip"), strips

    def is_odd():
        return lax.rem(lax.axis_index("strip"), 2) == 1

    packed_rows = TAPS * channels
    own_flat = up_to(third.pairs * third.x_rows, 16)
    ship_rows = own_flat + packed_rows + 16

    def halo_body(
        act_hbm, cot_hbm, bias_hbm, act_ref, cot_ref, both_ref, swap_ref, cross_ref, xs, cs, ts
    ):
        both_ref[0:2, :] = twice(bias_hbm[...])
        section = lax.axis_index("section")
        odd = is_odd()

        live = jnp.int32(fine.rows)
        for level in levels[1:]:
            live = jnp.where(section == level.level, level.rows, live)
        for p in range(pair_count):
            at = slice(p * LANES, (p + 1) * LANES)
            act_ref[:, at] = act_hbm[:, at]
            cot_ref[:, at] = cot_hbm[:, at]
            xs[p, 0:row_count, :] = act_hbm[:, at].astype(F32)
            cs[p, 0:row_count, :] = cot_hbm[:, at].astype(F32)
            ts[0, p, 0:x_margin, :] = xs[p, 0:x_margin, :]
            ts[0, p, x_margin : x_margin + g_margin, :] = cs[p, 0:g_margin, :]
            ts[1, p, 0:x_margin, :] = xs[p, pl.ds(live - x_margin, x_margin), :]
            ts[1, p, x_margin : x_margin + g_margin, :] = cs[p, row_count - g_margin : row_count, :]
            upper = ts[0, p, 0:payload, :]
            lower = ts[1, p, 0:payload, :]
            swap_ref[:, at] = jnp.where(odd, upper, lower).astype(BF16)
            cross_ref[:, at] = jnp.where(odd, lower, upper).astype(BF16)

    strip_shape = sds((row_count, flat_width), BF16)
    halo_shape = sds((payload, flat_width), BF16)
    taps = weights.reshape(2 * TAPS, channels, channels)
    act, cot, bias_own, to_swap, to_cross = call(
        halo_body,
        [
            strip_shape, strip_shape, sds((8, LANES), F32), halo_shape, halo_shape,
        ],
        [
            pltpu.VMEM((pair_count, row_count + 16, LANES), F32),
            pltpu.VMEM((pair_count, row_count + 16, LANES), F32),
            pltpu.VMEM((2, pair_count, payload + 16, LANES), F32),
        ],
        [activations[0, 0], cotangent[0], biases[0]],
        outside=(0, 1, 2),
    )
    swap_pairs = [(i, i ^ 1) for i in range(strips)]
    cross_pairs = [(i, i + 1) for i in range(1, strips - 1, 2)] + [(i + 1, i) for i in range(1, strips - 1, 2)]
    from_cross = lax.ppermute(to_cross, "strip", cross_pairs)
    from_swap = lax.ppermute(to_swap, "strip", swap_pairs)


    def expand(tap_list, forward_ref, back_ref):
        for c in range(2):
            chosen = tap_list[c * TAPS : (c + 1) * TAPS]
            forward_ref[c, :, :] = toeplitz(chosen).astype(BF16)
            back_ref[c, :, :] = toeplitz_back(chosen).astype(BF16)

    def matrix_body(taps_ref, bias_ref, forward_ref, back_ref):
        expand([taps_ref[t].astype(F32) for t in range(2 * TAPS)], forward_ref, back_ref)

    matrix_shape = sds((2, 2 * LANES, 3 * LANES), BF16)
    fwd_own, back_own = call(matrix_body, [matrix_shape, matrix_shape], [], [taps, bias_own])

    def across(value, pairs):
        return lax.ppermute(value, "section", pairs)

    inside = [[(17, row_count)], [(16, row_count)]]
    ends = [[(0, 24), (row_count + 10, 24)], [(0, 24), (row_count + 8, 24)]]
    assert fine.error == 15 and fine.x_margin == 17 and row_count >= 32
    g_in = (4, second.rows - 8)
    g_end = second.error + g_in[0]
    in_rows = up_to(second.pairs * g_in[1], 16)
    rim_rows = up_to(second.pairs * 2 * g_end, 16)

    def error_of(level, gb, eo, mask_place):
        def error(first, size, a, rows, value):
            mask = image_mask(level, a - level.error, rows, *mask_place)
            part = gb[first : first + size, a : a + rows, :]
            eo[first + 1 : first + 1 + size, a : a + rows, :] = jnp.where(mask, rounded(part * value), 0.0)

        return error

    def inside_body(
        act_ref, cot_ref, fwd_ref, back_ref, bias_ref, hop_ref, xb, hb, db, gb, eo, ei, bi, gu, rc, flat,
    ):
        section = lax.axis_index("section")

        @pl.when(section == 0)
        def _():
            level = fine
            own_input(level, xb, act_ref)
            zero_after(level, xb)
            zero_edges(eo, level)
            zero_tail(hb, level, level.hidden_rows)
            zero_tail(ei, level, level.alloc)
            for p in range(level.pairs):
                gb[p, g_margin : g_margin + row_count, :] = cot_ref[:, p * LANES : (p + 1) * LANES].astype(F32)
            forward(
                level, xb, hb, [fwd_ref.at[0], fwd_ref.at[1]], bias_ref, db, error_of(level, gb, eo, place()),
                place(), chunk, *inside,
            )
            backward(
                level, eo, ei, [back_ref.at[0], back_ref.at[1]], db, gb, 0, bi, gu, place(), chunk,
                inside[1], inside[1],
            )

            def emit(m, span, rows):
                flat[m * g_in[1] : (m + 1) * g_in[1], :] = rows

            coarsen(fine, second, gu, rc, [(0, 16)], [g_in], emit, place(), edges=False)
            hop_ref[...] = flat[0:in_rows, :].astype(BF16)

    coarse_buffer = pltpu.VMEM((fine.pairs, 3 * fine.k_count + 8, LANES), F32)
    state_shapes = [
        field(fine, 2), field(fine, 1), field(fine, 1), field(fine, 0),
        field(fine, 2), field(fine, 1), field(fine, 0), field(fine, 0),
    ]
    hop_in, *state = call(
        inside_body,
        [sds((in_rows, LANES), BF16), *state_shapes],
        [coarse_buffer, pltpu.VMEM((in_rows + 16, LANES), F32)],
        [act, cot, fwd_own, back_own, bias_own],
    )
    in_near = across(hop_in, [(0, 1), (1, 3), (3, 2), (2, 0)])

    def halo_readers(swap_ref, cross_ref):
        odd = is_odd()

        def top(at):
            return jnp.where(odd, swap_ref[:, at].astype(F32), cross_ref[:, at].astype(F32))

        def low(at):
            return jnp.where(odd, cross_ref[:, at].astype(F32), swap_ref[:, at].astype(F32))

        return top, low

    def rim_body(
        swap_ref, cross_ref, fwd_ref, back_ref, bias_ref, xi, hi, di, gi, oi, ii, bii, ui,
        rim_ref, xb, hb, db, gb, eo, ei, bi, gu, rc, flat, tmp,
    ):
        section = lax.axis_index("section")
        top, low = halo_readers(swap_ref, cross_ref)

        @pl.when(section == 0)
        def _():
            level = fine
            end = x_margin + row_count
            for p in range(level.pairs):
                at = slice(p * LANES, (p + 1) * LANES)
                tmp[0, 0:payload, :] = top(at)
                tmp[1, 0:payload, :] = low(at)
                xb[p + 1, 0:x_margin, :] = tmp[0, 0:x_margin, :]
                xb[p + 1, end : end + x_margin, :] = tmp[1, 0:x_margin, :]
                gb[p, 0:g_margin, :] = tmp[0, x_margin : x_margin + g_margin, :]
                gb[p, g_margin + row_count : 2 * g_margin + row_count, :] = tmp[
                    1, x_margin : x_margin + g_margin, :
                ]
            forward(
                level, xb, hb, [fwd_ref.at[0], fwd_ref.at[1]], bias_ref, db, error_of(level, gb, eo, place()),
                place(), chunk, ends[0], ends[0],
            )
            backward(
                level, eo, ei, [back_ref.at[0], back_ref.at[1]], db, gb, 0, bi, gu, place(), chunk, ends[1], ends[1]
            )

            def emit(m, span, rows):
                at = m * 2 * g_end + span * g_end
                flat[at : at + g_end, :] = rows[0:g_end]

            last_k = (second.rows + second.error) // 3
            coarsen(
                fine, second, gu, rc,
                [(fine.k_first, 8), (last_k - 7, 8)],
                [(-second.error, up_to(g_end, 8)), (g_in[0] + g_in[1], up_to(g_end, 8))],
                emit, place(),
            )
            rim_ref[...] = flat[0:rim_rows, :].astype(BF16)

    tmp_buffer = pltpu.VMEM((2, payload + 16, LANES), F32)
    rim, *state = call(
        rim_body,
        [sds((rim_rows, LANES), BF16), *state_shapes],
        [coarse_buffer, pltpu.VMEM((rim_rows + 32, LANES), F32), tmp_buffer],
        [from_swap, from_cross, fwd_own, back_own, bias_own, *state],
        aliases={5 + i: 1 + i for i in range(len(state_shapes))},
        flops=2 * 10**9,
    )
    rim_near = across(rim, [(0, 1), (1, 3), (3, 2), (2, 0)])

    def ship_body(act_ref, swap_ref, cross_ref, taps_ref, both_ref, rim_ref, ship_ref, tmp, flat, bias_tmp):
        top, low = halo_readers(swap_ref, cross_ref)

        @pl.when(lax.axis_index("section") == 2)
        def _():
            level = third
            margin = level.x_margin
            for p in range(level.pairs):
                at = slice(p * LANES, (p + 1) * LANES)
                tmp[0, 0:payload, :] = top(at)
                tmp[1, 0:payload, :] = low(at)
                to = p * level.x_rows
                end = to + margin + level.rows
                flat[to : to + margin, :] = tmp[0, x_margin - margin : x_margin, :]
                flat[to + margin : to + margin + level.own_rows, :] = act_ref[0 : level.own_rows, at].astype(F32)
                flat[end : end + margin, :] = tmp[1, 0:margin, :]
            ship_ref[0:own_flat, :] = flat[0:own_flat, :].astype(BF16)
            for t in range(2 * TAPS):
                at = own_flat + t * half
                value = taps_ref[t].astype(F32)
                ship_ref[at : at + half, :] = jnp.concatenate([value[:half], value[half:]], axis=1).astype(BF16)
            rest = both_ref[0:2, :]
            for term in range(3):
                part = rounded(rest)
                bias_tmp[2 * term : 2 * term + 2, :] = part
                rest = rest - part
            bias_tmp[6:16, :] = jnp.zeros((10, LANES), F32)
            ship_ref[own_flat + packed_rows : ship_rows, :] = bias_tmp[0:16, :].astype(BF16)

    (ship,) = call(
        ship_body,
        [sds((ship_rows, LANES), BF16)],
        [tmp_buffer, pltpu.VMEM((own_flat + 32, LANES), F32), pltpu.VMEM((32, LANES), F32)],
        [act, from_swap, from_cross, taps, bias_own, rim],
    )
    shipped = across(ship, [(2, 3)])

    grad_rows = 4 * channels + half + 16

    def gradients(level, source, hidden, err_in, err_out, rows_at, pair_out):
        scale = np.float32(1.0 / math.sqrt(strips * level.rows * level.cols))
        first = kernel_terms(source, err_in, level.odd_pairs, rows_at[2], rows_at[0], level)
        pack_kernel_terms(pair_out.at[0], *first, scale)
        then = kernel_terms(hidden, err_out, level.pairs, rows_at[3], rows_at[1], level)
        pack_kernel_terms(pair_out.at[1], *then, scale)

    def finish(level, source, hidden, ei, eo, pair_out):
        at = (level.error - 1, level.error, level.error + 1, level.error)
        gradients(level, source, hidden, ei, eo.at[1 : 1 + level.pairs], at, pair_out)

    def store_in(level, d_out):
        def store(first, size, a, rows, value):
            d_out[first : first + size, a : a + rows, :] = value

        return store

    def beside_body(
        act_ref, swap_ref, cross_ref, fwd_ref, bias_ref, x0, h0, o0, i0,
        din_ref, dout_ref, hid_ref, x_ref, pair_ref, tmp,
    ):
        section = lax.axis_index("section")
        top, low = halo_readers(swap_ref, cross_ref)

        @pl.when(section == 0)
        def _():
            finish(fine, x0, h0, i0, o0, pair_ref)

        for level in levels[1:]:

            @pl.when(section == level.level)
            def _(level=level):
                own_input(level, x_ref, act_ref)
                halo_input(level, x_ref, top, low, tmp, x_margin)
                zero_tail(hid_ref, level, level.hidden_rows)
                forward(
                    level, x_ref, hid_ref, [fwd_ref.at[0], fwd_ref.at[1]], bias_ref, din_ref,
                    store_in(level, dout_ref), place(), chunk,
                )

    pair_shape = sds((2, grad_rows, LANES), F32)
    din_own, dout_own, hid_own, x_own, pair_first = call(
        beside_body,
        [field(second, 1), field(second, 0), field(second, 1), field(second, 2), pair_shape],
        [tmp_buffer],
        [act, from_swap, from_cross, fwd_own, bias_own, state[0], state[1], state[4], state[5]],
    )

    def step(level, gb, grad_row, d_in, d_out, back, eo, ei, bi, gu):
        mask = image_mask(level, -level.error, level.out_rows, *place())
        zero_edges(eo, level)
        zero_tail(ei, level, level.alloc)
        for p in range(level.pairs):
            part = gb[p, grad_row : grad_row + level.out_rows, :] * d_out[p, 0 : level.out_rows, :]
            eo[p + 1, 0 : level.out_rows, :] = jnp.where(mask[0], rounded(part), 0.0)
        backward(level, eo, ei, [back.at[0], back.at[1]], d_in, gb, grad_row, bi, gu, place(), chunk)

    third_rows = third.rows + 2 * third.error
    third_flat = up_to(third.pairs * third_rows, 16)

    def hand_down(upper, lower, gu, rc, gb):
        def emit(m, span, value):
            gb[m, 0 : 3 * upper.k_count, :] = rounded(value)

        coarsen(
            upper, lower, gu, rc, [(upper.k_first, upper.k_count)], [(3 * upper.k_first, 3 * upper.k_count)],
            emit, place(),
        )

    def second_error(gb, d_out, eo, first, rows):
        mask = image_mask(second, first - second.error, rows, *place())
        for p in range(second.pairs):
            part = gb[p, first : first + rows, :] * d_out[p, first : first + rows, :]
            eo[p + 1, first : first + rows, :] = jnp.where(mask[0], rounded(part), 0.0)

    def second_inside_body(in_ref, din_o, dout_o, back_o, eo, ei, bi, gu, gb, mid):
        @pl.when(lax.axis_index("section") == 1)
        def _():
            mid[...] = in_ref[...].astype(F32)
            for p in range(second.pairs):
                gb[p, g_end : g_end + g_in[1], :] = mid[p * g_in[1] : (p + 1) * g_in[1], :]
            zero_edges(eo, second)
            zero_tail(ei, second, second.alloc)
            second_error(gb, dout_o, eo, g_end, g_in[1])
            parts = [(g_end, g_in[1])]
            backward(second, eo, ei, [back_o.at[0], back_o.at[1]], din_o, gb, 0, bi, gu, place(), chunk, parts, parts)

    inside_shapes = [
        field(second, 2), field(second, 1), field(second, 0),
        sds((second.pairs, second.alloc + 8, LANES), F32), field(second, 0),
    ]
    inside_state = call(
        second_inside_body,
        inside_shapes,
        [pltpu.VMEM((in_rows, LANES), F32)],
        [in_near, din_own, dout_own, back_own],
    )

    def second_rim_body(
        rim_ref, din_o, dout_o, back_o, eo_i, ei_i, bi_i, gu_i, gb_i, third_ref, eo, ei, bi, gu, gb, rc, rims, flat
    ):
        @pl.when(lax.axis_index("section") == 1)
        def _():
            rims[...] = rim_ref[...].astype(F32)
            low = g_end + g_in[1]
            for p in range(second.pairs):
                at = p * 2 * g_end
                gb[p, 0:g_end, :] = rims[at : at + g_end, :]
                gb[p, low : low + g_end, :] = rims[at + g_end : at + 2 * g_end, :]
            second_error(gb, dout_o, eo, 0, g_end)
            second_error(gb, dout_o, eo, low, g_end)
            rows = up_to(g_end + 2, 8)
            in_parts = [(0, rows), (low + g_end - rows, rows)]
            back_parts = [(0, rows), (low + g_end - 2 - rows, rows)]
            backward(
                second, eo, ei, [back_o.at[0], back_o.at[1]], din_o, gb, 0, bi, gu, place(), chunk,
                in_parts, back_parts,
            )
            hand_down(second, third, gu, rc, gb)
            at = second.up_shift
            for p in range(third.pairs):
                flat[p * third_rows : (p + 1) * third_rows, :] = gb[p, at : at + third_rows, :]
            third_ref[...] = flat[0:third_flat, :].astype(BF16)

    coarse_tmp = pltpu.VMEM((second.pairs, 3 * second.k_count + 8, LANES), F32)
    third_grad, eo_own, ei_own, bi_own, *_ = call(
        second_rim_body,
        [sds((third_flat, LANES), BF16), *inside_shapes],
        [coarse_tmp, pltpu.VMEM((rim_rows, LANES), F32), pltpu.VMEM((third_flat + 16, LANES), F32)],
        [rim_near, din_own, dout_own, back_own, *inside_state],
        aliases={4 + i: 1 + i for i in range(len(inside_shapes))},
        flops=4 * 10**9,
    )
    third_to_last = across(third_grad, [(1, 3), (3, 2), (2, 0), (0, 1)])
    third_to_own = across(third_grad, [(1, 2)])

    def shipped_body(ship_ref, own_ref, x_o, hid_o, eo_o, ei_o, din_s, dout_s, back_s, pair_ref, fwd_s, xb, hb, own):
        @pl.when(lax.axis_index("section") == 1)
        def _():
            finish(second, x_o, hid_o, ei_o, eo_o, pair_ref)

        @pl.when(lax.axis_index("section") == 3)
        def _():
            level = third
            values = []
            for t in range(2 * TAPS):
                pack = ship_ref[own_flat + t * half : own_flat + (t + 1) * half, :].astype(F32)
                values.append(jnp.concatenate([pack[:, :channels], pack[:, channels:]], axis=0))
            expand(values, fwd_s, back_s)
            terms = ship_ref[own_flat + packed_rows : ship_rows, :].astype(F32)
            bias = terms[0:2] + terms[2:4] + terms[4:6]
            own[0:own_flat, :] = ship_ref[0:own_flat, :].astype(F32)
            shipped_input(level, xb, own)
            zero_tail(hb, level, level.hidden_rows)
            forward(level, xb, hb, [fwd_s.at[0], fwd_s.at[1]], bias, din_s, store_in(level, dout_s), place(), chunk)

    din_s, dout_s, back_s, pair_second = call(
        shipped_body,
        [field(third, 1), field(third, 0), matrix_shape, pair_shape],
        [
            pltpu.VMEM((2, 2 * LANES, 3 * LANES), BF16),
            buffer(third, 2),
            buffer(third, 1),
            pltpu.VMEM((own_flat + 16, LANES), F32),
        ],
        [shipped, third_to_own, x_own, hid_own, eo_own, ei_own],
    )

    def last_body(
        pair0, pair1, own_ref, last_ref, din_o, dout_o, hid_o, x_o, back_o, din_s, dout_s, back_s,
        keep_ref, send_ref, bi, pair_out, gb, eo, ei, gu, rc, flat,
    ):
        section = lax.axis_index("section")
        odd = is_odd()

        def take(source):
            flat[0:third_flat, :] = source[...].astype(F32)
            for p in range(third.pairs):
                gb[p, 0:third_rows, :] = flat[p * third_rows : (p + 1) * third_rows, :]

        @pl.when(section == 0)
        def _():
            pair_out[...] = pair0[...]

        @pl.when(section == 1)
        def _():
            pair_out[...] = pair1[...]

        @pl.when(section == 2)
        def _():
            take(own_ref)
            step(third, gb, 0, din_o, dout_o, back_o, eo, ei, bi, None)
            finish(third, x_o, hid_o, ei, eo, pair_out)

        @pl.when(section == 3)
        def _():
            take(last_ref)
            step(third, gb, 0, din_s, dout_s, back_s, eo, ei, None, gu)
            hand_down(third, last, gu, rc, gb)
            step(last, gb, third.up_shift, din_o, dout_o, back_o, eo, ei, bi, None)
            finish(last, x_o, hid_o, ei, eo, pair_out)

        first, then = pair_out[0], pair_out[1]
        keep_ref[...] = jnp.where(odd, then, first)
        send_ref[...] = jnp.where(odd, first, then)

    half_shape = sds((grad_rows, LANES), F32)
    keep, send, bi_last = call(
        last_body,
        [half_shape, half_shape, field(third, 0)],
        [
            pltpu.VMEM((2, grad_rows, LANES), F32),
            buffer(third, 0),
            buffer(third, 2),
            buffer(third, 1),
            buffer(fine, 0),
            coarse_tmp,
            pltpu.VMEM((third_flat + 16, LANES), F32),
        ],
        [
            pair_first, pair_second, third_to_own, third_to_last, din_own, dout_own, hid_own, x_own, back_own,
            din_s, dout_s, back_s,
        ],
    )

    total = keep + lax.ppermute(send, "strip", swap_pairs)
    step = 2
    while step < strips:
        mine = lax.reduce_precision(total, 8, 7)
        small = mine.astype(BF16)
        offsets = (step, 2 * step, 3 * step) if 2 * step < strips else (step,)
        got = [lax.ppermute(small, "strip", [(i, i ^ o) for i in range(strips)]).astype(F32) for o in offsets]
        total = mine + got[0]
        if len(got) == 3:
            total = total + (got[1] + got[2])
        step *= len(got) + 1
    other = lax.ppermute(total, "strip", swap_pairs)

    def noise_body(bi_f, bi_o, bi_l, noise_ref):
        section = lax.axis_index("section")

        for level, source in ((fine, bi_f), (second, bi_o), (third, bi_l), (last, bi_l)):

            @pl.when(section == level.level)
            def _(level=level, source=source):
                write_noise(level, source, noise_ref)

    (noise,) = call(noise_body, [strip_shape], [], [state[6], bi_own, bi_last], final=(0,))

    def final_body(mine_ref, other_ref, kernel_ref, bias_ref):
        odd = is_odd()
        half = channels
        bias_rows = []
        for c in range(2):
            if c == 0:
                value = jnp.where(odd, other_ref[...], mine_ref[...])
            else:
                value = jnp.where(odd, mine_ref[...], other_ref[...])
            for dy in range(3):
                kernel_ref[c, dy * 192 : dy * 192 + 128, :] = value[dy * half : (dy + 1) * half].T
            pair = value[3 * half : 4 * half].T
            kernel_ref[c, 128:192, :] = pair[:half]
            kernel_ref[c, 320:384, :] = pair[half:]
            at = 4 * half + half // 2
            pair = value[4 * half : at].T
            kernel_ref[c, 512:576, :] = jnp.concatenate([pair[:half], pair[half:]], axis=1)
            bias_rows.append(value[at : at + 1, :half])
        bias_ref[...] = jnp.concatenate(bias_rows, axis=0)

    kernel_sum, bias_sum = call(
        final_body,
        [sds((2, TAPS * channels, channels), F32), sds((2, channels), F32)],
        [],
        [total, other],
        final=(0, 1),
    )
    return (
        noise[None, None],
        kernel_sum.reshape(1, 2, 3, 3, channels, channels),
        bias_sum[None],
    )


def solution(mesh):
    strips = mesh.shape["strip"]
    sections = mesh.shape["section"]
    return jax.shard_map(
        functools.partial(local, strips, sections),
        mesh=mesh,
        in_specs=(
            P(None, "strip", None),
            P("section", None, "strip", None),
            P("section", None, None, None, None, None),
            P("section", None, None),
        ),
        out_specs=(
            P("section", None, "strip", None),
            P("section", None, None, None, None, None),
            P("section", None, None),
        ),
        check_vma=False,
    )
```

```python
import functools
import math

import jax
import jax.numpy as jnp
import numpy as np
from jax import lax
from jax.experimental import pallas as pl
from jax.experimental.pallas import tpu as pltpu
from jax.sharding import PartitionSpec as P

LEAK = 0.05
LANES = 128
F32 = jnp.float32
BF16 = jnp.bfloat16
TAPS = 9
VMEM_BYTES = 24 * 1024 * 1024


def up_to(value, step):
    return -(-value // step) * step


class Level:
    def __init__(self, level, rows, cols):
        self.level = level
        self.rows = rows * 3**level // 4**level
        self.cols = cols * 3**level // 4**level
        self.pairs = -(-self.cols // 2)
        self.odd_pairs = -(-(self.cols + 1) // 2)

    def margin(self, error):
        self.error = error
        self.x_margin = error + 2
        self.x_rows = self.rows + 2 * (error + 2)
        self.hidden_rows = up_to(self.rows + 2 * (error + 1) + 2, 8) - 2
        self.out_rows = up_to(self.rows + 2 * error + 2, 8) - 2
        self.in_rows = up_to(self.rows + 2 * (error - 1) + 2, 8) - 2
        self.back_rows = up_to(self.rows + 2 * (error - 2) + 2, 8) - 2
        self.own_rows = up_to(self.rows, 16)
        self.alloc = up_to(max(self.hidden_rows + 2, self.x_margin + self.own_rows + 2), 8) + 8


def levels_of(rows, cols, count):
    levels = [Level(s, rows, cols) for s in range(count)]
    levels[-1].margin(2)
    for s in range(count - 2, -1, -1):
        fine, coarse = levels[s], levels[s + 1]
        first = -coarse.error
        last = coarse.rows + coarse.error - 1
        low = 4 * (first // 3) + (-1, 1, 2)[first % 3]
        high = 4 * (last // 3) + (1, 2, 4)[last % 3]
        fine.margin(max(-low, high - fine.rows + 1) + 2)
        fine.k_first = first // 3
        fine.k_count = up_to(last // 3 - fine.k_first + 1, 8)
        fine.up_shift = -3 * fine.k_first - coarse.error
        start = fine.error - 2 + 4 * fine.k_first - 1
        fine.gu_row = max(0, -start)
        fine.gu_start = start + fine.gu_row
        assert fine.rows % 4 == 0
    return levels


def column_weights(fine, coarse):
    matrix = np.zeros((coarse, fine), np.float32)
    for x in range(fine):
        num = max((2 * x + 1) * coarse - fine, 0)
        low = num // (2 * fine)
        frac = np.float32(num - 2 * fine * low) / np.float32(2 * fine)
        matrix[low, x] += np.float32(1.0) - frac
        matrix[min(low + 1, coarse - 1), x] += frac
    return matrix


def lane_index(shape):
    return lax.broadcasted_iota(jnp.int32, shape, len(shape) - 1)


def half_swap(value):
    return pltpu.roll(value, LANES // 2, value.ndim - 1)


def twice(bias):
    return jnp.concatenate([bias, bias], axis=1)


def rounded(value):
    return value.astype(BF16).astype(F32)


def image_mask(level, base, count, strip, strips):
    row = lax.broadcasted_iota(jnp.int32, (1, count, LANES), 1) + base
    low = jnp.where(strip == 0, 0, -(10**6))
    high = jnp.where(strip == strips - 1, level.rows, 10**6)
    return (row >= low) & (row < high)


def odd_column_mask(level, first, count, mask):
    if first > 0 and 2 * (first + count - 1) < level.cols:
        return mask
    shape = (count, mask.shape[1], LANES)
    half = lax.broadcasted_iota(jnp.int32, shape, 2) // (LANES // 2)
    col = 2 * (first + lax.broadcasted_iota(jnp.int32, shape, 0)) - 1 + half
    return mask & (col >= 0) & (col < level.cols)


def conv(source, kernel, count, segments, chunk, emit):
    total = sum(rows for _, rows in segments)
    for first in range(0, count, chunk):
        size = min(chunk, count - first)
        blocks = [source[first : first + size + 1, a : a + rows, :] for a, rows in segments]
        block = blocks[0] if len(blocks) == 1 else jnp.concatenate(blocks, axis=1)
        left = block[:size].reshape(size * total, LANES).astype(BF16)
        right = block[1:].reshape(size * total, LANES).astype(BF16)
        by_row = jnp.dot(jnp.concatenate([left, right], axis=1), kernel[...], preferred_element_type=F32)
        result = by_row[:, :LANES]
        for dy in (1, 2):
            part = by_row[:, dy * LANES : (dy + 1) * LANES]
            result = result + pltpu.roll(part, size * total - dy, 0)
        result = result.reshape(size, total, LANES)
        at = 0
        for a, rows in segments:
            emit(first, size, a, rows - 2, result[:, at : at + rows - 2])
            at += rows


def kernel_terms(source, error, count, source_row, error_row, level):
    rows = level.own_rows
    err = error[0:count, error_row : error_row + rows, :]
    if rows != level.rows:
        row = lax.broadcasted_iota(jnp.int32, (1, rows, LANES), 1)
        err = jnp.where(row < level.rows, err, 0.0)
    total = jnp.sum(err, axis=(0, 1)).reshape(1, LANES)
    parts = []
    for dy in range(3):
        block = source[0 : count + 1, source_row + dy : source_row + dy + rows, :].astype(BF16)
        parts.append(block[:count].reshape(count * rows, LANES))
        parts.append(block[1:].reshape(count * rows, LANES))
    stacked = jnp.concatenate(parts, axis=1)
    product = lax.dot_general(
        err.astype(BF16).reshape(count * rows, LANES),
        stacked,
        (((0,), (0,)), ((), ())),
        preferred_element_type=F32,
    )
    return product, total


def pack_kernel_terms(out_ref, product, total, scale):
    half = LANES // 2
    low = lane_index((1, LANES)) < half
    thirds = []
    for dy in range(3):
        first = product[:, 2 * dy * LANES : (2 * dy + 1) * LANES]
        then = product[:, (2 * dy + 1) * LANES : (2 * dy + 2) * LANES]
        moved = half_swap(then[half:])
        out_ref[dy * half : (dy + 1) * half, :] = (
            first[:half] + jnp.where(low, half_swap(first[half:]), moved)
        ) * scale
        thirds.append((then[:half] + moved) * scale)
    bias = (total + half_swap(total)) * scale
    out_ref[3 * half : 4 * half, :] = jnp.where(low, thirds[0], half_swap(thirds[1]))
    at = 4 * half + half // 2
    out_ref[4 * half : at, :] = jnp.where(low, thirds[2][: half // 2], half_swap(thirds[2][half // 2 :]))
    out_ref[at : at + 16, :] = jnp.broadcast_to(bias, (16, LANES))


def toeplitz(taps):
    half = LANES // 2
    zero = jnp.zeros((half, half), F32)
    columns = []
    for dy in range(3):
        rows = []
        for k in range(4):
            left = taps[dy * 3 + k] if k < 3 else zero
            right = taps[dy * 3 + k - 1] if k > 0 else zero
            rows.append(jnp.concatenate([left, right], axis=1))
        columns.append(jnp.concatenate(rows, axis=0))
    return jnp.concatenate(columns, axis=1)


def toeplitz_back(taps):
    half = LANES // 2
    zero = jnp.zeros((half, half), F32)
    by_row = []
    for dy in range(3):
        columns = []
        for k in range(4):
            top = taps[(2 - dy) * 3 + 2 - k] if k < 3 else zero
            bottom = taps[(2 - dy) * 3 + 3 - k] if k > 0 else zero
            columns.append(jnp.concatenate([top, bottom], axis=0))
        by_row.append(jnp.concatenate([jnp.concatenate(columns[i : i + 2], axis=1).T for i in (0, 2)], axis=0))
    return jnp.concatenate(by_row, axis=1)


def zero_tail(ref, level, rows):
    if level.alloc > rows:
        ref[0 : level.pairs + 1, rows : level.alloc, :] = jnp.zeros((level.pairs + 1, level.alloc - rows, LANES), F32)
    if level.odd_pairs < level.pairs + 1:
        ref[level.odd_pairs : level.pairs + 1, 0 : level.alloc, :] = jnp.zeros(
            (level.pairs + 1 - level.odd_pairs, level.alloc, LANES), F32
        )


def zero_edges(ref, level):
    zero = jnp.zeros((level.alloc, LANES), F32)
    ref[0, 0 : level.alloc, :] = zero
    ref[level.pairs + 1, 0 : level.alloc, :] = zero


def slope(value):
    return LEAK + (1.0 - LEAK) * (0.5 + 0.5 * jnp.tanh(0.5 * value))


def forward(level, xb, hb, kernels, bias, d_in, d_out, place, chunk, hidden_parts=None, out_parts=None):
    strip, strips = place
    bias_in, bias_out = bias[0:1], bias[1:2]

    def first_layer(first, size, a, rows, value):
        mask = image_mask(level, a - (level.error + 1), rows, strip, strips)
        pre = value + bias_in
        small = jnp.exp(-jnp.abs(pre))
        soft = jnp.maximum(pre, 0.0) + jnp.log(1.0 + small)
        act = LEAK * pre + (1.0 - LEAK) * soft
        keep = odd_column_mask(level, first, size, mask)
        hb[first : first + size, a : a + rows, :] = jnp.where(keep, rounded(act), 0.0)
        d_in[first : first + size, a : a + rows, :] = slope(pre)

    conv(xb, kernels[0], level.odd_pairs, hidden_parts or [(0, level.hidden_rows + 2)], chunk, first_layer)

    def second_layer(first, size, a, rows, value):
        d_out(first, size, a, rows, slope(value + bias_out))

    conv(hb, kernels[1], level.pairs, out_parts or [(0, level.out_rows + 2)], chunk, second_layer)


def backward(level, eo, ei, kernels, d_in, grad, grad_row, bi, gu, place, chunk, in_parts=None, back_parts=None):
    strip, strips = place

    def inner(first, size, a, rows, value):
        mask = image_mask(level, a - (level.error - 1), rows, strip, strips)
        keep = odd_column_mask(level, first, size, mask)
        part = d_in[first : first + size, 2 + a : 2 + a + rows, :]
        ei[first : first + size, a : a + rows, :] = jnp.where(keep, rounded(value * part), 0.0)

    conv(eo, kernels[1], level.odd_pairs, in_parts or [(0, level.in_rows + 2)], chunk, inner)

    def outer(first, size, a, rows, value):
        if bi is not None:
            bi[first : first + size, a : a + rows, :] = value
        if gu is not None:
            mask = image_mask(level, a - (level.error - 2), rows, strip, strips)
            part = grad[first : first + size, grad_row + 2 + a : grad_row + 2 + a + rows, :]
            at = level.gu_row + a
            gu[first : first + size, at : at + rows, :] = jnp.where(mask, rounded(part + value), 0.0)

    conv(ei, kernels[0], level.pairs, back_parts or [(0, level.back_rows + 2)], chunk, outer)


def write_noise(level, bi, noise):
    total_rows = noise.shape[0]
    row = lax.broadcasted_iota(jnp.int32, (level.own_rows, LANES), 0)
    lane = lane_index((level.own_rows, LANES))
    for p in range(noise.shape[1] // LANES):
        at = slice(p * LANES, (p + 1) * LANES)
        if p < level.pairs:
            part = bi[p, level.error - 2 : level.error - 2 + level.own_rows, :]
            if level.own_rows != level.rows:
                part = jnp.where(row < level.rows, part, 0.0)
            if 2 * p + 1 >= level.cols:
                part = jnp.where(lane < LANES // 2, part, 0.0)
            noise[0 : level.own_rows, at] = part.astype(BF16)
            if level.own_rows < total_rows:
                noise[level.own_rows : total_rows, at] = jnp.zeros((total_rows - level.own_rows, LANES), BF16)
        else:
            noise[:, at] = jnp.zeros((total_rows, LANES), BF16)


def coarsen(fine, coarse, gu, rc, ranges, spans, emit, place, edges=True):
    strip, strips = place
    for k, count in ranges:
        start = fine.gu_start + 4 * (k - fine.k_first)
        at = 3 * (k - fine.k_first)
        for p in range(fine.pairs):
            f = [gu[p, pl.ds(start + a, count, stride=4), :] for a in range(6)]
            rc[p, pl.ds(at, count, stride=3), :] = 0.125 * f[0] + 0.875 * f[1] + 0.375 * f[2]
            rc[p, pl.ds(at + 1, count, stride=3), :] = 0.625 * f[2] + 0.625 * f[3]
            rc[p, pl.ds(at + 2, count, stride=3), :] = 0.375 * f[3] + 0.875 * f[4] + 0.125 * f[5]
    if edges:
        top = -3 * fine.k_first
        low = top + coarse.rows - 1
        on_top = jnp.where(strip == 0, 1.0, 0.0).astype(F32)
        on_low = jnp.where(strip == strips - 1, 1.0, 0.0).astype(F32)
        every = slice(0, fine.pairs)
        rc[every, top : top + 1, :] = rc[every, top : top + 1, :] + on_top * rc[every, top - 1 : top, :]
        rc[every, low : low + 1, :] = rc[every, low : low + 1, :] + on_low * rc[every, low + 1 : low + 2, :]
    matrix = column_weights(fine.cols, coarse.cols)
    matrix = np.pad(matrix, ((0, 2 * coarse.pairs - coarse.cols), (0, 2 * fine.pairs - fine.cols)))
    lane = lane_index((1, LANES))

    def weights(low_lanes, high_lanes):
        return jnp.where(lane < LANES // 2, np.float32(low_lanes), np.float32(high_lanes))

    for span, (row, rows) in enumerate(spans):
        at = row - 3 * fine.k_first
        for m in range(coarse.pairs):
            total = None
            for q in range(fine.pairs):
                same = (matrix[2 * m, 2 * q], matrix[2 * m + 1, 2 * q + 1])
                cross = (matrix[2 * m, 2 * q + 1], matrix[2 * m + 1, 2 * q])
                value = rc[q, at : at + rows, :] if any(same) or any(cross) else None
                for pair, moved in ((same, False), (cross, True)):
                    if any(pair):
                        term = (half_swap(value) if moved else value) * weights(*pair)
                        total = term if total is None else total + term
            emit(m, span, total)


def own_input(level, xb, act):
    zero_edges(xb, level)
    lane = lane_index((1, LANES))
    for p in range(level.pairs):
        own = act[0 : level.own_rows, p * LANES : (p + 1) * LANES].astype(F32)
        if 2 * p + 1 >= level.cols:
            own = jnp.where(lane < LANES // 2, own, 0.0)
        xb[p + 1, level.x_margin : level.x_margin + level.own_rows, :] = own


def zero_after(level, xb):
    end = level.x_rows
    if end < level.alloc:
        xb[1 : level.pairs + 1, end : level.alloc, :] = jnp.zeros((level.pairs, level.alloc - end, LANES), F32)


def halo_input(level, xb, top, low, tmp, payload_rows):
    margin = level.x_margin
    end = margin + level.rows
    lane = lane_index((1, LANES))
    for p in range(level.pairs):
        at = slice(p * LANES, (p + 1) * LANES)
        upper, lower = top(at), low(at)
        if 2 * p + 1 >= level.cols:
            upper, lower = (jnp.where(lane < LANES // 2, v, 0.0) for v in (upper, lower))
        tmp[0, 0 : upper.shape[0], :] = upper
        tmp[1, 0 : lower.shape[0], :] = lower
        xb[p + 1, 0:margin, :] = tmp[0, payload_rows - margin : payload_rows, :]
        xb[p + 1, end : end + margin, :] = tmp[1, 0:margin, :]
    zero_after(level, xb)


def shipped_input(level, xb, own):
    zero_edges(xb, level)
    for p in range(level.pairs):
        xb[p + 1, 0 : level.x_rows, :] = own[p * level.x_rows : (p + 1) * level.x_rows, :]
    zero_after(level, xb)


def call(body, out_shape, scratch, operands, final=(), outside=(), aliases=None, flops=1000):
    operands = [
        pltpu.with_memory_space_constraint(x, pltpu.HBM if i in outside else pltpu.VMEM)
        for i, x in enumerate(operands)
    ]
    out_shape = [s if i in final else pltpu.VMEM(s.shape, s.dtype) for i, s in enumerate(out_shape)]
    return pl.pallas_call(
        body,
        out_shape=out_shape,
        in_specs=[pl.BlockSpec(memory_space=pltpu.VMEM)] * len(operands),
        out_specs=[pl.BlockSpec(memory_space=pltpu.VMEM)] * len(out_shape),
        scratch_shapes=scratch,
        input_output_aliases=aliases or {},
        compiler_params=pltpu.CompilerParams(vmem_limit_bytes=VMEM_BYTES),
        cost_estimate=pl.CostEstimate(flops=flops, bytes_accessed=1000, transcendentals=0),
    )(*operands)


def sds(shape, dtype):
    return jax.ShapeDtypeStruct(shape, dtype)


def field(level, extra):
    return sds((level.pairs + extra, level.alloc, LANES), F32)


def buffer(level, extra):
    return pltpu.VMEM((level.pairs + extra, level.alloc, LANES), F32)


def local(strips, sections, cotangent, activations, weights, biases):
    row_count, flat_width = activations.shape[2:]
    channels = weights.shape[-1]
    half = channels // 2
    cols = flat_width // channels
    assert 2 * channels == LANES and sections == 4 and cotangent.shape[0] == 1
    levels = levels_of(row_count, cols, sections)
    fine, second, third, last = levels
    x_margin, g_margin = fine.x_margin, fine.error
    payload = up_to(x_margin + g_margin, 16)
    pair_count = fine.pairs
    chunk = 4

    def place():
        return lax.axis_index("strip"), strips

    def is_odd():
        return lax.rem(lax.axis_index("strip"), 2) == 1

    packed_rows = TAPS * channels
    own_flat = up_to(third.pairs * third.x_rows, 16)
    ship_rows = own_flat + packed_rows + 16

    def halo_body(
        act_hbm, cot_hbm, bias_hbm, act_ref, cot_ref, both_ref, swap_ref, cross_ref, xs, cs, ts
    ):
        both_ref[0:2, :] = twice(bias_hbm[...])
        section = lax.axis_index("section")
        odd = is_odd()

        live = jnp.int32(fine.rows)
        for level in levels[1:]:
            live = jnp.where(section == level.level, level.rows, live)
        for p in range(pair_count):
            at = slice(p * LANES, (p + 1) * LANES)
            act_ref[:, at] = act_hbm[:, at]
            cot_ref[:, at] = cot_hbm[:, at]
            xs[p, 0:row_count, :] = act_hbm[:, at].astype(F32)
            cs[p, 0:row_count, :] = cot_hbm[:, at].astype(F32)
            ts[0, p, 0:x_margin, :] = xs[p, 0:x_margin, :]
            ts[0, p, x_margin : x_margin + g_margin, :] = cs[p, 0:g_margin, :]
            ts[1, p, 0:x_margin, :] = xs[p, pl.ds(live - x_margin, x_margin), :]
            ts[1, p, x_margin : x_margin + g_margin, :] = cs[p, row_count - g_margin : row_count, :]
            upper = ts[0, p, 0:payload, :]
            lower = ts[1, p, 0:payload, :]
            swap_ref[:, at] = jnp.where(odd, upper, lower).astype(BF16)
            cross_ref[:, at] = jnp.where(odd, lower, upper).astype(BF16)

    strip_shape = sds((row_count, flat_width), BF16)
    halo_shape = sds((payload, flat_width), BF16)
    taps = weights.reshape(2 * TAPS, channels, channels)
    act, cot, bias_own, to_swap, to_cross = call(
        halo_body,
        [
            strip_shape, strip_shape, sds((8, LANES), F32), halo_shape, halo_shape,
        ],
        [
            pltpu.VMEM((pair_count, row_count + 16, LANES), F32),
            pltpu.VMEM((pair_count, row_count + 16, LANES), F32),
            pltpu.VMEM((2, pair_count, payload + 16, LANES), F32),
        ],
        [activations[0, 0], cotangent[0], biases[0]],
        outside=(0, 1, 2),
    )
    swap_pairs = [(i, i ^ 1) for i in range(strips)]
    cross_pairs = [(i, i + 1) for i in range(1, strips - 1, 2)] + [(i + 1, i) for i in range(1, strips - 1, 2)]
    from_cross = lax.ppermute(to_cross, "strip", cross_pairs)
    from_swap = lax.ppermute(to_swap, "strip", swap_pairs)


    def expand(tap_list, forward_ref, back_ref):
        for c in range(2):
            chosen = tap_list[c * TAPS : (c + 1) * TAPS]
            forward_ref[c, :, :] = toeplitz(chosen).astype(BF16)
            back_ref[c, :, :] = toeplitz_back(chosen).astype(BF16)

    def matrix_body(taps_ref, bias_ref, forward_ref, back_ref):
        expand([taps_ref[t].astype(F32) for t in range(2 * TAPS)], forward_ref, back_ref)

    matrix_shape = sds((2, 2 * LANES, 3 * LANES), BF16)
    fwd_own, back_own = call(matrix_body, [matrix_shape, matrix_shape], [], [taps, bias_own])

    def across(value, pairs):
        return lax.ppermute(value, "section", pairs)

    inside = [[(17, row_count)], [(16, row_count)]]
    ends = [[(0, 24), (row_count + 10, 24)], [(0, 24), (row_count + 8, 24)]]
    assert fine.error == 15 and fine.x_margin == 17 and row_count >= 32
    g_in = (4, second.rows - 8)
    g_end = second.error + g_in[0]
    in_rows = up_to(second.pairs * g_in[1], 16)
    rim_rows = up_to(second.pairs * 2 * g_end, 16)

    def error_of(level, gb, eo, mask_place):
        def error(first, size, a, rows, value):
            mask = image_mask(level, a - level.error, rows, *mask_place)
            part = gb[first : first + size, a : a + rows, :]
            eo[first + 1 : first + 1 + size, a : a + rows, :] = jnp.where(mask, rounded(part * value), 0.0)

        return error

    def inside_body(
        act_ref, cot_ref, fwd_ref, back_ref, bias_ref, hop_ref, xb, hb, db, gb, eo, ei, bi, gu, rc, flat,
    ):
        section = lax.axis_index("section")

        @pl.when(section == 0)
        def _():
            level = fine
            own_input(level, xb, act_ref)
            zero_after(level, xb)
            zero_edges(eo, level)
            zero_tail(hb, level, level.hidden_rows)
            zero_tail(ei, level, level.alloc)
            for p in range(level.pairs):
                gb[p, g_margin : g_margin + row_count, :] = cot_ref[:, p * LANES : (p + 1) * LANES].astype(F32)
            forward(
                level, xb, hb, [fwd_ref.at[0], fwd_ref.at[1]], bias_ref, db, error_of(level, gb, eo, place()),
                place(), chunk, *inside,
            )
            backward(
                level, eo, ei, [back_ref.at[0], back_ref.at[1]], db, gb, 0, bi, gu, place(), chunk,
                inside[1], inside[1],
            )

            def emit(m, span, rows):
                flat[m * g_in[1] : (m + 1) * g_in[1], :] = rows

            coarsen(fine, second, gu, rc, [(0, 16)], [g_in], emit, place(), edges=False)
            hop_ref[...] = flat[0:in_rows, :].astype(BF16)

    coarse_buffer = pltpu.VMEM((fine.pairs, 3 * fine.k_count + 8, LANES), F32)
    state_shapes = [
        field(fine, 2), field(fine, 1), field(fine, 1), field(fine, 0),
        field(fine, 2), field(fine, 1), field(fine, 0), field(fine, 0),
    ]
    hop_in, *state = call(
        inside_body,
        [sds((in_rows, LANES), BF16), *state_shapes],
        [coarse_buffer, pltpu.VMEM((in_rows + 16, LANES), F32)],
        [act, cot, fwd_own, back_own, bias_own],
    )
    in_near = across(hop_in, [(0, 1), (1, 3), (3, 2), (2, 0)])

    def halo_readers(swap_ref, cross_ref):
        odd = is_odd()

        def top(at):
            return jnp.where(odd, swap_ref[:, at].astype(F32), cross_ref[:, at].astype(F32))

        def low(at):
            return jnp.where(odd, cross_ref[:, at].astype(F32), swap_ref[:, at].astype(F32))

        return top, low

    def rim_body(
        swap_ref, cross_ref, fwd_ref, back_ref, bias_ref, xi, hi, di, gi, oi, ii, bii, ui,
        rim_ref, xb, hb, db, gb, eo, ei, bi, gu, rc, flat, tmp,
    ):
        section = lax.axis_index("section")
        top, low = halo_readers(swap_ref, cross_ref)

        @pl.when(section == 0)
        def _():
            level = fine
            end = x_margin + row_count
            for p in range(level.pairs):
                at = slice(p * LANES, (p + 1) * LANES)
                tmp[0, 0:payload, :] = top(at)
                tmp[1, 0:payload, :] = low(at)
                xb[p + 1, 0:x_margin, :] = tmp[0, 0:x_margin, :]
                xb[p + 1, end : end + x_margin, :] = tmp[1, 0:x_margin, :]
                gb[p, 0:g_margin, :] = tmp[0, x_margin : x_margin + g_margin, :]
                gb[p, g_margin + row_count : 2 * g_margin + row_count, :] = tmp[
                    1, x_margin : x_margin + g_margin, :
                ]
            forward(
                level, xb, hb, [fwd_ref.at[0], fwd_ref.at[1]], bias_ref, db, error_of(level, gb, eo, place()),
                place(), chunk, ends[0], ends[0],
            )
            backward(
                level, eo, ei, [back_ref.at[0], back_ref.at[1]], db, gb, 0, bi, gu, place(), chunk, ends[1], ends[1]
            )

            def emit(m, span, rows):
                at = m * 2 * g_end + span * g_end
                flat[at : at + g_end, :] = rows[0:g_end]

            last_k = (second.rows + second.error) // 3
            coarsen(
                fine, second, gu, rc,
                [(fine.k_first, 8), (last_k - 7, 8)],
                [(-second.error, up_to(g_end, 8)), (g_in[0] + g_in[1], up_to(g_end, 8))],
                emit, place(),
            )
            rim_ref[...] = flat[0:rim_rows, :].astype(BF16)

    tmp_buffer = pltpu.VMEM((2, payload + 16, LANES), F32)
    rim, *state = call(
        rim_body,
        [sds((rim_rows, LANES), BF16), *state_shapes],
        [coarse_buffer, pltpu.VMEM((rim_rows + 32, LANES), F32), tmp_buffer],
        [from_swap, from_cross, fwd_own, back_own, bias_own, *state],
        aliases={5 + i: 1 + i for i in range(len(state_shapes))},
        flops=2 * 10**9,
    )
    rim_near = across(rim, [(0, 1), (1, 3), (3, 2), (2, 0)])

    def ship_body(act_ref, swap_ref, cross_ref, taps_ref, both_ref, rim_ref, ship_ref, tmp, flat, bias_tmp):
        top, low = halo_readers(swap_ref, cross_ref)

        @pl.when(lax.axis_index("section") == 2)
        def _():
            level = third
            margin = level.x_margin
            for p in range(level.pairs):
                at = slice(p * LANES, (p + 1) * LANES)
                tmp[0, 0:payload, :] = top(at)
                tmp[1, 0:payload, :] = low(at)
                to = p * level.x_rows
                end = to + margin + level.rows
                flat[to : to + margin, :] = tmp[0, x_margin - margin : x_margin, :]
                flat[to + margin : to + margin + level.own_rows, :] = act_ref[0 : level.own_rows, at].astype(F32)
                flat[end : end + margin, :] = tmp[1, 0:margin, :]
            ship_ref[0:own_flat, :] = flat[0:own_flat, :].astype(BF16)
            for t in range(2 * TAPS):
                at = own_flat + t * half
                value = taps_ref[t].astype(F32)
                ship_ref[at : at + half, :] = jnp.concatenate([value[:half], value[half:]], axis=1).astype(BF16)
            rest = both_ref[0:2, :]
            for term in range(3):
                part = rounded(rest)
                bias_tmp[2 * term : 2 * term + 2, :] = part
                rest = rest - part
            bias_tmp[6:16, :] = jnp.zeros((10, LANES), F32)
            ship_ref[own_flat + packed_rows : ship_rows, :] = bias_tmp[0:16, :].astype(BF16)

    (ship,) = call(
        ship_body,
        [sds((ship_rows, LANES), BF16)],
        [tmp_buffer, pltpu.VMEM((own_flat + 32, LANES), F32), pltpu.VMEM((32, LANES), F32)],
        [act, from_swap, from_cross, taps, bias_own, rim],
    )
    shipped = across(ship, [(2, 3)])

    grad_rows = 4 * channels + half + 16

    def gradients(level, source, hidden, err_in, err_out, rows_at, pair_out):
        scale = np.float32(1.0 / math.sqrt(strips * level.rows * level.cols))
        first = kernel_terms(source, err_in, level.odd_pairs, rows_at[2], rows_at[0], level)
        pack_kernel_terms(pair_out.at[0], *first, scale)
        then = kernel_terms(hidden, err_out, level.pairs, rows_at[3], rows_at[1], level)
        pack_kernel_terms(pair_out.at[1], *then, scale)

    def finish(level, source, hidden, ei, eo, pair_out):
        at = (level.error - 1, level.error, level.error + 1, level.error)
        gradients(level, source, hidden, ei, eo.at[1 : 1 + level.pairs], at, pair_out)

    def store_in(level, d_out):
        def store(first, size, a, rows, value):
            d_out[first : first + size, a : a + rows, :] = value

        return store

    def beside_body(
        act_ref, swap_ref, cross_ref, fwd_ref, bias_ref, x0, h0, o0, i0,
        din_ref, dout_ref, hid_ref, x_ref, pair_ref, tmp,
    ):
        section = lax.axis_index("section")
        top, low = halo_readers(swap_ref, cross_ref)

        @pl.when(section == 0)
        def _():
            finish(fine, x0, h0, i0, o0, pair_ref)

        for level in levels[1:]:

            @pl.when(section == level.level)
            def _(level=level):
                own_input(level, x_ref, act_ref)
                halo_input(level, x_ref, top, low, tmp, x_margin)
                zero_tail(hid_ref, level, level.hidden_rows)
                forward(
                    level, x_ref, hid_ref, [fwd_ref.at[0], fwd_ref.at[1]], bias_ref, din_ref,
                    store_in(level, dout_ref), place(), chunk,
                )

    pair_shape = sds((2, grad_rows, LANES), F32)
    din_own, dout_own, hid_own, x_own, pair_first = call(
        beside_body,
        [field(second, 1), field(second, 0), field(second, 1), field(second, 2), pair_shape],
        [tmp_buffer],
        [act, from_swap, from_cross, fwd_own, bias_own, state[0], state[1], state[4], state[5]],
    )

    def step(level, gb, grad_row, d_in, d_out, back, eo, ei, bi, gu):
        mask = image_mask(level, -level.error, level.out_rows, *place())
        zero_edges(eo, level)
        zero_tail(ei, level, level.alloc)
        for p in range(level.pairs):
            part = gb[p, grad_row : grad_row + level.out_rows, :] * d_out[p, 0 : level.out_rows, :]
            eo[p + 1, 0 : level.out_rows, :] = jnp.where(mask[0], rounded(part), 0.0)
        backward(level, eo, ei, [back.at[0], back.at[1]], d_in, gb, grad_row, bi, gu, place(), chunk)

    third_rows = third.rows + 2 * third.error
    third_flat = up_to(third.pairs * third_rows, 16)

    def hand_down(upper, lower, gu, rc, gb):
        def emit(m, span, value):
            gb[m, 0 : 3 * upper.k_count, :] = rounded(value)

        coarsen(
            upper, lower, gu, rc, [(upper.k_first, upper.k_count)], [(3 * upper.k_first, 3 * upper.k_count)],
            emit, place(),
        )

    def second_error(gb, d_out, eo, first, rows):
        mask = image_mask(second, first - second.error, rows, *place())
        for p in range(second.pairs):
            part = gb[p, first : first + rows, :] * d_out[p, first : first + rows, :]
            eo[p + 1, first : first + rows, :] = jnp.where(mask[0], rounded(part), 0.0)

    def second_inside_body(in_ref, din_o, dout_o, back_o, eo, ei, bi, gu, gb, mid):
        @pl.when(lax.axis_index("section") == 1)
        def _():
            mid[...] = in_ref[...].astype(F32)
            for p in range(second.pairs):
                gb[p, g_end : g_end + g_in[1], :] = mid[p * g_in[1] : (p + 1) * g_in[1], :]
            zero_edges(eo, second)
            zero_tail(ei, second, second.alloc)
            second_error(gb, dout_o, eo, g_end, g_in[1])
            parts = [(g_end, g_in[1])]
            backward(second, eo, ei, [back_o.at[0], back_o.at[1]], din_o, gb, 0, bi, gu, place(), chunk, parts, parts)

    inside_shapes = [
        field(second, 2), field(second, 1), field(second, 0),
        sds((second.pairs, second.alloc + 8, LANES), F32), field(second, 0),
    ]
    inside_state = call(
        second_inside_body,
        inside_shapes,
        [pltpu.VMEM((in_rows, LANES), F32)],
        [in_near, din_own, dout_own, back_own],
    )

    def second_rim_body(
        rim_ref, din_o, dout_o, back_o, eo_i, ei_i, bi_i, gu_i, gb_i, third_ref, eo, ei, bi, gu, gb, rc, rims, flat
    ):
        @pl.when(lax.axis_index("section") == 1)
        def _():
            rims[...] = rim_ref[...].astype(F32)
            low = g_end + g_in[1]
            for p in range(second.pairs):
                at = p * 2 * g_end
                gb[p, 0:g_end, :] = rims[at : at + g_end, :]
                gb[p, low : low + g_end, :] = rims[at + g_end : at + 2 * g_end, :]
            second_error(gb, dout_o, eo, 0, g_end)
            second_error(gb, dout_o, eo, low, g_end)
            rows = up_to(g_end + 2, 8)
            in_parts = [(0, rows), (low + g_end - rows, rows)]
            back_parts = [(0, rows), (low + g_end - 2 - rows, rows)]
            backward(
                second, eo, ei, [back_o.at[0], back_o.at[1]], din_o, gb, 0, bi, gu, place(), chunk,
                in_parts, back_parts,
            )
            hand_down(second, third, gu, rc, gb)
            at = second.up_shift
            for p in range(third.pairs):
                flat[p * third_rows : (p + 1) * third_rows, :] = gb[p, at : at + third_rows, :]
            third_ref[...] = flat[0:third_flat, :].astype(BF16)

    coarse_tmp = pltpu.VMEM((second.pairs, 3 * second.k_count + 8, LANES), F32)
    third_grad, eo_own, ei_own, bi_own, *_ = call(
        second_rim_body,
        [sds((third_flat, LANES), BF16), *inside_shapes],
        [coarse_tmp, pltpu.VMEM((rim_rows, LANES), F32), pltpu.VMEM((third_flat + 16, LANES), F32)],
        [rim_near, din_own, dout_own, back_own, *inside_state],
        aliases={4 + i: 1 + i for i in range(len(inside_shapes))},
        flops=4 * 10**9,
    )
    third_to_last = across(third_grad, [(1, 3), (3, 2), (2, 0), (0, 1)])
    third_to_own = across(third_grad, [(1, 2)])

    def shipped_body(ship_ref, own_ref, x_o, hid_o, eo_o, ei_o, din_s, dout_s, back_s, pair_ref, fwd_s, xb, hb, own):
        @pl.when(lax.axis_index("section") == 1)
        def _():
            finish(second, x_o, hid_o, ei_o, eo_o, pair_ref)

        @pl.when(lax.axis_index("section") == 3)
        def _():
            level = third
            values = []
            for t in range(2 * TAPS):
                pack = ship_ref[own_flat + t * half : own_flat + (t + 1) * half, :].astype(F32)
                values.append(jnp.concatenate([pack[:, :channels], pack[:, channels:]], axis=0))
            expand(values, fwd_s, back_s)
            terms = ship_ref[own_flat + packed_rows : ship_rows, :].astype(F32)
            bias = terms[0:2] + terms[2:4] + terms[4:6]
            own[0:own_flat, :] = ship_ref[0:own_flat, :].astype(F32)
            shipped_input(level, xb, own)
            zero_tail(hb, level, level.hidden_rows)
            forward(level, xb, hb, [fwd_s.at[0], fwd_s.at[1]], bias, din_s, store_in(level, dout_s), place(), chunk)

    din_s, dout_s, back_s, pair_second = call(
        shipped_body,
        [field(third, 1), field(third, 0), matrix_shape, pair_shape],
        [
            pltpu.VMEM((2, 2 * LANES, 3 * LANES), BF16),
            buffer(third, 2),
            buffer(third, 1),
            pltpu.VMEM((own_flat + 16, LANES), F32),
        ],
        [shipped, third_to_own, x_own, hid_own, eo_own, ei_own],
    )

    def last_body(
        pair0, pair1, own_ref, last_ref, din_o, dout_o, hid_o, x_o, back_o, din_s, dout_s, back_s,
        keep_ref, send_ref, bi, pair_out, gb, eo, ei, gu, rc, flat,
    ):
        section = lax.axis_index("section")
        odd = is_odd()

        def take(source):
            flat[0:third_flat, :] = source[...].astype(F32)
            for p in range(third.pairs):
                gb[p, 0:third_rows, :] = flat[p * third_rows : (p + 1) * third_rows, :]

        @pl.when(section == 0)
        def _():
            pair_out[...] = pair0[...]

        @pl.when(section == 1)
        def _():
            pair_out[...] = pair1[...]

        @pl.when(section == 2)
        def _():
            take(own_ref)
            step(third, gb, 0, din_o, dout_o, back_o, eo, ei, bi, None)
            finish(third, x_o, hid_o, ei, eo, pair_out)

        @pl.when(section == 3)
        def _():
            take(last_ref)
            step(third, gb, 0, din_s, dout_s, back_s, eo, ei, None, gu)
            hand_down(third, last, gu, rc, gb)
            step(last, gb, third.up_shift, din_o, dout_o, back_o, eo, ei, bi, None)
            finish(last, x_o, hid_o, ei, eo, pair_out)

        first, then = pair_out[0], pair_out[1]
        keep_ref[...] = jnp.where(odd, then, first)
        send_ref[...] = jnp.where(odd, first, then)

    half_shape = sds((grad_rows, LANES), F32)
    keep, send, bi_last = call(
        last_body,
        [half_shape, half_shape, field(third, 0)],
        [
            pltpu.VMEM((2, grad_rows, LANES), F32),
            buffer(third, 0),
            buffer(third, 2),
            buffer(third, 1),
            buffer(fine, 0),
            coarse_tmp,
            pltpu.VMEM((third_flat + 16, LANES), F32),
        ],
        [
            pair_first, pair_second, third_to_own, third_to_last, din_own, dout_own, hid_own, x_own, back_own,
            din_s, dout_s, back_s,
        ],
    )

    total = keep + lax.ppermute(send, "strip", swap_pairs)
    step = 2
    while step < strips:
        mine = lax.reduce_precision(total, 8, 7)
        small = mine.astype(BF16)
        offsets = (step, 2 * step, 3 * step) if 2 * step < strips else (step,)
        got = [lax.ppermute(small, "strip", [(i, i ^ o) for i in range(strips)]).astype(F32) for o in offsets]
        total = mine + got[0]
        if len(got) == 3:
            total = total + (got[1] + got[2])
        step *= len(got) + 1
    other = lax.ppermute(total, "strip", swap_pairs)

    def noise_body(bi_f, bi_o, bi_l, noise_ref):
        section = lax.axis_index("section")

        for level, source in ((fine, bi_f), (second, bi_o), (third, bi_l), (last, bi_l)):

            @pl.when(section == level.level)
            def _(level=level, source=source):
                write_noise(level, source, noise_ref)

    (noise,) = call(noise_body, [strip_shape], [], [state[6], bi_own, bi_last], final=(0,))

    def in_taps(value, ref):
        half = channels
        for dy in range(3):
            ref[dy * 192 : dy * 192 + 128, :] = value[dy * half : (dy + 1) * half].T
        pair = value[3 * half : 4 * half].T
        ref[128:192, :] = pair[:half]
        ref[320:384, :] = pair[half:]
        at = 4 * half + half // 2
        pair = value[4 * half : at].T
        ref[512:576, :] = jnp.concatenate([pair[:half], pair[half:]], axis=1)
        ref[576:584, :] = value[at : at + 8, :half]

    tap_rows = TAPS * channels + 8

    def mine_body(mine_ref, taps_ref):
        in_taps(mine_ref[...], taps_ref)

    (mine_taps,) = call(mine_body, [sds((tap_rows, channels), F32)], [], [total])

    def final_body(mine_ref, other_ref, kernel_ref, bias_ref, other_taps):
        odd = is_odd()
        in_taps(other_ref[...], other_taps)
        mine, theirs = mine_ref[...], other_taps[...]
        first, then = jnp.where(odd, theirs, mine), jnp.where(odd, mine, theirs)
        kernel_ref[0, :, :] = first[: tap_rows - 8]
        kernel_ref[1, :, :] = then[: tap_rows - 8]
        bias_ref[...] = jnp.concatenate([first[tap_rows - 8 : tap_rows - 7], then[tap_rows - 8 : tap_rows - 7]], axis=0)

    kernel_sum, bias_sum = call(
        final_body,
        [sds((2, TAPS * channels, channels), F32), sds((2, channels), F32)],
        [pltpu.VMEM((tap_rows, channels), F32)],
        [mine_taps, other],
        final=(0, 1),
    )
    return (
        noise[None, None],
        kernel_sum.reshape(1, 2, 3, 3, channels, channels),
        bias_sum[None],
    )


def solution(mesh):
    strips = mesh.shape["strip"]
    sections = mesh.shape["section"]
    return jax.shard_map(
        functools.partial(local, strips, sections),
        mesh=mesh,
        in_specs=(
            P(None, "strip", None),
            P("section", None, "strip", None),
            P("section", None, None, None, None, None),
            P("section", None, None),
        ),
        out_specs=(
            P("section", None, "strip", None),
            P("section", None, None, None, None, None),
            P("section", None, None),
        ),
        check_vma=False,
    )
```
